128 devices in a mesh: seq: 8 (over x, core), head: 16 (over z, y).
Axes of the slice: x: 4, y: 4, z: 4, core: 2. Of those that a mesh axis runs over, the one named last changes fastest.
Arguments:
- tokens: bfloat16 [1024, 6144], P('seq'), may hold values from -6 to 6
- log_decay: float32 [1024, 32], P('seq', 'head'), may hold values from -1 to 0
- carried_state: float32 [32, 128, 128], P('head'), may hold values from -48 to 48
- q_weight: bfloat16 [6144, 4096], P(None, 'head'), may hold values from -0.078125 to 0.078125
- k_weight: bfloat16 [6144, 4096], P(None, 'head'), may hold values from -0.078125 to 0.078125
- v_weight: bfloat16 [6144, 4096], P(None, 'head'), may hold values from -0.078125 to 0.078125
- out_weight: bfloat16 [4096, 6144], P('head'), may hold values from -0.09375 to 0.09375
- final_gain: bfloat16 [6144], replicated, may hold values from 0.099609375 to 1.8984375
- vocab_weight: bfloat16 [6144, 131072], P(None, ('seq', 'head')), may hold values from -5 to 5
- targets: int32 [1024], replicated, may hold values from 0 to 131071
Outputs:
- loglik: float32 [1024], P('seq')
The draws below stay inside these ranges and needn't reach their ends.
All inputs are finite; a program needn't handle non-finite values.
Results may differ from the reference program's by a relative error of at most 0.002.
Values may be sent and summed in bfloat16 or wider, within the bound.
No kernel may reach another device: no remote copies, remote signals or barrier semaphores. Data moves between devices by JAX's collectives and lax.ppermute only.
A program may use at most 128 MiB of HBM per device.

```python
import math
import jax
import jax.numpy as jnp
import numpy as np
from jax import lax

D = 6144
HEAD_GROUP = 32
DK = 128
VOCAB = 131072
TOK_DEV = 128
TOKEN_SPAN = 1024


def draw_log_decay(key, part):
    key_rows = jax.random.split(jax.random.fold_in(key, 11), 6)
    slow_share = 0.5
    slow = jax.random.uniform(key_rows[0], (HEAD_GROUP,)) < slow_share
    fast_rate = jnp.exp(jax.random.uniform(key_rows[1], (HEAD_GROUP,), jnp.float32, math.log(1.0 / 50.0), math.log(1.0 / 30.0)))
    slow_rate = jnp.exp(jax.random.uniform(key_rows[2], (HEAD_GROUP,), jnp.float32, math.log(0.05), math.log(0.4))) / TOKEN_SPAN
    rate = jnp.where(slow, slow_rate, fast_rate)
    factor = jnp.exp(jax.random.uniform(key_rows[3], (TOKEN_SPAN // TOK_DEV, HEAD_GROUP), jnp.float32, math.log(0.5), math.log(2.0)))
    position_loglik = jnp.repeat(factor, TOK_DEV, axis=0) * rate[None, :]
    spike_mask = jax.random.randint(key_rows[4], (2, HEAD_GROUP), 0, TOKEN_SPAN)
    spike_length = jnp.log(jax.random.uniform(key_rows[5], (2, HEAD_GROUP), jnp.float32, 0.5, 0.8))
    token_position = jnp.arange(TOKEN_SPAN)[:, None]
    token_spike = jnp.where(token_position == spike_mask[0][None, :], spike_length[0][None, :], 0.0)
    token_spike = token_spike + jnp.where(token_position == spike_mask[1][None, :], spike_length[1][None, :], 0.0)
    return jnp.maximum(token_spike - position_loglik, -1.0).astype(jnp.float32)


def draw_vocab_weight(key, part):
    key_rows = jax.random.split(jax.random.fold_in(key, 23), 2)
    base = jnp.clip(jax.random.normal(key_rows[0], (D, VOCAB), jnp.float32), -6.0, 6.0) * D ** (-0.5)
    column_scale = jnp.exp(jax.random.uniform(key_rows[1], (VOCAB,), jnp.float32, 0.0, math.log(10.0)))
    return jnp.clip(base * column_scale[None, :], -5.0, 5.0).astype(jnp.bfloat16)


def place_ends(result, stream_key, smallest, high):
    dims = result.shape
    place = [jax.random.randint(jax.random.fold_in(stream_key, axis), (), 0, dims[axis]) for axis in range(len(dims))]
    result = result.at[tuple(place)].set(smallest)
    longest = dims.index(max(dims))
    place[longest] = (place[longest] + 1) % dims[longest]
    return result.at[tuple(place)].set(high)


def level_of(key, extent, shards, low, largest):
    loudness = 1.0
    for dim, parts in shards:
        draws = jax.random.uniform(jax.random.fold_in(jax.random.fold_in(key, 6), dim), (parts,), jnp.float32, low / len(shards), largest / len(shards))
        loudness = loudness * jnp.repeat(jnp.exp(draws), extent[dim] // parts).reshape((-1,) + (1,) * (len(extent) - 1 - dim))
    return loudness


def skewed_wide(rng, dims, number_of, skew):
    portions = [min(1 << octave, number_of + 1 - (1 << octave)) * (1 << 20) // math.isqrt((1 << octave) ** skew) + 1 for octave in range((number_of + 1).bit_length()) if 1 << octave <= number_of]
    deviation = 1 + sum(portions) // (1 << 30)
    listing = np.cumsum(np.array([max(1, weight // deviation) for weight in portions]))
    pick = jax.random.randint(jax.random.fold_in(rng, 1), dims, 0, int(listing[len(portions) - 1]))
    start = jnp.left_shift(1, jnp.searchsorted(jnp.asarray(listing, jnp.int32), pick, side="right").astype(jnp.int32))
    standing = start - 1 + jax.random.randint(jax.random.fold_in(rng, 4), dims, 0, 1 << 30) % jnp.minimum(start, number_of + 1 - start)
    return jax.random.permutation(jax.random.fold_in(rng, 2), number_of)[standing].astype(jnp.int32)


def centred(key, shape, width, bound, cuts=(), dtype=jnp.bfloat16):
    values = jax.random.normal(key, shape, jnp.float32) * width
    if len(cuts) > 0:
        values = level_of(key, shape, cuts, -0.22, 0.18) * values
    return jnp.clip(values, min=-bound, max=bound).astype(dtype)


def setup_inputs(seed: int = 0) -> dict:
    key_of = jax.random.split(jax.random.key(seed), 11)
    return {
        "tokens": centred(key_of[0], (TOKEN_SPAN, D), 1.0, 6.0, ((0, 8),)),
        "log_decay": draw_log_decay(jax.random.fold_in(key_of[10], 71), 0),
        "carried_state": centred(key_of[2], (HEAD_GROUP, DK, DK), 8.0, 48.0, ((0, 16),), jnp.float32),
        "q_weight": centred(key_of[3], (D, HEAD_GROUP * DK), D ** -0.5, 0.078125, ((1, 16),)),
        "k_weight": centred(key_of[4], (D, HEAD_GROUP * DK), D ** -0.5, 0.078125, ((1, 16),)),
        "v_weight": centred(key_of[5], (D, HEAD_GROUP * DK), D ** -0.5, 0.078125, ((1, 16),)),
        "out_weight": centred(key_of[6], (HEAD_GROUP * DK, D), (HEAD_GROUP * DK) ** -0.5, 0.09375, ((0, 16),)),
        "final_gain": jnp.clip(1.0 + 0.18 * jax.random.normal(key_of[7], (D,), jnp.float32), 0.099609375, 1.8984375).astype(jnp.bfloat16),
        "vocab_weight": draw_vocab_weight(jax.random.fold_in(key_of[10], 71), 0),
        "targets": place_ends(skewed_wide(key_of[9], (TOKEN_SPAN,), VOCAB, 2), jax.random.fold_in(key_of[9], 3), 0, VOCAB - 1).astype(jnp.int32),
    }


def reference(tokens, log_decay, carried_state, q_weight, k_weight, v_weight, out_weight, final_gain, vocab_weight, targets):
    hp = lax.Precision.HIGHEST
    q_all = jnp.dot(tokens, q_weight, preferred_element_type=jnp.float32).astype(jnp.bfloat16)
    k_all = jnp.dot(tokens, k_weight, preferred_element_type=jnp.float32).astype(jnp.bfloat16)
    v_all = jnp.dot(tokens, v_weight, preferred_element_type=jnp.float32).astype(jnp.bfloat16)
    blocks = TOKEN_SPAN // TOK_DEV
    shape4 = (blocks, TOK_DEV, HEAD_GROUP, DK)
    q_blk = q_all.reshape(shape4)
    k_blk = k_all.reshape(shape4)
    v_blk = v_all.reshape(shape4)
    d_blk = log_decay.reshape(blocks, TOK_DEV, HEAD_GROUP)
    lower = jnp.arange(TOK_DEV)[:, None] >= jnp.arange(TOK_DEV)[None, :]

    def step(state, items):
        qb, kb, vb, db = items
        cumul = jnp.cumsum(db, axis=0)
        last = cumul[-1]
        scores = jnp.einsum('thd,shd->hts', qb.astype(jnp.float32), kb.astype(jnp.float32))
        diff = jnp.transpose(cumul[:, None, :] - cumul[None, :, :], (2, 0, 1))
        decay_w = jnp.exp(jnp.where(lower[None], diff, -1e+30))
        weight = (scores * decay_w).astype(jnp.bfloat16)
        intra = jnp.einsum('hts,shd->thd', weight.astype(jnp.float32), vb.astype(jnp.float32))
        inter = jnp.exp(cumul)[:, :, None] * jnp.einsum('thd,hde->the', qb.astype(jnp.float32), state, precision=hp)
        attended = intra + inter
        ends = jnp.exp(last[None, :] - cumul)
        local_state = jnp.einsum('thd,the->hde', kb.astype(jnp.float32) * ends[:, :, None], vb.astype(jnp.float32), precision=hp)
        new_state = jnp.exp(last)[:, None, None] * state + local_state
        return (new_state, attended)
    final_state, attended = lax.scan(step, carried_state.astype(jnp.float32), (q_blk, k_blk, v_blk, d_blk))
    attended = attended.reshape(TOKEN_SPAN, HEAD_GROUP, DK)
    normed_heads = attended * lax.rsqrt(lax.optimization_barrier(jnp.mean(attended * attended, axis=-1, keepdims=True)) + 1e-06)
    normed_heads = normed_heads.astype(jnp.bfloat16).reshape(TOKEN_SPAN, HEAD_GROUP * DK)
    mixed = jnp.dot(normed_heads, out_weight, preferred_element_type=jnp.float32)
    resid = tokens.astype(jnp.float32) + mixed
    final_rows = resid * lax.rsqrt(lax.optimization_barrier(jnp.mean(resid * resid, axis=-1, keepdims=True)) + 1e-06) * final_gain.astype(jnp.float32)
    final_rows = final_rows.astype(jnp.bfloat16)

    def score(items):
        rows_blk, want = items
        logits = jnp.dot(rows_blk, vocab_weight, preferred_element_type=jnp.float32)
        top = lax.optimization_barrier(jnp.max(logits, axis=1))
        total = lax.optimization_barrier(jnp.sum(jnp.exp(logits - top[:, None]), axis=1))
        hit = jnp.take_along_axis(logits, want[:, None].astype(jnp.int32), axis=1)[:, 0]
        return hit - top - jnp.log(total)
    loglik = lax.map(score, (final_rows.reshape(blocks, TOK_DEV, D), targets.reshape(blocks, TOK_DEV)))
    return loglik.reshape(TOKEN_SPAN)
```

```python
import jax
import jax.numpy as jnp
from jax import lax
from jax.sharding import Mesh, PartitionSpec as P

X, CORE, Z, Y = 4, 2, 4, 4
ALL = ("x", "core", "z", "y")
F32 = jnp.float32
BF16 = jnp.bfloat16


def move(array, target):
    pairs = []
    for i in range(X * CORE * Z * Y):
        at = (i // (CORE * Z * Y), i // (Z * Y) % CORE, i // Y % Z, i % Y)
        to = target(*at)
        if to is not None:
            pairs.append((i, ((to[0] * CORE + to[1]) * Z + to[2]) * Y + to[3]))
    return lax.ppermute(array, ALL, pairs)


def other_core(x, c, z, y):
    return (x, 1 - c, z, y)


def along_x(s):
    return lambda x, c, z, y: ((x + s) % X, c, z, y)


def along_y(s):
    return lambda x, c, z, y: (x, c, z, (y + s) % Y)


def along_z(s):
    return lambda x, c, z, y: (x, c, (z + s) % Z, y)


def along_first(s):
    return lambda x, c, z, y: (x, c, z, (y + s) % Y) if c == 0 else (x, c, (z + s) % Z, y)


def along_second(s):
    return lambda x, c, z, y: (x, c, (z + s) % Z, y) if c == 0 else (x, c, z, (y + s) % Y)


def later_x(s):
    return lambda x, c, z, y: (x + s, c, z, y) if x + s < X else None


def spread(block, here, target):
    rows = block.shape[0]
    parts = [block] + [move(block, target(s)) for s in (1, 3, 2)]
    whole = jnp.zeros((4 * rows,) + block.shape[1:], block.dtype)
    for s, part in zip((0, 1, 3, 2), parts):
        whole = lax.dynamic_update_slice_in_dim(whole, part, lax.rem(here + 4 - s, 4) * rows, 0)
    return whole


def merge(parts):
    top = parts[0][0]
    for p in parts[1:]:
        top = jnp.maximum(top, p[0])
    total = sum(p[1] * jnp.exp(p[0] - top) for p in parts)
    hit = sum(p[2] for p in parts)
    return jnp.stack([top, total, hit])


def shards(
    tokens,
    log_decay,
    carried_state,
    q_weight,
    k_weight,
    v_weight,
    out_weight,
    final_gain,
    vocab_weight,
    targets,
):
    highest = lax.Precision.HIGHEST
    x, c, z, y = (lax.axis_index(a) for a in ALL)
    rows_here = tokens.shape[0]
    heads_here = carried_state.shape[0]
    head_size = carried_state.shape[1]
    view = (rows_here, heads_here, head_size)

    keys = jnp.dot(tokens, k_weight, preferred_element_type=F32).astype(BF16).reshape(view)
    values = jnp.dot(tokens, v_weight, preferred_element_type=F32).astype(BF16).reshape(view)
    lower = jnp.arange(rows_here)[:, None] >= jnp.arange(rows_here)[None, :]
    cumul = jnp.dot(lower.astype(F32), log_decay, precision=highest)
    last_cum = cumul[-1]
    ends = jnp.exp(last_cum[None, :] - cumul)
    state = jnp.einsum(
        "thd,the->hde",
        keys.astype(F32) * ends[:, :, None],
        values.astype(F32),
        precision=highest,
    )
    decay = jnp.broadcast_to(jnp.exp(last_cum)[:, None, None], (heads_here, 8, head_size))
    mine = jnp.concatenate([state, decay], axis=1)
    theirs = move(mine, other_core)
    first = jnp.where(c == 0, mine, theirs)
    second = jnp.where(c == 0, theirs, mine)
    first_s, first_d = first[:, :head_size], first[:, head_size : head_size + 1]
    second_s, second_d = second[:, :head_size], second[:, head_size : head_size + 1]
    chip = jnp.concatenate(
        [second_d * first_s + second_s, second[:, head_size:] * first[:, head_size:]], axis=1
    )
    arrived = [(s, move(chip, later_x(s))) for s in (3, 2, 1)]

    queries = jnp.dot(tokens, q_weight, preferred_element_type=F32).astype(BF16).reshape(view)
    scores = jnp.einsum("thd,shd->hts", queries, keys, preferred_element_type=F32)
    diff = jnp.transpose(cumul[:, None, :] - cumul[None, :, :], (2, 0, 1))
    weight = (scores * jnp.exp(jnp.where(lower[None], diff, -1e30))).astype(BF16)
    intra = jnp.einsum("hts,shd->thd", weight, values, preferred_element_type=F32)

    state_in = carried_state
    for s, message in arrived:
        d = jnp.where(x >= s, message[:, head_size : head_size + 1], 1.0)
        state_in = d * state_in + message[:, :head_size]
    state_in = jnp.where(c == 1, first_d * state_in + first_s, state_in)
    inter = jnp.exp(cumul)[:, :, None] * jnp.einsum(
        "thd,hde->the", queries.astype(F32), state_in, precision=highest
    )
    attended = intra + inter
    normed_heads = attended * lax.rsqrt(
        jnp.mean(attended * attended, axis=-1, keepdims=True) + 1e-06
    )
    flat_heads = normed_heads.astype(BF16).reshape(rows_here, heads_here * head_size)

    n_head = Z * Y
    rows_mine = rows_here // n_head
    share = jnp.dot(flat_heads, out_weight, preferred_element_type=F32).astype(BF16)
    shares = lax.all_to_all(share.reshape(n_head, rows_mine, -1), ("z", "y"), 0, 0)
    mixed = jnp.sum(shares.astype(F32), axis=0)
    own_tokens = lax.dynamic_slice_in_dim(tokens, (z * Y + y) * rows_mine, rows_mine, 0)
    resid = own_tokens.astype(F32) + mixed
    final_rows = (
        resid
        * lax.rsqrt(jnp.mean(resid * resid, axis=-1, keepdims=True) + 1e-06)
        * final_gain.astype(F32)
    ).astype(BF16)

    vocab_local = vocab_weight.shape[1]
    offset = (((x * CORE + c) * Z + z) * Y + y) * vocab_local
    columns = jnp.arange(vocab_local, dtype=jnp.int32)
    wanted = (targets - offset).reshape(X, CORE, Z, Y, rows_mine)
    wanted_by = (
        jnp.transpose(wanted[:, 0], (1, 2, 0, 3)).reshape(Z, -1),
        jnp.transpose(wanted[:, 1], (2, 1, 0, 3)).reshape(Y, -1),
    )

    def score(rows, want):
        logits = jnp.dot(rows, vocab_weight, preferred_element_type=F32)
        top = jnp.max(logits, axis=1)
        total = jnp.sum(jnp.exp(logits - top[:, None]), axis=1)
        hit = jnp.sum(jnp.where(columns[None, :] == want[:, None], logits, 0.0), axis=1)
        return jnp.stack([top, total, hit])

    on_x = spread(final_rows, x, along_x)
    plane = jnp.where(c == 0, y, z)
    ours = spread(on_x, plane.astype(jnp.int32), along_first)
    blocks = [(0, ours)] + [(s, move(ours, along_second(s))) for s in (1, 3, 2)]
    stats = jnp.zeros((3, CORE, 4, 128), F32)
    for s, block in blocks:
        swapped = move(block, other_core)
        for rows, core, place in ((block, c, jnp.where(c == 0, z, y)), (swapped, 1 - c, jnp.where(c == 0, y, z))):
            place = lax.rem(place + 4 - s, 4)
            want = jnp.where(
                core == 0,
                lax.dynamic_index_in_dim(wanted_by[0], place, 0, False),
                lax.dynamic_index_in_dim(wanted_by[1], place, 0, False),
            )
            found = score(rows, want)
            stats = lax.dynamic_update_slice(stats, found[:, None, None], (0, core, place, 0))

    stats = stats.reshape(3, CORE * 4 * 128)
    stats = merge([stats, move(stats, other_core)])
    for along in (along_x, along_z, along_y):
        stats = merge([stats] + [move(stats, along(s)) for s in (1, 3, 2)])
    loglik = stats[2] - stats[0] - jnp.log(stats[1])
    loglik = loglik.reshape(CORE, 4, 4, X, rows_mine)
    loglik = lax.dynamic_index_in_dim(loglik, x, 3, False)
    loglik = jnp.where(c == 0, loglik[0], jnp.transpose(loglik[1], (1, 0, 2)))
    return loglik.reshape(rows_here)


def solution(mesh):
    fine = Mesh(mesh.devices.reshape(X, CORE, Z, Y), ALL)
    seq, head = (("x", "core"), ("z", "y"))
    return jax.shard_map(
        shards,
        mesh=fine,
        in_specs=(
            P(seq, None),
            P(seq, head),
            P(head, None, None),
            P(None, head),
            P(None, head),
            P(None, head),
            P(head, None),
            P(),
            P(None, ALL),
            P(),
        ),
        out_specs=P(seq),
        check_vma=False,
    )
```

```python
import functools

import jax
import jax.numpy as jnp
from jax import lax
from jax.experimental import pallas as pl
from jax.experimental.pallas import tpu as pltpu
from jax.sharding import Mesh, PartitionSpec as P

X, CORE, Z, Y = 4, 2, 4, 4
ALL = ("x", "core", "z", "y")
F32 = jnp.float32
BF16 = jnp.bfloat16
HIGHEST = lax.Precision.HIGHEST


def move(array, target):
    pairs = []
    for i in range(X * CORE * Z * Y):
        at = (i // (CORE * Z * Y), i // (Z * Y) % CORE, i // Y % Z, i % Y)
        to = target(*at)
        if to is not None:
            pairs.append((i, ((to[0] * CORE + to[1]) * Z + to[2]) * Y + to[3]))
    return lax.ppermute(array, ALL, pairs)


def other_core(x, c, z, y):
    return (x, 1 - c, z, y)


def along_x(s):
    return lambda x, c, z, y: ((x + s) % X, c, z, y)


def along_y(s):
    return lambda x, c, z, y: (x, c, z, (y + s) % Y)


def along_z(s):
    return lambda x, c, z, y: (x, c, (z + s) % Z, y)


def along_p(s):
    return lambda x, c, z, y: (x, c, z, (y + s) % Y) if c == 0 else (x, c, (z + s) % Z, y)


def along_q(s):
    return lambda x, c, z, y: (x, c, (z + s) % Z, y) if c == 0 else (x, c, z, (y + s) % Y)


def later_x(s):
    return lambda x, c, z, y: (x + s, c, z, y) if x + s < X else None


def on_chip(shape, dtype):
    return pltpu.VMEM(shape, dtype)


def pin(array):
    return pltpu.with_memory_space_constraint(array, pltpu.VMEM)


SCALARS = pl.BlockSpec(memory_space=pltpu.SMEM)
WHOLE = pl.BlockSpec(memory_space=pltpu.VMEM)


def local(kernel, outs, scalars, *arrays, scratch=(), flops=0, bytes_=0, name=None):
    many = isinstance(outs, list)
    specs = [WHOLE] * len(outs) if many else WHOLE
    return pl.pallas_call(
        kernel,
        out_shape=outs,
        in_specs=[SCALARS] + [WHOLE] * len(arrays),
        out_specs=specs,
        scratch_shapes=list(scratch),
        compiler_params=pltpu.CompilerParams(vmem_limit_bytes=16 * 1024 * 1024),
        cost_estimate=pl.CostEstimate(flops=flops, bytes_accessed=bytes_, transcendentals=0),
        name=name,
    )(scalars, *[pin(a) for a in arrays])


def project_kernel(at, heads, weight, own, one, two, three, rolled):
    p = at[4]
    for s in range(4):
        start = pl.multiple_of((p + s) % 4 * 32, 32)
        rolled[pl.ds(32 * s, 32), :] = heads[pl.ds(start, 32), :]
    wide = 512 if weight.shape[1] % 512 == 0 else 128

    def step(n, carry):
        cols = pl.ds(pl.multiple_of(n * wide, wide), wide)
        out = jnp.dot(rolled[...], weight[:, cols], preferred_element_type=F32)
        own[:, cols] = out[:32]
        one[:, cols] = out[32:64].astype(BF16)
        two[:, cols] = out[64:96].astype(BF16)
        three[:, cols] = out[96:].astype(BF16)
        return carry

    lax.fori_loop(0, weight.shape[1] // wide, step, 0)


def partial_kernel(at, own, one, two, three, mine, first, second, third, total):
    q = at[5]
    total[...] = (
        own[...]
        + one[...].astype(F32)
        + two[...].astype(F32)
        + three[...].astype(F32)
    )
    for s, out in enumerate((mine, first, second, third)):
        start = pl.multiple_of((q + s) % 4 * 8, 8)
        out[...] = total[pl.ds(start, 8), :].astype(out.dtype)


def norm_kernel(at, own, one, two, three, tokens, gain, out):
    resid = (
        tokens[...]
        + own[...]
        + one[...].astype(F32)
        + two[...].astype(F32)
        + three[...].astype(F32)
    )
    scale = lax.rsqrt(jnp.mean(resid * resid, axis=1, keepdims=True) + 1e-06)
    out[...] = (resid * scale * gain[...].astype(F32)).astype(BF16)


def stack_kernel(at, a, b, c, d, out):
    rows = a.shape[0]
    out[0 : 2 * rows, :] = jnp.concatenate([a[...], b[...]], axis=0)
    out[2 * rows : 4 * rows, :] = jnp.concatenate([c[...], d[...]], axis=0)


def gather(block, target, scalars, name):
    parts = [move(block, target(s)) for s in (1, 2, 3)]
    rows, width = block.shape
    return local(
        stack_kernel,
        on_chip((4 * rows, width), block.dtype),
        scalars,
        block,
        *parts,
        bytes_=16 * rows * width,
        name=name,
    )


def score_kernel(shift, own, at, targets, rows, weight, out, logits):
    x = at[0]
    p, q, core = (at[4], at[5], at[1]) if own else (at[5], at[4], 1 - at[1])
    n_rows, width = rows.shape[0], weight.shape[1]
    tile = 256

    def step(n, carry):
        cols = pl.ds(pl.multiple_of(n * tile, tile), tile)
        logits[:, cols] = jnp.dot(rows[...], weight[:, cols], preferred_element_type=F32)
        return carry

    lax.fori_loop(0, width // tile, step, 0)
    i = lax.broadcasted_iota(jnp.int32, (n_rows, n_rows), 0)
    j = lax.broadcasted_iota(jnp.int32, (n_rows, n_rows), 1)
    lands = (
        (((p + 4 - i // 32) & 3) == j // 32)
        & (((x + 4 - (i // 8 & 3)) & 3) == (j // 8 & 3))
        & ((i & 7) == (j & 7))
    )
    place = core * 4 + ((q + 4 - shift) & 3)
    line = targets[pl.ds(place, 1), :] - at[6]
    want = jnp.sum(jnp.where(lands, line, 0), axis=1, keepdims=True)
    found = logits[...]
    top = jnp.max(found, axis=1, keepdims=True)
    total = jnp.sum(jnp.exp(found - top), axis=1, keepdims=True)
    column = lax.broadcasted_iota(jnp.int32, found.shape, 1)
    hit = jnp.sum(jnp.where(column == want, found, 0.0), axis=1, keepdims=True)
    both = jnp.where(j == 0, top, jnp.where(j == 1, total, jnp.where(j == 2, hit, 0.0)))
    turned = jnp.transpose(both)[:8]
    out[...] = jnp.dot(
        turned, lands.astype(F32), precision=HIGHEST, preferred_element_type=F32
    )


def place_kernel(at, *refs):
    blocks, out = refs[:-1], refs[-1]
    for k, block in enumerate(blocks):
        shift, own = k // 2, k % 2 == 0
        q, core = (at[5], at[1]) if own else (at[4], 1 - at[1])
        place = core * 4 + ((q + 4 - shift) & 3)
        for row in range(3):
            out[pl.ds(8 * row + place, 1), :] = block[row : row + 1, :]


def merged(parts):
    top = parts[0][0:8, :]
    for part in parts[1:]:
        top = jnp.maximum(top, part[0:8, :])
    total = sum(part[8:16, :] * jnp.exp(part[0:8, :] - top) for part in parts)
    hit = sum(part[16:24, :] for part in parts)
    return top, total, hit


def merge_kernel(at, *refs):
    top, total, hit = merged(refs[:-1])
    refs[-1][0:8, :] = top
    refs[-1][8:16, :] = total
    refs[-1][16:24, :] = hit


def finish_kernel(at, *refs):
    top, total, hit = merged(refs[:-2])
    out, found = refs[-2], refs[-1]
    found[...] = hit - top - jnp.log(total)
    i = lax.broadcasted_iota(jnp.int32, (128, 128), 0)
    j = lax.broadcasted_iota(jnp.int32, (128, 128), 1)
    here = jnp.zeros((1, 128), F32)
    for q in range(4):
        takes = (
            (i // 32 == j // 32)
            & ((i // 8 & 3) == at[0])
            & ((j // 8 & 3) == q)
            & ((i & 7) == (j & 7))
        )
        here = here + jnp.dot(
            found[pl.ds(at[1] * 4 + q, 1), :],
            takes.astype(F32),
            precision=HIGHEST,
            preferred_element_type=F32,
        )
    out[...] = here


def shards(
    tokens,
    log_decay,
    carried_state,
    q_weight,
    k_weight,
    v_weight,
    out_weight,
    final_gain,
    vocab_weight,
    targets,
):
    x, c, z, y = (lax.axis_index(a) for a in ALL)
    p, q = jnp.where(c == 0, y, z), jnp.where(c == 0, z, y)
    rows_here, width = tokens.shape
    heads_here = carried_state.shape[0]
    head_size = carried_state.shape[1]
    view = (rows_here, heads_here, head_size)
    vocab_local = vocab_weight.shape[1]
    offset = (((x * CORE + c) * Z + z) * Y + y) * vocab_local
    scalars = jnp.stack([x, c, z, y, p, q, offset, offset]).astype(jnp.int32)

    keys = jnp.dot(tokens, k_weight, preferred_element_type=F32).astype(BF16).reshape(view)
    values = jnp.dot(tokens, v_weight, preferred_element_type=F32).astype(BF16).reshape(view)
    lower = jnp.arange(rows_here)[:, None] >= jnp.arange(rows_here)[None, :]
    cumul = jnp.dot(lower.astype(F32), log_decay, precision=HIGHEST)
    last_cum = cumul[-1]
    ends = jnp.exp(last_cum[None, :] - cumul)
    state = jnp.einsum(
        "thd,the->hde",
        keys.astype(F32) * ends[:, :, None],
        values.astype(F32),
        precision=HIGHEST,
    )
    decay = jnp.broadcast_to(jnp.exp(last_cum)[:, None, None], (heads_here, 8, head_size))
    mine = jnp.concatenate([state, decay], axis=1)
    theirs = move(mine, other_core)
    first = jnp.where(c == 0, mine, theirs)
    second = jnp.where(c == 0, theirs, mine)
    first_s, first_d = first[:, :head_size], first[:, head_size : head_size + 1]
    second_s, second_d = second[:, :head_size], second[:, head_size : head_size + 1]
    chip = jnp.concatenate(
        [second_d * first_s + second_s, second[:, head_size:] * first[:, head_size:]], axis=1
    )
    arrived = [(s, move(chip, later_x(s))) for s in (3, 2, 1)]

    queries = jnp.dot(tokens, q_weight, preferred_element_type=F32).astype(BF16).reshape(view)
    scores = jnp.einsum("thd,shd->hts", queries, keys, preferred_element_type=F32)
    diff = jnp.transpose(cumul[:, None, :] - cumul[None, :, :], (2, 0, 1))
    weight = (scores * jnp.exp(jnp.where(lower[None], diff, -1e30))).astype(BF16)
    intra = jnp.einsum("hts,shd->thd", weight, values, preferred_element_type=F32)

    state_in = carried_state
    for s, message in arrived:
        d = jnp.where(x >= s, message[:, head_size : head_size + 1], 1.0)
        state_in = d * state_in + message[:, :head_size]
    state_in = jnp.where(c == 1, first_d * state_in + first_s, state_in)
    inter = jnp.exp(cumul)[:, :, None] * jnp.einsum(
        "thd,hde->the", queries.astype(F32), state_in, precision=HIGHEST
    )
    attended = intra + inter
    normed_heads = attended * lax.rsqrt(
        jnp.mean(attended * attended, axis=-1, keepdims=True) + 1e-06
    )
    flat_heads = normed_heads.astype(BF16).reshape(rows_here, heads_here * head_size)

    own, *sent = local(
        project_kernel,
        [on_chip((32, width), F32)] + [on_chip((32, width), BF16)] * 3,
        scalars,
        flat_heads,
        out_weight,
        scratch=[pltpu.VMEM(flat_heads.shape, BF16)],
        flops=2 * rows_here * flat_heads.shape[1] * width,
        bytes_=2 * width * (flat_heads.shape[1] + rows_here),
        name="project",
    )
    came = [move(part, along_p(s)) for s, part in zip((1, 2, 3), sent)]
    own, *sent = local(
        partial_kernel,
        [on_chip((8, width), F32)] + [on_chip((8, width), BF16)] * 3,
        scalars,
        own,
        *came,
        scratch=[pltpu.VMEM((32, width), F32)],
        bytes_=32 * width * 8,
        name="partial",
    )
    came = [move(part, along_q(s)) for s, part in zip((1, 2, 3), sent)]
    own_tokens = lax.dynamic_slice_in_dim(tokens, 32 * p + 8 * q, 8, 0).astype(F32)
    final_rows = local(
        norm_kernel,
        on_chip((8, width), BF16),
        scalars,
        own,
        *came,
        own_tokens,
        final_gain.reshape(1, width),
        bytes_=8 * width * 16,
        name="norm",
    )

    on_x = gather(final_rows, along_x, scalars, "stack_x")
    ours = gather(on_x, along_p, scalars, "stack_p")
    theirs = move(ours, other_core)
    ours, theirs = lax.optimization_barrier((ours, theirs))
    lines = jnp.transpose(targets.reshape(X, CORE, 4, 4, 8), (1, 3, 2, 0, 4)).reshape(8, 128)
    pairs = [(ours, theirs)]
    for s in (1, 3, 2):
        block = move(ours, along_q(s))
        pairs.append((block, move(block, other_core)))
    pairs = [pairs[0], pairs[1], pairs[3], pairs[2]]
    found = []
    for s, pair in enumerate(pairs):
        for mine_too, block in zip((True, False), pair):
            found.append(
                local(
                    functools.partial(score_kernel, s, mine_too),
                    on_chip((8, 128), F32),
                    scalars,
                    lines,
                    block,
                    vocab_weight,
                    scratch=[pltpu.VMEM((128, vocab_local), F32)],
                    flops=2 * 128 * width * vocab_local,
                    bytes_=2 * width * (128 + vocab_local),
                    name="score",
                )
            )
    stats = local(place_kernel, on_chip((24, 128), F32), scalars, *found, name="place")
    stats = local(
        merge_kernel, on_chip((24, 128), F32), scalars, stats, move(stats, other_core), name="merge"
    )
    for along in (along_x, along_z):
        parts = [stats] + [move(stats, along(s)) for s in (1, 3, 2)]
        stats = local(merge_kernel, on_chip((24, 128), F32), scalars, *parts, name="merge")
    parts = [stats] + [move(stats, along_y(s)) for s in (1, 3, 2)]
    loglik = local(
        finish_kernel,
        jax.ShapeDtypeStruct((1, 128), F32),
        scalars,
        *parts,
        scratch=[pltpu.VMEM((8, 128), F32)],
        name="finish",
    )
    return loglik.reshape(rows_here)


def solution(mesh):
    fine = Mesh(mesh.devices.reshape(X, CORE, Z, Y), ALL)
    seq, head = (("x", "core"), ("z", "y"))
    return jax.shard_map(
        shards,
        mesh=fine,
        in_specs=(
            P(seq, None),
            P(seq, head),
            P(head, None, None),
            P(None, head),
            P(None, head),
            P(None, head),
            P(head, None),
            P(),
            P(None, ALL),
            P(),
        ),
        out_specs=P(seq),
        check_vma=False,
    )
```

```python
import functools

import jax
import jax.numpy as jnp
from jax import lax
from jax.experimental import pallas as pl
from jax.experimental.pallas import tpu as pltpu
from jax.sharding import Mesh, PartitionSpec as P

X, CORE, Z, Y = 4, 2, 4, 4
ALL = ("x", "core", "z", "y")
F32 = jnp.float32
BF16 = jnp.bfloat16
HIGHEST = lax.Precision.HIGHEST


def move(array, target):
    pairs = []
    for i in range(X * CORE * Z * Y):
        at = (i // (CORE * Z * Y), i // (Z * Y) % CORE, i // Y % Z, i % Y)
        to = target(*at)
        if to is not None:
            pairs.append((i, ((to[0] * CORE + to[1]) * Z + to[2]) * Y + to[3]))
    return lax.ppermute(array, ALL, pairs)


def other_core(x, c, z, y):
    return (x, 1 - c, z, y)


def along_x(s):
    return lambda x, c, z, y: ((x + s) % X, c, z, y)


def along_y(s):
    return lambda x, c, z, y: (x, c, z, (y + s) % Y)


def along_z(s):
    return lambda x, c, z, y: (x, c, (z + s) % Z, y)


def along_p(s):
    return lambda x, c, z, y: (x, c, z, (y + s) % Y) if c == 0 else (x, c, (z + s) % Z, y)


def along_q(s):
    return lambda x, c, z, y: (x, c, (z + s) % Z, y) if c == 0 else (x, c, z, (y + s) % Y)


def later_x(s):
    return lambda x, c, z, y: (x + s, c, z, y) if x + s < X else None


def on_chip(shape, dtype):
    return pltpu.VMEM(shape, dtype)


def pin(array):
    return pltpu.with_memory_space_constraint(array, pltpu.VMEM)


ANYWHERE = pl.BlockSpec(memory_space=pl.ANY)
SCALARS = pl.BlockSpec(memory_space=pltpu.SMEM)
WHOLE = pl.BlockSpec(memory_space=pltpu.VMEM)


def local(kernel, outs, scalars, *arrays, unread=(), scratch=(), flops=0, bytes_=0, mib=4, name=None):
    many = isinstance(outs, list)
    specs = [WHOLE] * len(outs) if many else WHOLE
    return pl.pallas_call(
        kernel,
        out_shape=outs,
        in_specs=[SCALARS] + [WHOLE] * len(arrays) + [ANYWHERE] * len(unread),
        out_specs=specs,
        scratch_shapes=list(scratch),
        compiler_params=pltpu.CompilerParams(vmem_limit_bytes=mib * 1024 * 1024),
        cost_estimate=pl.CostEstimate(flops=flops, bytes_accessed=bytes_, transcendentals=0),
        name=name,
    )(scalars, *[pin(a) for a in (*arrays, *unread)])


def tie_kernel(a, b, out_a, out_b):
    pass


def tie(a, b):
    return pl.pallas_call(
        tie_kernel,
        out_shape=[on_chip(a.shape, a.dtype), on_chip(b.shape, b.dtype)],
        in_specs=[ANYWHERE] * 2,
        out_specs=[ANYWHERE] * 2,
        input_output_aliases={0: 0, 1: 1},
        compiler_params=pltpu.CompilerParams(vmem_limit_bytes=1024 * 1024),
        name="tie",
    )(pin(a), pin(b))


def project_kernel(at, heads, weight, own, one, two, three, rolled):
    p = at[4]
    for s in range(4):
        start = pl.multiple_of((p + s) % 4 * 32, 32)
        rolled[pl.ds(32 * s, 32), :] = heads[pl.ds(start, 32), :]
    wide = 512 if weight.shape[1] % 512 == 0 else 128

    def step(n, carry):
        cols = pl.ds(pl.multiple_of(n * wide, wide), wide)
        out = jnp.dot(rolled[...], weight[:, cols], preferred_element_type=F32)
        own[:, cols] = out[:32]
        one[:, cols] = out[32:64].astype(BF16)
        two[:, cols] = out[64:96].astype(BF16)
        three[:, cols] = out[96:].astype(BF16)
        return carry

    lax.fori_loop(0, weight.shape[1] // wide, step, 0)


def partial_kernel(at, own, one, two, three, mine, first, second, third, total):
    q = at[5]
    total[...] = (
        own[...]
        + one[...].astype(F32)
        + two[...].astype(F32)
        + three[...].astype(F32)
    )
    for s, out in enumerate((mine, first, second, third)):
        start = pl.multiple_of((q + s) % 4 * 8, 8)
        out[...] = total[pl.ds(start, 8), :].astype(out.dtype)


def norm_kernel(at, own, one, two, three, tokens, gain, out):
    resid = (
        tokens[...]
        + own[...]
        + one[...].astype(F32)
        + two[...].astype(F32)
        + three[...].astype(F32)
    )
    scale = lax.rsqrt(jnp.mean(resid * resid, axis=1, keepdims=True) + 1e-06)
    out[...] = (resid * scale * gain[...].astype(F32)).astype(BF16)


def stack_kernel(at, a, b, c, d, out):
    rows = a.shape[0]
    out[0 : 2 * rows, :] = jnp.concatenate([a[...], b[...]], axis=0)
    out[2 * rows : 4 * rows, :] = jnp.concatenate([c[...], d[...]], axis=0)


def gather(block, target, scalars, name):
    parts = [move(block, target(s)) for s in (1, 2, 3)]
    rows, width = block.shape
    return local(
        stack_kernel,
        on_chip((4 * rows, width), block.dtype),
        scalars,
        block,
        *parts,
        bytes_=16 * rows * width,
        mib=8,
        name=name,
    )


def score_kernel(shift, own, at, targets, logits, rows, out):
    x = at[0]
    p, q, core = (at[4], at[5], at[1]) if own else (at[5], at[4], 1 - at[1])
    n_rows = rows.shape[0]
    i = lax.broadcasted_iota(jnp.int32, (n_rows, n_rows), 0)
    j = lax.broadcasted_iota(jnp.int32, (n_rows, n_rows), 1)
    lands = (
        (((p + 4 - i // 32) & 3) == j // 32)
        & (((x + 4 - (i // 8 & 3)) & 3) == (j // 8 & 3))
        & ((i & 7) == (j & 7))
    )
    place = core * 4 + ((q + 4 - shift) & 3)
    line = targets[pl.ds(place, 1), :] - at[6]
    want = jnp.sum(jnp.where(lands, line, 0), axis=1, keepdims=True)
    found = logits[...]
    top = jnp.max(found, axis=1, keepdims=True)
    total = jnp.sum(jnp.exp(found - top), axis=1, keepdims=True)
    column = lax.broadcasted_iota(jnp.int32, found.shape, 1)
    hit = jnp.sum(jnp.where(column == want, found, 0.0), axis=1, keepdims=True)
    both = jnp.where(j == 0, top, jnp.where(j == 1, total, jnp.where(j == 2, hit, 0.0)))
    turned = jnp.transpose(both)[:8]
    out[...] = jnp.dot(
        turned, lands.astype(F32), precision=HIGHEST, preferred_element_type=F32
    )


def place_kernel(at, *refs):
    blocks, out = refs[:-1], refs[-1]
    for k, block in enumerate(blocks):
        shift, own = k // 2, k % 2 == 0
        q, core = (at[5], at[1]) if own else (at[4], 1 - at[1])
        place = core * 4 + ((q + 4 - shift) & 3)
        for row in range(3):
            out[pl.ds(8 * row + place, 1), :] = block[row : row + 1, :]


def merged(parts):
    top = parts[0][0:8, :]
    for part in parts[1:]:
        top = jnp.maximum(top, part[0:8, :])
    total = sum(part[8:16, :] * jnp.exp(part[0:8, :] - top) for part in parts)
    hit = sum(part[16:24, :] for part in parts)
    return top, total, hit


def merge_kernel(at, *refs):
    top, total, hit = merged(refs[:-1])
    refs[-1][0:8, :] = top
    refs[-1][8:16, :] = total
    refs[-1][16:24, :] = hit


def finish_kernel(at, *refs):
    top, total, hit = merged(refs[:-2])
    out, found = refs[-2], refs[-1]
    found[...] = hit - top - jnp.log(total)
    i = lax.broadcasted_iota(jnp.int32, (128, 128), 0)
    j = lax.broadcasted_iota(jnp.int32, (128, 128), 1)
    here = jnp.zeros((1, 128), F32)
    for q in range(4):
        takes = (
            (i // 32 == j // 32)
            & ((i // 8 & 3) == at[0])
            & ((j // 8 & 3) == q)
            & ((i & 7) == (j & 7))
        )
        here = here + jnp.dot(
            found[pl.ds(at[1] * 4 + q, 1), :],
            takes.astype(F32),
            precision=HIGHEST,
            preferred_element_type=F32,
        )
    out[...] = here


def shards(
    tokens,
    log_decay,
    carried_state,
    q_weight,
    k_weight,
    v_weight,
    out_weight,
    final_gain,
    vocab_weight,
    targets,
):
    x, c, z, y = (lax.axis_index(a) for a in ALL)
    p, q = jnp.where(c == 0, y, z), jnp.where(c == 0, z, y)
    rows_here, width = tokens.shape
    heads_here = carried_state.shape[0]
    head_size = carried_state.shape[1]
    view = (rows_here, heads_here, head_size)
    vocab_local = vocab_weight.shape[1]
    offset = (((x * CORE + c) * Z + z) * Y + y) * vocab_local
    scalars = jnp.stack([x, c, z, y, p, q, offset, offset]).astype(jnp.int32)

    keys = jnp.dot(tokens, k_weight, preferred_element_type=F32).astype(BF16).reshape(view)
    values = jnp.dot(tokens, v_weight, preferred_element_type=F32).astype(BF16).reshape(view)
    lower = jnp.arange(rows_here)[:, None] >= jnp.arange(rows_here)[None, :]
    cumul = jnp.dot(lower.astype(F32), log_decay, precision=HIGHEST)
    last_cum = cumul[-1]
    ends = jnp.exp(last_cum[None, :] - cumul)
    state = jnp.einsum(
        "thd,the->hde",
        keys.astype(F32) * ends[:, :, None],
        values.astype(F32),
        precision=HIGHEST,
    )
    decay = jnp.broadcast_to(jnp.exp(last_cum)[:, None, None], (heads_here, 8, head_size))
    mine = jnp.concatenate([state, decay], axis=1)
    theirs = move(mine, other_core)
    first = jnp.where(c == 0, mine, theirs)
    second = jnp.where(c == 0, theirs, mine)
    first_s, first_d = first[:, :head_size], first[:, head_size : head_size + 1]
    second_s, second_d = second[:, :head_size], second[:, head_size : head_size + 1]
    chip = jnp.concatenate(
        [second_d * first_s + second_s, second[:, head_size:] * first[:, head_size:]], axis=1
    )
    arrived = [(s, move(chip, later_x(s))) for s in (3, 2, 1)]

    queries = jnp.dot(tokens, q_weight, preferred_element_type=F32).astype(BF16).reshape(view)
    scores = jnp.einsum("thd,shd->hts", queries, keys, preferred_element_type=F32)
    diff = jnp.transpose(cumul[:, None, :] - cumul[None, :, :], (2, 0, 1))
    weight = (scores * jnp.exp(jnp.where(lower[None], diff, -1e30))).astype(BF16)
    intra = jnp.einsum("hts,shd->thd", weight, values, preferred_element_type=F32)

    state_in = carried_state
    for s, message in arrived:
        d = jnp.where(x >= s, message[:, head_size : head_size + 1], 1.0)
        state_in = d * state_in + message[:, :head_size]
    state_in = jnp.where(c == 1, first_d * state_in + first_s, state_in)
    inter = jnp.exp(cumul)[:, :, None] * jnp.einsum(
        "thd,hde->the", queries.astype(F32), state_in, precision=HIGHEST
    )
    attended = intra + inter
    normed_heads = attended * lax.rsqrt(
        jnp.mean(attended * attended, axis=-1, keepdims=True) + 1e-06
    )
    flat_heads = normed_heads.astype(BF16).reshape(rows_here, heads_here * head_size)

    own, *sent = local(
        project_kernel,
        [on_chip((32, width), F32)] + [on_chip((32, width), BF16)] * 3,
        scalars,
        flat_heads,
        out_weight,
        scratch=[pltpu.VMEM(flat_heads.shape, BF16)],
        flops=2 * rows_here * flat_heads.shape[1] * width,
        bytes_=2 * width * (flat_heads.shape[1] + rows_here),
        mib=16,
        name="project",
    )
    came = [move(part, along_p(s)) for s, part in zip((1, 2, 3), sent)]
    own, *sent = local(
        partial_kernel,
        [on_chip((8, width), F32)] + [on_chip((8, width), BF16)] * 3,
        scalars,
        own,
        *came,
        scratch=[pltpu.VMEM((32, width), F32)],
        bytes_=32 * width * 8,
        mib=8,
        name="partial",
    )
    came = [move(part, along_q(s)) for s, part in zip((1, 2, 3), sent)]
    own_tokens = lax.dynamic_slice_in_dim(tokens, 32 * p + 8 * q, 8, 0).astype(F32)
    final_rows = local(
        norm_kernel,
        on_chip((8, width), BF16),
        scalars,
        own,
        *came,
        own_tokens,
        final_gain.reshape(1, width),
        bytes_=8 * width * 16,
        name="norm",
    )

    on_x = gather(final_rows, along_x, scalars, "stack_x")
    ours = gather(on_x, along_p, scalars, "stack_p")
    theirs = move(ours, other_core)
    ours, theirs = tie(ours, theirs)
    lines = jnp.transpose(targets.reshape(X, CORE, 4, 4, 8), (1, 3, 2, 0, 4)).reshape(8, 128)
    pairs = [(ours, theirs)]
    for s in (1, 3, 2):
        block = move(ours, along_q(s))
        pairs.append((block, move(block, other_core)))
    pairs = [pairs[0], pairs[1], pairs[3], pairs[2]]
    found = []
    for s, pair in enumerate(pairs):
        for mine_too, block in zip((True, False), pair):
            logits = jnp.dot(block, vocab_weight, preferred_element_type=F32)
            found.append(
                local(
                    functools.partial(score_kernel, s, mine_too),
                    on_chip((8, 128), F32),
                    scalars,
                    lines,
                    logits,
                    unread=(block,),
                    bytes_=4 * 128 * vocab_local,
                    name="score",
                )
            )
    stats = local(place_kernel, on_chip((24, 128), F32), scalars, *found, name="place")
    stats = local(
        merge_kernel, on_chip((24, 128), F32), scalars, stats, move(stats, other_core), name="merge"
    )
    for along in (along_x, along_z):
        parts = [stats] + [move(stats, along(s)) for s in (1, 3, 2)]
        stats = local(merge_kernel, on_chip((24, 128), F32), scalars, *parts, name="merge")
    parts = [stats] + [move(stats, along_y(s)) for s in (1, 3, 2)]
    loglik = local(
        finish_kernel,
        jax.ShapeDtypeStruct((1, 128), F32),
        scalars,
        *parts,
        scratch=[pltpu.VMEM((8, 128), F32)],
        name="finish",
    )
    return loglik.reshape(rows_here)


def solution(mesh):
    fine = Mesh(mesh.devices.reshape(X, CORE, Z, Y), ALL)
    seq, head = (("x", "core"), ("z", "y"))
    return jax.shard_map(
        shards,
        mesh=fine,
        in_specs=(
            P(seq, None),
            P(seq, head),
            P(head, None, None),
            P(None, head),
            P(None, head),
            P(None, head),
            P(head, None),
            P(),
            P(None, ALL),
            P(),
        ),
        out_specs=P(seq),
        check_vma=False,
    )
```

```python
import functools

import jax
import jax.numpy as jnp
from jax import lax
from jax.experimental import pallas as pl
from jax.experimental.pallas import tpu as pltpu
from jax.sharding import Mesh, PartitionSpec as P

X, CORE, Z, Y = 4, 2, 4, 4
ALL = ("x", "core", "z", "y")
F32 = jnp.float32
BF16 = jnp.bfloat16
HIGHEST = lax.Precision.HIGHEST


def move(array, target):
    pairs = []
    for i in range(X * CORE * Z * Y):
        at = (i // (CORE * Z * Y), i // (Z * Y) % CORE, i // Y % Z, i % Y)
        to = target(*at)
        if to is not None:
            pairs.append((i, ((to[0] * CORE + to[1]) * Z + to[2]) * Y + to[3]))
    return lax.ppermute(array, ALL, pairs)


def other_core(x, c, z, y):
    return (x, 1 - c, z, y)


def near(axis, step):
    def target(*at):
        to = list(at)
        to[axis] = (at[axis] + (1 if at[axis] % 2 == step else 3)) % 4
        return tuple(to)

    return target


def along_x(s):
    return lambda x, c, z, y: ((x + s) % X, c, z, y)


def along_p(s):
    return lambda x, c, z, y: (x, c, z, (y + s) % Y) if c == 0 else (x, c, (z + s) % Z, y)


def along_q(s):
    return lambda x, c, z, y: (x, c, (z + s) % Z, y) if c == 0 else (x, c, z, (y + s) % Y)


def later_x(s):
    return lambda x, c, z, y: (x + s, c, z, y) if x + s < X else None


def on_chip(shape, dtype):
    return pltpu.VMEM(shape, dtype)


def pin(array):
    return pltpu.with_memory_space_constraint(array, pltpu.VMEM)


ANYWHERE = pl.BlockSpec(memory_space=pl.ANY)
SCALARS = pl.BlockSpec(memory_space=pltpu.SMEM)
WHOLE = pl.BlockSpec(memory_space=pltpu.VMEM)


def local(kernel, outs, scalars, *arrays, unread=(), scratch=(), flops=0, bytes_=0, mib=4, name=None):
    many = isinstance(outs, list)
    specs = [WHOLE] * len(outs) if many else WHOLE
    return pl.pallas_call(
        kernel,
        out_shape=outs,
        in_specs=[SCALARS] + [WHOLE] * len(arrays) + [ANYWHERE] * len(unread),
        out_specs=specs,
        scratch_shapes=list(scratch),
        compiler_params=pltpu.CompilerParams(vmem_limit_bytes=mib * 1024 * 1024),
        cost_estimate=pl.CostEstimate(flops=flops, bytes_accessed=bytes_, transcendentals=0),
        name=name,
    )(scalars, *[pin(a) for a in (*arrays, *unread)])


def tie_kernel(a, b, out_a, out_b):
    pass


def tie(a, b):
    return pl.pallas_call(
        tie_kernel,
        out_shape=[on_chip(a.shape, a.dtype), on_chip(b.shape, b.dtype)],
        in_specs=[ANYWHERE] * 2,
        out_specs=[ANYWHERE] * 2,
        input_output_aliases={0: 0, 1: 1},
        compiler_params=pltpu.CompilerParams(vmem_limit_bytes=1024 * 1024),
        name="tie",
    )(pin(a), pin(b))


def project_kernel(at, heads, weight, own, one, two, three, rolled):
    @pl.when(pl.program_id(0) == 0)
    def _():
        for s in range(4):
            start = pl.multiple_of((at[4] + s) % 4 * 32, 32)
            rolled[pl.ds(32 * s, 32), :] = heads[pl.ds(start, 32), :]

    out = jnp.dot(rolled[...], weight[...], preferred_element_type=F32)
    own[...] = out[:32]
    one[...] = out[32:64].astype(BF16)
    two[...] = out[64:96].astype(BF16)
    three[...] = out[96:].astype(BF16)


def partial_kernel(at, own, one, two, three, mine, first, second, third, total):
    q = at[5]
    total[...] = (
        own[...]
        + one[...].astype(F32)
        + two[...].astype(F32)
        + three[...].astype(F32)
    )
    for s, out in enumerate((mine, first, second, third)):
        start = pl.multiple_of((q + s) % 4 * 8, 8)
        out[...] = total[pl.ds(start, 8), :].astype(out.dtype)


def norm_kernel(at, own, one, two, three, tokens, gain, out):
    resid = (
        tokens[...]
        + own[...]
        + one[...].astype(F32)
        + two[...].astype(F32)
        + three[...].astype(F32)
    )
    scale = lax.rsqrt(jnp.mean(resid * resid, axis=1, keepdims=True) + 1e-06)
    out[...] = (resid * scale * gain[...].astype(F32)).astype(BF16)


def stack_kernel(at, a, b, c, d, out):
    rows = a.shape[0]
    out[0 : 2 * rows, :] = jnp.concatenate([a[...], b[...]], axis=0)
    out[2 * rows : 4 * rows, :] = jnp.concatenate([c[...], d[...]], axis=0)


def gather(block, target, scalars, name):
    parts = [move(block, target(s)) for s in (1, 2, 3)]
    rows, width = block.shape
    return local(
        stack_kernel,
        on_chip((4 * rows, width), block.dtype),
        scalars,
        block,
        *parts,
        bytes_=16 * rows * width,
        mib=8,
        name=name,
    )


def score_kernel(shift, own, parts, at, targets, *refs):
    x = at[0]
    p, q, core = (at[4], at[5], at[1]) if own else (at[5], at[4], 1 - at[1])
    out = refs[-1]
    found = jnp.concatenate([ref[...] for ref in refs[:parts]], axis=0)
    n_rows = found.shape[0]
    i = lax.broadcasted_iota(jnp.int32, (n_rows, n_rows), 0)
    j = lax.broadcasted_iota(jnp.int32, (n_rows, n_rows), 1)
    lands = (
        (((p + 4 - i // 32) & 3) == j // 32)
        & (((x + 4 - (i // 8 & 3)) & 3) == (j // 8 & 3))
        & ((i & 7) == (j & 7))
    )
    place = core * 4 + ((q + 4 - shift) & 3)
    line = targets[pl.ds(place, 1), :] - at[6]
    want = jnp.sum(jnp.where(lands, line, 0), axis=1, keepdims=True)
    top = jnp.max(found, axis=1, keepdims=True)
    total = jnp.sum(jnp.exp(found - top), axis=1, keepdims=True)
    column = lax.broadcasted_iota(jnp.int32, found.shape, 1)
    hit = jnp.sum(jnp.where(column == want, found, 0.0), axis=1, keepdims=True)
    both = jnp.where(j == 0, top, jnp.where(j == 1, total, jnp.where(j == 2, hit, 0.0)))
    turned = jnp.transpose(both)[:8]
    out[...] = jnp.dot(
        turned, lands.astype(F32), precision=HIGHEST, preferred_element_type=F32
    )


def place_kernel(at, *refs):
    blocks, out = refs[:-1], refs[-1]
    for k, block in enumerate(blocks):
        shift, own = k // 2, k % 2 == 0
        q, core = (at[5], at[1]) if own else (at[4], 1 - at[1])
        place = core * 4 + ((q + 4 - shift) & 3)
        for row in range(3):
            out[pl.ds(8 * row + place, 1), :] = block[row : row + 1, :]


def merged(parts):
    top = parts[0][0:8, :]
    for part in parts[1:]:
        top = jnp.maximum(top, part[0:8, :])
    total = sum(part[8:16, :] * jnp.exp(part[0:8, :] - top) for part in parts)
    hit = sum(part[16:24, :] for part in parts)
    return top, total, hit


def merge_kernel(at, *refs):
    top, total, hit = merged(refs[:-1])
    refs[-1][0:8, :] = top
    refs[-1][8:16, :] = total
    refs[-1][16:24, :] = hit


def finish_kernel(at, *refs):
    top, total, hit = merged(refs[:-2])
    out, turned = refs[-2], refs[-1]
    found = hit - top - jnp.log(total)
    lane = lax.broadcasted_iota(jnp.int32, (8, 128), 1)
    here = jnp.zeros((1, 128), F32)
    for q in range(4):
        turn = (8 * q + 128 - 8 * at[0]) % 128
        turned[...] = jnp.where((lane // 8 & 3) == q, pltpu.roll(found, turn, 1), 0.0)
        here = here + turned[pl.ds(at[1] * 4 + q, 1), :]
    out[...] = here


def shards(
    tokens,
    log_decay,
    carried_state,
    q_weight,
    k_weight,
    v_weight,
    out_weight,
    final_gain,
    vocab_weight,
    targets,
):
    x, c, z, y = (lax.axis_index(a) for a in ALL)
    p, q = jnp.where(c == 0, y, z), jnp.where(c == 0, z, y)
    rows_here, width = tokens.shape
    heads_here = carried_state.shape[0]
    head_size = carried_state.shape[1]
    view = (rows_here, heads_here, head_size)
    vocab_local = vocab_weight.shape[1]
    offset = (((x * CORE + c) * Z + z) * Y + y) * vocab_local
    scalars = jnp.stack([x, c, z, y, p, q, offset, offset]).astype(jnp.int32)

    keys = jnp.dot(tokens, k_weight, preferred_element_type=F32).astype(BF16).reshape(view)
    values = jnp.dot(tokens, v_weight, preferred_element_type=F32).astype(BF16).reshape(view)
    lower = jnp.arange(rows_here)[:, None] >= jnp.arange(rows_here)[None, :]
    cumul = jnp.dot(lower.astype(F32), log_decay, precision=HIGHEST)
    last_cum = cumul[-1]
    ends = jnp.exp(last_cum[None, :] - cumul)
    state = jnp.einsum(
        "thd,the->hde",
        keys.astype(F32) * ends[:, :, None],
        values.astype(F32),
        precision=HIGHEST,
    )
    decay = jnp.broadcast_to(jnp.exp(last_cum)[:, None, None], (heads_here, 8, head_size))
    mine = jnp.concatenate([state, decay], axis=1)
    theirs = move(mine, other_core)
    first = jnp.where(c == 0, mine, theirs)
    second = jnp.where(c == 0, theirs, mine)
    first_s, first_d = first[:, :head_size], first[:, head_size : head_size + 1]
    second_s, second_d = second[:, :head_size], second[:, head_size : head_size + 1]
    chip = jnp.concatenate(
        [second_d * first_s + second_s, second[:, head_size:] * first[:, head_size:]], axis=1
    )
    arrived = [(s, move(chip, later_x(s))) for s in (3, 2, 1)]

    queries = jnp.dot(tokens, q_weight, preferred_element_type=F32).astype(BF16).reshape(view)
    scores = jnp.einsum("thd,shd->hts", queries, keys, preferred_element_type=F32)
    diff = jnp.transpose(cumul[:, None, :] - cumul[None, :, :], (2, 0, 1))
    weight = (scores * jnp.exp(jnp.where(lower[None], diff, -1e30))).astype(BF16)
    intra = jnp.einsum("hts,shd->thd", weight, values, preferred_element_type=F32)

    state_in = carried_state
    for s, message in arrived:
        d = jnp.where(x >= s, message[:, head_size : head_size + 1], 1.0)
        state_in = d * state_in + message[:, :head_size]
    state_in = jnp.where(c == 1, first_d * state_in + first_s, state_in)
    inter = jnp.exp(cumul)[:, :, None] * jnp.einsum(
        "thd,hde->the", queries.astype(F32), state_in, precision=HIGHEST
    )
    attended = intra + inter
    normed_heads = attended * lax.rsqrt(
        jnp.mean(attended * attended, axis=-1, keepdims=True) + 1e-06
    )
    flat_heads = normed_heads.astype(BF16).reshape(rows_here, heads_here * head_size)

    inner = flat_heads.shape[1]
    wide = width // 6 if width % 768 == 0 else width
    share = pl.BlockSpec((32, wide), lambda n: (0, n))
    own, *sent = pl.pallas_call(
        project_kernel,
        out_shape=[jax.ShapeDtypeStruct((32, width), F32)]
        + [jax.ShapeDtypeStruct((32, width), BF16)] * 3,
        grid=(width // wide,),
        in_specs=[
            SCALARS,
            pl.BlockSpec((rows_here, inner), lambda n: (0, 0)),
            pl.BlockSpec((inner, wide), lambda n: (0, n)),
        ],
        out_specs=[share] * 4,
        scratch_shapes=[pltpu.VMEM((rows_here, inner), BF16)],
        compiler_params=pltpu.CompilerParams(vmem_limit_bytes=8 * 1024 * 1024),
        cost_estimate=pl.CostEstimate(
            flops=2 * rows_here * inner * width,
            bytes_accessed=2 * width * (inner + rows_here),
            transcendentals=0,
        ),
        name="project",
    )(scalars, flat_heads, out_weight)
    came = [move(part, along_p(s)) for s, part in zip((1, 2, 3), sent)]
    own, *sent = local(
        partial_kernel,
        [on_chip((8, width), F32)] + [on_chip((8, width), BF16)] * 3,
        scalars,
        own,
        *came,
        scratch=[pltpu.VMEM((32, width), F32)],
        bytes_=32 * width * 8,
        mib=8,
        name="partial",
    )
    came = [move(part, along_q(s)) for s, part in zip((1, 2, 3), sent)]
    own_tokens = lax.dynamic_slice_in_dim(tokens, 32 * p + 8 * q, 8, 0).astype(F32)
    final_rows = local(
        norm_kernel,
        on_chip((8, width), BF16),
        scalars,
        own,
        *came,
        own_tokens,
        final_gain.reshape(1, width),
        bytes_=8 * width * 16,
        name="norm",
    )

    on_x = gather(final_rows, along_x, scalars, "stack_x")
    ours = gather(on_x, along_p, scalars, "stack_p")
    theirs = move(ours, other_core)
    ours, theirs = tie(ours, theirs)
    lines = jnp.transpose(targets.reshape(X, CORE, 4, 4, 8), (1, 3, 2, 0, 4)).reshape(8, 128)
    up, down = move(ours, along_q(1)), move(ours, along_q(3))
    half = up.shape[0] // 2
    far = (move(up[:half], along_q(1)), move(down[half:], along_q(3)))
    found = {}
    for s, parts in ((0, (ours,)), (1, (up,)), (3, (down,)), (2, far)):
        if s == 2:
            parts, found = lax.optimization_barrier((parts, found))
        swapped = (theirs,) if s == 0 else tuple(move(part, other_core) for part in parts)
        for mine_too, blocks in ((True, parts), (False, swapped)):
            logits = [jnp.dot(b, vocab_weight, preferred_element_type=F32) for b in blocks]
            found[s, mine_too] = local(
                functools.partial(score_kernel, s, mine_too, len(blocks)),
                on_chip((8, 128), F32),
                scalars,
                lines,
                *logits,
                unread=blocks,
                bytes_=4 * 128 * vocab_local,
                name="score",
            )
    found = [found[k // 2, k % 2 == 0] for k in range(8)]
    stats = local(place_kernel, on_chip((24, 128), F32), scalars, *found, name="place")
    steps = [other_core]
    for axis in (0, 2, 3):
        steps += [near(axis, 0), near(axis, 1)]
    for step in steps[:-1]:
        stats = local(
            merge_kernel, on_chip((24, 128), F32), scalars, stats, move(stats, step), name="merge"
        )
    parts = [stats, move(stats, steps[-1])]
    loglik = local(
        finish_kernel,
        jax.ShapeDtypeStruct((1, 128), F32),
        scalars,
        *parts,
        scratch=[pltpu.VMEM((8, 128), F32)],
        name="finish",
    )
    return loglik.reshape(rows_here)


def solution(mesh):
    fine = Mesh(mesh.devices.reshape(X, CORE, Z, Y), ALL)
    seq, head = (("x", "core"), ("z", "y"))
    return jax.shard_map(
        shards,
        mesh=fine,
        in_specs=(
            P(seq, None),
            P(seq, head),
            P(head, None, None),
            P(None, head),
            P(None, head),
            P(None, head),
            P(head, None),
            P(),
            P(None, ALL),
            P(),
        ),
        out_specs=P(seq),
        check_vma=False,
    )
```

```python
import functools

import jax
import jax.numpy as jnp
from jax import lax
from jax.experimental import pallas as pl
from jax.experimental.pallas import tpu as pltpu
from jax.sharding import Mesh, PartitionSpec as P

X, CORE, Z, Y = 4, 2, 4, 4
ALL = ("x", "core", "z", "y")
F32 = jnp.float32
BF16 = jnp.bfloat16
HIGHEST = lax.Precision.HIGHEST


def move(array, target):
    pairs = []
    for i in range(X * CORE * Z * Y):
        at = (i // (CORE * Z * Y), i // (Z * Y) % CORE, i // Y % Z, i % Y)
        to = target(*at)
        pairs.append((i, ((to[0] * CORE + to[1]) * Z + to[2]) * Y + to[3]))
    return lax.ppermute(array, ALL, pairs)


def other_core(x, c, z, y):
    return (x, 1 - c, z, y)


def near(axis, step):
    def target(*at):
        to = list(at)
        to[axis] = (at[axis] + (1 if at[axis] % 2 == step else 3)) % 4
        return tuple(to)

    return target


def along_x(s):
    return lambda x, c, z, y: ((x + s) % X, c, z, y)


def along_p(s):
    return lambda x, c, z, y: (x, c, z, (y + s) % Y) if c == 0 else (x, c, (z + s) % Z, y)


def along_q(s):
    return lambda x, c, z, y: (x, c, (z + s) % Z, y) if c == 0 else (x, c, z, (y + s) % Y)


def on_chip(shape, dtype):
    return pltpu.VMEM(shape, dtype)


def pin(array):
    return pltpu.with_memory_space_constraint(array, pltpu.VMEM)


ANYWHERE = pl.BlockSpec(memory_space=pl.ANY)
SCALARS = pl.BlockSpec(memory_space=pltpu.SMEM)
WHOLE = pl.BlockSpec(memory_space=pltpu.VMEM)


def local(kernel, outs, scalars, *arrays, loose=(), unread=(), scratch=(), flops=0, bytes_=0, mib=4, name=None):
    many = isinstance(outs, list)
    specs = [WHOLE] * len(outs) if many else WHOLE
    return pl.pallas_call(
        kernel,
        out_shape=outs,
        in_specs=[SCALARS] + [WHOLE] * len((*arrays, *loose)) + [ANYWHERE] * len(unread),
        out_specs=specs,
        scratch_shapes=list(scratch),
        compiler_params=pltpu.CompilerParams(vmem_limit_bytes=mib * 1024 * 1024),
        cost_estimate=pl.CostEstimate(flops=flops, bytes_accessed=bytes_, transcendentals=0),
        name=name,
    )(scalars, *[pin(a) for a in arrays], *loose, *[pin(a) for a in unread])


def tie_kernel(a, b, out_a, out_b):
    pass


def tie(a, b):
    return pl.pallas_call(
        tie_kernel,
        out_shape=[on_chip(a.shape, a.dtype), on_chip(b.shape, b.dtype)],
        in_specs=[ANYWHERE] * 2,
        out_specs=[ANYWHERE] * 2,
        input_output_aliases={0: 0, 1: 1},
        compiler_params=pltpu.CompilerParams(vmem_limit_bytes=1024 * 1024),
        name="tie",
    )(pin(a), pin(b))


def project_kernel(at, heads, weight, own, one, two, three, rolled):
    @pl.when(pl.program_id(0) == 0)
    def _():
        for s in range(4):
            start = pl.multiple_of((at[4] + s) % 4 * 32, 32)
            rolled[pl.ds(32 * s, 32), :] = heads[pl.ds(start, 32), :]

    out = jnp.dot(rolled[...], weight[...], preferred_element_type=F32)
    own[...] = out[:32]
    one[...] = out[32:64].astype(BF16)
    two[...] = out[64:96].astype(BF16)
    three[...] = out[96:].astype(BF16)


def partial_kernel(at, one, two, three, own, mine, first, second, third, total):
    q = at[5]
    total[...] = (
        own[...]
        + one[...].astype(F32)
        + two[...].astype(F32)
        + three[...].astype(F32)
    )
    for s, out in enumerate((mine, first, second, third)):
        start = pl.multiple_of((q + s) % 4 * 8, 8)
        out[...] = total[pl.ds(start, 8), :].astype(out.dtype)


def norm_kernel(at, own, one, two, three, tokens, gain, out):
    resid = (
        tokens[...]
        + own[...]
        + one[...].astype(F32)
        + two[...].astype(F32)
        + three[...].astype(F32)
    )
    scale = lax.rsqrt(jnp.mean(resid * resid, axis=1, keepdims=True) + 1e-06)
    out[...] = (resid * scale * gain[...].astype(F32)).astype(BF16)


def stack_kernel(at, a, b, c, d, out):
    rows = a.shape[0]
    out[0 : 2 * rows, :] = jnp.concatenate([a[...], b[...]], axis=0)
    out[2 * rows : 4 * rows, :] = jnp.concatenate([c[...], d[...]], axis=0)


def gather(block, target, scalars, name):
    parts = [move(block, target(s)) for s in (3, 2, 1)]
    rows, width = block.shape
    return local(
        stack_kernel,
        on_chip((4 * rows, width), block.dtype),
        scalars,
        block,
        *parts,
        bytes_=16 * rows * width,
        mib=8,
        name=name,
    )


def in_place(values, lane, p, x):
    values = pltpu.roll(values, 32 * p, 1)
    return jnp.where(
        (lane & 31) >= 8 * x,
        pltpu.roll(values, 8 * x, 1),
        pltpu.roll(values, (8 * x + 96) % 128, 1),
    )


def as_gathered(values, lane, p, x):
    values = pltpu.roll(values, (128 - 32 * p) % 128, 1)
    return jnp.where(
        (lane & 31) < 32 - 8 * x,
        pltpu.roll(values, (128 - 8 * x) % 128, 1),
        pltpu.roll(values, (160 - 8 * x) % 128, 1),
    )


def score_kernel(shift, at, targets, mine, theirs, rows_mine, rows_theirs, out_mine, out_theirs):
    x = at[0]
    lane = lax.broadcasted_iota(jnp.int32, (8, 128), 1)
    i = lax.broadcasted_iota(jnp.int32, (128, 128), 0)
    j = lax.broadcasted_iota(jnp.int32, (128, 128), 1)
    for logits, out, p, q, core in (
        (mine, out_mine, at[4], at[5], at[1]),
        (theirs, out_theirs, at[5], at[4], 1 - at[1]),
    ):
        found = logits[...]
        place = core * 4 + ((q + 4 - shift) & 3)
        line = jnp.broadcast_to(targets[pl.ds(place, 1), :] - at[6], (8, 128))
        line = as_gathered(line, lane, p, x)[:1]
        want = jnp.sum(jnp.where(i == j, line, 0), axis=1, keepdims=True)
        top = jnp.max(found, axis=1, keepdims=True)
        total = jnp.sum(jnp.exp(found - top), axis=1, keepdims=True)
        column = lax.broadcasted_iota(jnp.int32, found.shape, 1)
        hit = jnp.sum(jnp.where(column == want, found, 0.0), axis=1, keepdims=True)
        both = jnp.where(j == 0, top, jnp.where(j == 1, total, jnp.where(j == 2, hit, 0.0)))
        out[...] = in_place(jnp.transpose(both)[:8], lane, p, x)


def place_kernel(at, *refs):
    blocks, out, held = refs[:-2], refs[-2], refs[-1]
    for k, block in enumerate(blocks):
        shift, own = k // 2, k % 2 == 0
        q, core = (at[5], at[1]) if own else (at[4], 1 - at[1])
        place = core * 4 + ((q + 4 - shift) & 3)
        for row in range(3):
            held[pl.ds(8 * row + place, 1), :] = block[row : row + 1, :]
    lane = lax.broadcasted_iota(jnp.int32, (8, 128), 1)
    for row in range(3):
        values = held[8 * row : 8 * row + 8, :]
        turned = {8 * k: pltpu.roll(values, 8 * k, 1) if k else values for k in range(16)}
        for x in range(X):
            picked = [
                jnp.where((lane // 8 & 3) == q, turned[(8 * q - 8 * x) % 128], 0.0) for q in range(4)
            ]
            for core in range(CORE):
                line = sum(picked[q][4 * core + q : 4 * core + q + 1, :] for q in range(4))
                out[x * CORE + core, row : row + 1, :] = line


def merged(parts):
    top = parts[0][0:1]
    for part in parts[1:]:
        top = jnp.maximum(top, part[0:1])
    total = sum(part[1:2] * jnp.exp(part[0:1] - top) for part in parts)
    hit = sum(part[2:3] for part in parts)
    return top, total, hit


def block_kernel(at, found, out):
    parts = [found[k] for k in range(X * CORE)]
    out[0:1, :], out[1:2, :], out[2:3, :] = merged(parts)


def merge_kernel(at, here, there, out):
    out[0:1, :], out[1:2, :], out[2:3, :] = merged([here[...], there[...]])


def finish_kernel(at, here, there, out):
    top, total, hit = merged([here[...], there[...]])
    out[...] = hit - top - jnp.log(total)


def shards(
    tokens,
    log_decay,
    carried_state,
    q_weight,
    k_weight,
    v_weight,
    out_weight,
    final_gain,
    vocab_weight,
    targets,
):
    x, c, z, y = (lax.axis_index(a) for a in ALL)
    p, q = jnp.where(c == 0, y, z), jnp.where(c == 0, z, y)
    rows_here, width = tokens.shape
    heads_here = carried_state.shape[0]
    head_size = carried_state.shape[1]
    view = (rows_here, heads_here, head_size)
    vocab_local = vocab_weight.shape[1]
    offset = (((x * CORE + c) * Z + z) * Y + y) * vocab_local
    scalars = jnp.stack([x, c, z, y, p, q, offset, offset]).astype(jnp.int32)

    keys = jnp.dot(tokens, k_weight, preferred_element_type=F32).astype(BF16).reshape(view)
    values = jnp.dot(tokens, v_weight, preferred_element_type=F32).astype(BF16).reshape(view)
    lower = jnp.arange(rows_here)[:, None] >= jnp.arange(rows_here)[None, :]
    cumul = jnp.dot(lower.astype(F32), log_decay, precision=HIGHEST)
    last_cum = cumul[-1]
    ends = jnp.exp(last_cum[None, :] - cumul)
    state = jnp.einsum(
        "thd,the->hde",
        keys.astype(F32) * ends[:, :, None],
        values.astype(F32),
        precision=HIGHEST,
    )
    decay = jnp.broadcast_to(jnp.exp(last_cum)[:, None, None], (heads_here, 8, head_size))
    mine = jnp.concatenate([state, decay], axis=1)
    theirs = move(mine, other_core)
    first = jnp.where(c == 0, mine, theirs)
    second = jnp.where(c == 0, theirs, mine)
    first_s, first_d = first[:, :head_size], first[:, head_size : head_size + 1]
    second_s = second[:, :head_size]
    second_d = second[:, head_size:]
    both_d = second_d * first[:, head_size:]
    coarse = both_d.astype(BF16)
    chip = jnp.concatenate(
        [
            (second_d[:, :1] * first_s + second_s).astype(BF16),
            coarse,
            (both_d - coarse.astype(F32)).astype(BF16),
        ],
        axis=1,
    )
    arrived = [(s, move(chip, along_x(s))) for s in (3, 2, 1)]

    queries = jnp.dot(tokens, q_weight, preferred_element_type=F32).astype(BF16).reshape(view)
    scores = jnp.einsum("thd,shd->hts", queries, keys, preferred_element_type=F32)
    diff = jnp.transpose(cumul[:, None, :] - cumul[None, :, :], (2, 0, 1))
    weight = (scores * jnp.exp(jnp.where(lower[None], diff, -1e30))).astype(BF16)
    intra = jnp.einsum("hts,shd->thd", weight, values, preferred_element_type=F32)

    state_in = carried_state
    for s, message in arrived:
        message = message.astype(F32)
        d = message[:, head_size : head_size + 1] + message[:, head_size + 8 : head_size + 9]
        later = d * state_in + message[:, :head_size]
        state_in = jnp.where(x >= s, later, state_in)
    state_in = jnp.where(c == 1, first_d * state_in + first_s, state_in)
    inter = jnp.exp(cumul)[:, :, None] * jnp.einsum(
        "thd,hde->the", queries.astype(F32), state_in, precision=HIGHEST
    )
    attended = intra + inter
    normed_heads = attended * lax.rsqrt(
        jnp.mean(attended * attended, axis=-1, keepdims=True) + 1e-06
    )
    flat_heads = normed_heads.astype(BF16).reshape(rows_here, heads_here * head_size)

    inner = flat_heads.shape[1]
    wide = width // 6 if width % 768 == 0 else width
    share = pl.BlockSpec((32, wide), lambda n: (0, n))
    own, *sent = pl.pallas_call(
        project_kernel,
        out_shape=[jax.ShapeDtypeStruct((32, width), F32)]
        + [jax.ShapeDtypeStruct((32, width), BF16)] * 3,
        grid=(width // wide,),
        in_specs=[
            SCALARS,
            pl.BlockSpec((rows_here, inner), lambda n: (0, 0)),
            pl.BlockSpec((inner, wide), lambda n: (0, n)),
        ],
        out_specs=[share] * 4,
        scratch_shapes=[pltpu.VMEM((rows_here, inner), BF16)],
        compiler_params=pltpu.CompilerParams(vmem_limit_bytes=8 * 1024 * 1024),
        cost_estimate=pl.CostEstimate(
            flops=2 * rows_here * inner * width,
            bytes_accessed=2 * width * (inner + rows_here),
            transcendentals=0,
        ),
        name="project",
    )(scalars, flat_heads, out_weight)
    came = [move(part, along_p(s)) for s, part in zip((1, 2, 3), sent)]
    own, *sent = local(
        partial_kernel,
        [on_chip((8, width), F32)] + [on_chip((8, width), BF16)] * 3,
        scalars,
        *came,
        loose=(own,),
        scratch=[pltpu.VMEM((32, width), F32)],
        bytes_=32 * width * 8,
        mib=8,
        name="partial",
    )
    came = [move(part, along_q(s)) for s, part in zip((1, 2, 3), sent)]
    own_tokens = lax.dynamic_slice_in_dim(tokens, 32 * p + 8 * q, 8, 0).astype(F32)
    final_rows = local(
        norm_kernel,
        on_chip((8, width), BF16),
        scalars,
        own,
        *came,
        own_tokens,
        final_gain.reshape(1, width),
        bytes_=8 * width * 16,
        name="norm",
    )

    on_x = gather(final_rows, along_x, scalars, "stack_x")
    ours = gather(on_x, along_p, scalars, "stack_p")
    theirs = move(ours, other_core)
    ours, theirs = tie(ours, theirs)
    lines = jnp.transpose(targets.reshape(X, CORE, 4, 4, 8), (1, 3, 2, 0, 4)).reshape(8, 128)
    up, down = move(ours, along_q(1)), move(ours, along_q(3))
    half = up.shape[0] // 2
    far = (move(up[:half], along_q(1)), move(down[half:], along_q(3)))
    found = {}
    for s, block in ((0, ours), (1, up), (3, down), (2, far)):
        if s == 0:
            swapped = theirs
        elif s == 2:
            block, found = lax.optimization_barrier((block, found))
            swapped = jnp.concatenate([move(part, other_core) for part in block], axis=0)
            block = jnp.concatenate(block, axis=0)
        else:
            swapped = move(block, other_core)
        logits = [jnp.dot(b, vocab_weight, preferred_element_type=F32) for b in (block, swapped)]
        found[s] = local(
            functools.partial(score_kernel, s),
            [on_chip((8, 128), F32)] * 2,
            scalars,
            lines,
            *logits,
            unread=(block, swapped),
            bytes_=8 * 128 * vocab_local,
            name="score",
        )
    sent = local(
        place_kernel,
        on_chip((X * CORE, 8, 128), F32),
        scalars,
        *[found[s][k] for s in range(4) for k in range(2)],
        scratch=[pltpu.VMEM((24, 128), F32)],
        name="place",
    )
    came = lax.all_to_all(sent, ("x", "core"), 0, 0)
    stats = local(block_kernel, on_chip((8, 128), F32), scalars, came, name="block")
    steps = [near(axis, step) for axis in (2, 3) for step in (0, 1)]
    for step in steps[:-1]:
        stats = local(
            merge_kernel, on_chip((8, 128), F32), scalars, stats, move(stats, step), name="merge"
        )
    loglik = local(
        finish_kernel,
        jax.ShapeDtypeStruct((1, 128), F32),
        scalars,
        stats,
        move(stats, steps[-1]),
        name="finish",
    )
    return loglik.reshape(rows_here)


def solution(mesh):
    fine = Mesh(mesh.devices.reshape(X, CORE, Z, Y), ALL)
    seq, head = (("x", "core"), ("z", "y"))
    return jax.shard_map(
        shards,
        mesh=fine,
        in_specs=(
            P(seq, None),
            P(seq, head),
            P(head, None, None),
            P(None, head),
            P(None, head),
            P(None, head),
            P(head, None),
            P(),
            P(None, ALL),
            P(),
        ),
        out_specs=P(seq),
        check_vma=False,
    )
```

```python
import functools

import jax
import jax.numpy as jnp
from jax import lax
from jax.experimental import pallas as pl
from jax.experimental.pallas import tpu as pltpu
from jax.sharding import Mesh, PartitionSpec as P

X, CORE, Z, Y = 4, 2, 4, 4
ALL = ("x", "core", "z", "y")
F32 = jnp.float32
BF16 = jnp.bfloat16
HIGHEST = lax.Precision.HIGHEST


def move(array, target):
    pairs = []
    for i in range(X * CORE * Z * Y):
        at = (i // (CORE * Z * Y), i // (Z * Y) % CORE, i // Y % Z, i % Y)
        to = target(*at)
        pairs.append((i, ((to[0] * CORE + to[1]) * Z + to[2]) * Y + to[3]))
    return lax.ppermute(array, ALL, pairs)


def other_core(x, c, z, y):
    return (x, 1 - c, z, y)


def along_x(s):
    return lambda x, c, z, y: ((x + s) % X, c, z, y)


def along_p(s):
    return lambda x, c, z, y: (x, c, z, (y + s) % Y) if c == 0 else (x, c, (z + s) % Z, y)


def along_q(s):
    return lambda x, c, z, y: (x, c, (z + s) % Z, y) if c == 0 else (x, c, z, (y + s) % Y)


def on_chip(shape, dtype):
    return pltpu.VMEM(shape, dtype)


def in_hbm(shape, dtype):
    return pltpu.HBM(shape, dtype)


def leave(array):
    return pltpu.with_memory_space_constraint(array, pltpu.HBM)


def pin(array):
    return pltpu.with_memory_space_constraint(array, pltpu.VMEM)


ANYWHERE = pl.BlockSpec(memory_space=pl.ANY)
SCALARS = pl.BlockSpec(memory_space=pltpu.SMEM)
WHOLE = pl.BlockSpec(memory_space=pltpu.VMEM)


def local(kernel, outs, scalars, *arrays, loose=(), unread=(), scratch=(), flops=0, bytes_=0, mib=4, name=None):
    many = isinstance(outs, list)
    specs = [WHOLE] * len(outs) if many else WHOLE
    return pl.pallas_call(
        kernel,
        out_shape=outs,
        in_specs=[SCALARS] + [WHOLE] * len((*arrays, *loose)) + [ANYWHERE] * len(unread),
        out_specs=specs,
        scratch_shapes=list(scratch),
        compiler_params=pltpu.CompilerParams(vmem_limit_bytes=mib * 1024 * 1024),
        cost_estimate=pl.CostEstimate(flops=flops, bytes_accessed=bytes_, transcendentals=0),
        name=name,
    )(scalars, *[pin(a) for a in arrays], *[leave(a) for a in loose], *[pin(a) for a in unread])


def tie_kernel(a, b, out_a, out_b):
    pass


def tie(a, b):
    return pl.pallas_call(
        tie_kernel,
        out_shape=[on_chip(a.shape, a.dtype), on_chip(b.shape, b.dtype)],
        in_specs=[ANYWHERE] * 2,
        out_specs=[ANYWHERE] * 2,
        input_output_aliases={0: 0, 1: 1},
        compiler_params=pltpu.CompilerParams(vmem_limit_bytes=1024 * 1024),
        name="tie",
    )(pin(a), pin(b))


def combine_kernel(at, mine, theirs, chip):
    size = mine.shape[2]
    low = at[1] == 0
    for h in range(mine.shape[0]):
        first = jnp.where(low, mine[h], theirs[h])
        second = jnp.where(low, theirs[h], mine[h])
        decay = jnp.broadcast_to((second[size:] * first[size:])[:1], (16, size))
        coarse = decay.astype(BF16).astype(F32)
        row = lax.broadcasted_iota(jnp.int32, (16, size), 0)
        chip[h, :size, :] = (second[size : size + 1] * first[:size] + second[:size]).astype(BF16)
        chip[h, size:, :] = jnp.where(row < 8, coarse, decay - coarse).astype(BF16)


def state_kernel(at, carried, three, two, one, theirs, out):
    size = carried.shape[2]
    for h in range(carried.shape[0]):
        state = carried[h]
        for s, message in ((3, three), (2, two), (1, one)):
            part = message[h].astype(F32)
            decay = part[size : size + 1] + part[size + 8 : size + 9]
            state = jnp.where(at[0] >= s, decay * state + part[:size], state)
        part = theirs[h]
        out[h] = jnp.where(at[1] == 1, part[size : size + 1] * state + part[:size], state)


def project_kernel(at, heads, weight, own, one, two, three, rolled):
    @pl.when(pl.program_id(0) == 0)
    def _():
        for s in range(4):
            start = pl.multiple_of((at[4] + s) % 4 * 32, 32)
            rolled[pl.ds(32 * s, 32), :] = heads[pl.ds(start, 32), :]

    out = jnp.dot(rolled[...], weight[...], preferred_element_type=F32)
    own[...] = out[:32]
    one[...] = out[32:64].astype(BF16)
    two[...] = out[64:96].astype(BF16)
    three[...] = out[96:].astype(BF16)


def partial_kernel(at, one, two, three, own, mine, first, second, third, total):
    q = at[5]
    total[...] = (
        own[...]
        + one[...].astype(F32)
        + two[...].astype(F32)
        + three[...].astype(F32)
    )
    for s, out in enumerate((mine, first, second, third)):
        start = pl.multiple_of((q + s) % 4 * 8, 8)
        out[...] = total[pl.ds(start, 8), :].astype(out.dtype)


def norm_kernel(at, own, one, two, three, tokens, gain, out):
    resid = (
        tokens[...]
        + own[...]
        + one[...].astype(F32)
        + two[...].astype(F32)
        + three[...].astype(F32)
    )
    scale = lax.rsqrt(jnp.mean(resid * resid, axis=1, keepdims=True) + 1e-06)
    out[...] = (resid * scale * gain[...].astype(F32)).astype(BF16)


def stack_kernel(at, a, b, c, d, out):
    rows = a.shape[0]
    out[0 : 2 * rows, :] = jnp.concatenate([a[...], b[...]], axis=0)
    out[2 * rows : 4 * rows, :] = jnp.concatenate([c[...], d[...]], axis=0)


def gather(block, target, scalars, name):
    parts = [move(block, target(s)) for s in (3, 2, 1)]
    rows, width = block.shape
    return local(
        stack_kernel,
        on_chip((4 * rows, width), block.dtype),
        scalars,
        block,
        *parts,
        bytes_=16 * rows * width,
        mib=8,
        name=name,
    )


def in_place(values, lane, p, x):
    values = pltpu.roll(values, 32 * p, 1)
    return jnp.where(
        (lane & 31) >= 8 * x,
        pltpu.roll(values, 8 * x, 1),
        pltpu.roll(values, (8 * x + 96) % 128, 1),
    )


def as_gathered(values, lane, p, x):
    values = pltpu.roll(values, (128 - 32 * p) % 128, 1)
    return jnp.where(
        (lane & 31) < 32 - 8 * x,
        pltpu.roll(values, (128 - 8 * x) % 128, 1),
        pltpu.roll(values, (160 - 8 * x) % 128, 1),
    )


def score_kernel(shift, at, targets, mine, theirs, rows_mine, rows_theirs, out_mine, out_theirs):
    x = at[0]
    lane = lax.broadcasted_iota(jnp.int32, (8, 128), 1)
    i = lax.broadcasted_iota(jnp.int32, (128, 128), 0)
    j = lax.broadcasted_iota(jnp.int32, (128, 128), 1)
    for logits, out, p, q, core in (
        (mine, out_mine, at[4], at[5], at[1]),
        (theirs, out_theirs, at[5], at[4], 1 - at[1]),
    ):
        found = logits[...]
        place = core * 4 + ((q + 4 - shift) & 3)
        line = jnp.broadcast_to(targets[pl.ds(place, 1), :] - at[6], (8, 128))
        line = as_gathered(line, lane, p, x)[:1]
        want = jnp.sum(jnp.where(i == j, line, 0), axis=1, keepdims=True)
        top = jnp.max(found, axis=1, keepdims=True)
        total = jnp.sum(jnp.exp(found - top), axis=1, keepdims=True)
        column = lax.broadcasted_iota(jnp.int32, found.shape, 1)
        hit = jnp.sum(jnp.where(column == want, found, 0.0), axis=1, keepdims=True)
        both = jnp.where(j == 0, top, jnp.where(j == 1, total, jnp.where(j == 2, hit, 0.0)))
        out[...] = in_place(jnp.transpose(both)[:8], lane, p, x)


def place_kernel(at, *refs):
    blocks, out, held = refs[:-2], refs[-2], refs[-1]
    for k, block in enumerate(blocks):
        shift, own = k // 2, k % 2 == 0
        q, core = (at[5], at[1]) if own else (at[4], 1 - at[1])
        place = core * 4 + ((q + 4 - shift) & 3)
        for row in range(3):
            held[pl.ds(8 * row + place, 1), :] = block[row : row + 1, :]
    lane = lax.broadcasted_iota(jnp.int32, (8, 128), 1)
    for row in range(3):
        values = held[8 * row : 8 * row + 8, :]
        turned = {8 * k: pltpu.roll(values, 8 * k, 1) if k else values for k in range(16)}
        for x in range(X):
            picked = [
                jnp.where((lane // 8 & 3) == q, turned[(8 * q - 8 * x) % 128], 0.0) for q in range(4)
            ]
            for core in range(CORE):
                line = sum(picked[q][4 * core + q : 4 * core + q + 1, :] for q in range(4))
                out[x * CORE + core, row : row + 1, :] = line


def merged(parts):
    top = parts[0][0:1]
    for part in parts[1:]:
        top = jnp.maximum(top, part[0:1])
    total = sum(part[1:2] * jnp.exp(part[0:1] - top) for part in parts)
    hit = sum(part[2:3] for part in parts)
    return top, total, hit


def block_kernel(at, found, out):
    top, total, hit = merged([found[k] for k in range(X * CORE)])
    for k in range(Z * Y):
        out[k, 0:1, :], out[k, 1:2, :], out[k, 2:3, :] = top, total, hit


def finish_kernel(at, found, out):
    top, total, hit = merged([found[k] for k in range(Z * Y)])
    out[...] = hit - top - jnp.log(total)


def shards(
    tokens,
    log_decay,
    carried_state,
    q_weight,
    k_weight,
    v_weight,
    out_weight,
    final_gain,
    vocab_weight,
    targets,
):
    x, c, z, y = (lax.axis_index(a) for a in ALL)
    p, q = jnp.where(c == 0, y, z), jnp.where(c == 0, z, y)
    rows_here, width = tokens.shape
    heads_here = carried_state.shape[0]
    head_size = carried_state.shape[1]
    view = (rows_here, heads_here, head_size)
    vocab_local = vocab_weight.shape[1]
    offset = (((x * CORE + c) * Z + z) * Y + y) * vocab_local
    scalars = jnp.stack([x, c, z, y, p, q, offset, offset]).astype(jnp.int32)

    keys = jnp.dot(tokens, k_weight, preferred_element_type=F32).astype(BF16).reshape(view)
    values = jnp.dot(tokens, v_weight, preferred_element_type=F32).astype(BF16).reshape(view)
    lower = jnp.arange(rows_here)[:, None] >= jnp.arange(rows_here)[None, :]
    cumul = jnp.dot(lower.astype(F32), log_decay, precision=HIGHEST)
    last_cum = cumul[-1]
    ends = jnp.exp(last_cum[None, :] - cumul)
    state = jnp.einsum(
        "thd,the->hde",
        keys.astype(F32) * ends[:, :, None],
        values.astype(F32),
        precision=HIGHEST,
    )
    decay = jnp.broadcast_to(jnp.exp(last_cum)[:, None, None], (heads_here, 8, head_size))
    mine = jnp.concatenate([state, decay], axis=1)
    theirs = move(mine, other_core)
    chip = local(
        combine_kernel,
        on_chip((heads_here, head_size + 16, head_size), BF16),
        scalars,
        mine,
        theirs,
        name="combine",
    )
    tokens_then, chip = lax.optimization_barrier((tokens, chip))
    arrived = [(s, move(chip, along_x(s))) for s in (3, 2, 1)]

    queries = jnp.dot(tokens_then, q_weight, preferred_element_type=F32).astype(BF16).reshape(view)
    scores = jnp.einsum("thd,shd->hts", queries, keys, preferred_element_type=F32)
    diff = jnp.transpose(cumul[:, None, :] - cumul[None, :, :], (2, 0, 1))
    weight = (scores * jnp.exp(jnp.where(lower[None], diff, -1e30))).astype(BF16)
    intra = jnp.einsum("hts,shd->thd", weight, values, preferred_element_type=F32)

    state_in = local(
        state_kernel,
        on_chip(carried_state.shape, F32),
        scalars,
        carried_state,
        *[message for _, message in arrived],
        theirs,
        name="state",
    )
    inter = jnp.exp(cumul)[:, :, None] * jnp.einsum(
        "thd,hde->the", queries.astype(F32), state_in, precision=HIGHEST
    )
    attended = intra + inter
    normed_heads = attended * lax.rsqrt(
        jnp.mean(attended * attended, axis=-1, keepdims=True) + 1e-06
    )
    flat_heads = normed_heads.astype(BF16).reshape(rows_here, heads_here * head_size)

    inner = flat_heads.shape[1]
    wide = width // 3 if width % 384 == 0 else width
    share = pl.BlockSpec((32, wide), lambda n: (0, n))
    own, *sent = pl.pallas_call(
        project_kernel,
        out_shape=[in_hbm((32, width), F32)] + [in_hbm((32, width), BF16)] * 3,
        grid=(width // wide,),
        in_specs=[
            SCALARS,
            pl.BlockSpec((rows_here, inner), lambda n: (0, 0)),
            pl.BlockSpec((inner, wide), lambda n: (0, n)),
        ],
        out_specs=[share] * 4,
        scratch_shapes=[pltpu.VMEM((rows_here, inner), BF16)],
        compiler_params=pltpu.CompilerParams(vmem_limit_bytes=12 * 1024 * 1024),
        cost_estimate=pl.CostEstimate(
            flops=2 * rows_here * inner * width,
            bytes_accessed=2 * width * (inner + rows_here),
            transcendentals=0,
        ),
        name="project",
    )(scalars, flat_heads, leave(out_weight))
    came = [move(part, along_p(s)) for s, part in zip((1, 2, 3), sent)]
    own, *sent = local(
        partial_kernel,
        [on_chip((8, width), F32)] + [on_chip((8, width), BF16)] * 3,
        scalars,
        *came,
        loose=(own,),
        scratch=[pltpu.VMEM((32, width), F32)],
        bytes_=32 * width * 8,
        mib=8,
        name="partial",
    )
    came = [move(part, along_q(s)) for s, part in zip((1, 2, 3), sent)]
    own_tokens = lax.dynamic_slice_in_dim(tokens, 32 * p + 8 * q, 8, 0).astype(F32)
    final_rows = local(
        norm_kernel,
        on_chip((8, width), BF16),
        scalars,
        own,
        *came,
        own_tokens,
        final_gain.reshape(1, width),
        bytes_=8 * width * 16,
        name="norm",
    )

    on_x = gather(final_rows, along_x, scalars, "stack_x")
    ours = gather(on_x, along_p, scalars, "stack_p")
    theirs = move(ours, other_core)
    ours, theirs = tie(ours, theirs)
    lines = jnp.transpose(targets.reshape(X, CORE, 4, 4, 8), (1, 3, 2, 0, 4)).reshape(8, 128)
    up, down = move(ours, along_q(1)), move(ours, along_q(3))
    half = up.shape[0] // 2
    far = (move(up[:half], along_q(1)), move(down[half:], along_q(3)))
    found = {}
    for s, block in ((0, ours), (1, up), (3, down), (2, far)):
        if s == 0:
            swapped = theirs
        elif s == 2:
            block, found = lax.optimization_barrier((block, found))
            swapped = jnp.concatenate([move(part, other_core) for part in block], axis=0)
            block = jnp.concatenate(block, axis=0)
        else:
            swapped = move(block, other_core)
        logits = [jnp.dot(b, vocab_weight, preferred_element_type=F32) for b in (block, swapped)]
        found[s] = local(
            functools.partial(score_kernel, s),
            [on_chip((8, 128), F32)] * 2,
            scalars,
            lines,
            *logits,
            unread=(block, swapped),
            bytes_=8 * 128 * vocab_local,
            name="score",
        )
    sent = local(
        place_kernel,
        on_chip((X * CORE, 8, 128), F32),
        scalars,
        *[found[s][k] for s in range(4) for k in range(2)],
        scratch=[pltpu.VMEM((24, 128), F32)],
        name="place",
    )
    came = lax.all_to_all(sent, ("x", "core"), 0, 0)
    sent = local(block_kernel, on_chip((Z * Y, 8, 128), F32), scalars, came, name="block")
    came = lax.all_to_all(sent, ("z", "y"), 0, 0)
    loglik = local(
        finish_kernel, jax.ShapeDtypeStruct((1, 128), F32), scalars, came, name="finish"
    )
    return loglik.reshape(rows_here)


def solution(mesh):
    fine = Mesh(mesh.devices.reshape(X, CORE, Z, Y), ALL)
    seq, head = (("x", "core"), ("z", "y"))
    return jax.shard_map(
        shards,
        mesh=fine,
        in_specs=(
            P(seq, None),
            P(seq, head),
            P(head, None, None),
            P(None, head),
            P(None, head),
            P(None, head),
            P(head, None),
            P(),
            P(None, ALL),
            P(),
        ),
        out_specs=P(seq),
        check_vma=False,
    )
```

```python
import functools

import jax
import jax.numpy as jnp
from jax import lax
from jax.experimental import pallas as pl
from jax.experimental.pallas import tpu as pltpu
from jax.sharding import Mesh, PartitionSpec as P

X, CORE, Z, Y = 4, 2, 4, 4
ALL = ("x", "core", "z", "y")
F32 = jnp.float32
BF16 = jnp.bfloat16
HIGHEST = lax.Precision.HIGHEST


def move(array, target):
    pairs = []
    for i in range(X * CORE * Z * Y):
        at = (i // (CORE * Z * Y), i // (Z * Y) % CORE, i // Y % Z, i % Y)
        to = target(*at)
        pairs.append((i, ((to[0] * CORE + to[1]) * Z + to[2]) * Y + to[3]))
    return lax.ppermute(array, ALL, pairs)


def other_core(x, c, z, y):
    return (x, 1 - c, z, y)


def along_x(s):
    return lambda x, c, z, y: ((x + s) % X, c, z, y)


def along_p(s):
    return lambda x, c, z, y: (x, c, z, (y + s) % Y) if c == 0 else (x, c, (z + s) % Z, y)


def along_q(s):
    return lambda x, c, z, y: (x, c, (z + s) % Z, y) if c == 0 else (x, c, z, (y + s) % Y)


def on_chip(shape, dtype):
    return pltpu.VMEM(shape, dtype)


def in_hbm(shape, dtype):
    return pltpu.HBM(shape, dtype)


def leave(array):
    return pltpu.with_memory_space_constraint(array, pltpu.HBM)


def pin(array):
    return pltpu.with_memory_space_constraint(array, pltpu.VMEM)


ANYWHERE = pl.BlockSpec(memory_space=pl.ANY)
SCALARS = pl.BlockSpec(memory_space=pltpu.SMEM)
WHOLE = pl.BlockSpec(memory_space=pltpu.VMEM)


def local(kernel, outs, scalars, *arrays, loose=(), unread=(), scratch=(), flops=0, bytes_=0, mib=4, name=None):
    many = isinstance(outs, list)
    specs = [WHOLE] * len(outs) if many else WHOLE
    return pl.pallas_call(
        kernel,
        out_shape=outs,
        in_specs=[SCALARS] + [WHOLE] * len((*arrays, *loose)) + [ANYWHERE] * len(unread),
        out_specs=specs,
        scratch_shapes=list(scratch),
        compiler_params=pltpu.CompilerParams(vmem_limit_bytes=mib * 1024 * 1024),
        cost_estimate=pl.CostEstimate(flops=flops, bytes_accessed=bytes_, transcendentals=0),
        name=name,
    )(scalars, *[pin(a) for a in arrays], *[leave(a) for a in loose], *[pin(a) for a in unread])


def load_kernel(source, out, done):
    copy = pltpu.make_async_copy(source, out, done)
    copy.start()
    copy.wait()


def combine_kernel(at, mine, theirs, chip):
    size = mine.shape[2]
    low = at[1] == 0
    for h in range(mine.shape[0]):
        first = jnp.where(low, mine[h], theirs[h])
        second = jnp.where(low, theirs[h], mine[h])
        decay = jnp.broadcast_to((second[size:] * first[size:])[:1], (16, size))
        coarse = decay.astype(BF16).astype(F32)
        row = lax.broadcasted_iota(jnp.int32, (16, size), 0)
        chip[h, :size, :] = (second[size : size + 1] * first[:size] + second[:size]).astype(BF16)
        chip[h, size:, :] = jnp.where(row < 8, coarse, decay - coarse).astype(BF16)


def state_kernel(at, carried, three, two, one, theirs, out):
    size = carried.shape[2]
    for h in range(carried.shape[0]):
        state = carried[h]
        for s, message in ((3, three), (2, two), (1, one)):
            part = message[h].astype(F32)
            decay = part[size : size + 1] + part[size + 8 : size + 9]
            state = jnp.where(at[0] >= s, decay * state + part[:size], state)
        part = theirs[h]
        out[h] = jnp.where(at[1] == 1, part[size : size + 1] * state + part[:size], state)


def project_kernel(at, heads, weight, own, one, two, three, rolled):
    @pl.when(pl.program_id(0) == 0)
    def _():
        for s in range(4):
            start = pl.multiple_of((at[4] + s) % 4 * 32, 32)
            rolled[pl.ds(32 * s, 32), :] = heads[pl.ds(start, 32), :]

    out = jnp.dot(rolled[...], weight[...], preferred_element_type=F32)
    own[...] = out[:32]
    one[...] = out[32:64].astype(BF16)
    two[...] = out[64:96].astype(BF16)
    three[...] = out[96:].astype(BF16)


def partial_kernel(at, one, two, three, own, mine, first, second, third, total):
    q = at[5]
    total[...] = (
        own[...]
        + one[...].astype(F32)
        + two[...].astype(F32)
        + three[...].astype(F32)
    )
    for s, out in enumerate((mine, first, second, third)):
        start = pl.multiple_of((q + s) % 4 * 8, 8)
        out[...] = total[pl.ds(start, 8), :].astype(out.dtype)


def norm_kernel(at, own, one, two, three, tokens, gain, out):
    resid = (
        tokens[...]
        + own[...]
        + one[...].astype(F32)
        + two[...].astype(F32)
        + three[...].astype(F32)
    )
    scale = lax.rsqrt(jnp.mean(resid * resid, axis=1, keepdims=True) + 1e-06)
    out[...] = (resid * scale * gain[...].astype(F32)).astype(BF16)


def stack_kernel(at, a, b, c, d, out):
    rows = a.shape[0]
    out[0 : 2 * rows, :] = jnp.concatenate([a[...], b[...]], axis=0)
    out[2 * rows : 4 * rows, :] = jnp.concatenate([c[...], d[...]], axis=0)


def gather(block, target, scalars, name):
    parts = [move(block, target(s)) for s in (3, 2, 1)]
    rows, width = block.shape
    return local(
        stack_kernel,
        on_chip((4 * rows, width), block.dtype),
        scalars,
        block,
        *parts,
        bytes_=16 * rows * width,
        mib=8,
        name=name,
    )


def in_place(values, lane, p, x):
    values = pltpu.roll(values, 32 * p, 1)
    return jnp.where(
        (lane & 31) >= 8 * x,
        pltpu.roll(values, 8 * x, 1),
        pltpu.roll(values, (8 * x + 96) % 128, 1),
    )


def as_gathered(values, lane, p, x):
    values = pltpu.roll(values, (128 - 32 * p) % 128, 1)
    return jnp.where(
        (lane & 31) < 32 - 8 * x,
        pltpu.roll(values, (128 - 8 * x) % 128, 1),
        pltpu.roll(values, (160 - 8 * x) % 128, 1),
    )


def score_kernel(low, high, at, targets, mine, theirs, rows_mine, rows_theirs, out_mine, out_theirs):
    x = at[0]
    lane = lax.broadcasted_iota(jnp.int32, (8, 128), 1)
    i = lax.broadcasted_iota(jnp.int32, (128, 128), 0)
    j = lax.broadcasted_iota(jnp.int32, (128, 128), 1)
    for logits, out, p, q, core in (
        (mine, out_mine, at[4], at[5], at[1]),
        (theirs, out_theirs, at[5], at[4], 1 - at[1]),
    ):
        found = logits[...]
        lines = []
        for shift in (low, high):
            line = targets[pl.ds(core * 4 + ((q + 4 - shift) & 3), 1), :] - at[6]
            lines.append(as_gathered(jnp.broadcast_to(line, (8, 128)), lane, p, x))
        line = jnp.where(lane < 64, *lines)[:1]
        want = jnp.sum(jnp.where(i == j, line, 0), axis=1, keepdims=True)
        top = jnp.max(found, axis=1, keepdims=True)
        total = jnp.sum(jnp.exp(found - top), axis=1, keepdims=True)
        column = lax.broadcasted_iota(jnp.int32, found.shape, 1)
        hit = jnp.sum(jnp.where(column == want, found, 0.0), axis=1, keepdims=True)
        both = jnp.where(j == 0, top, jnp.where(j == 1, total, jnp.where(j == 2, hit, 0.0)))
        out[...] = in_place(jnp.transpose(both)[:8], lane, p, x)


def place_kernel(at, *refs):
    blocks, out, held = refs[:-2], refs[-2], refs[-1]
    lane = lax.broadcasted_iota(jnp.int32, (8, 128), 1)
    for k in range(2):
        p, q, core = (at[4], at[5], at[1]) if k == 0 else (at[5], at[4], 1 - at[1])
        here, early, late, far = (blocks[2 * g + k][...] for g in range(4))
        low = ((lane // 32 + 4 - p) & 3) < 2
        for shift, values in (
            (0, here),
            (1, jnp.where(low, early, late)),
            (2, far),
            (3, jnp.where(low, late, early)),
        ):
            place = core * 4 + ((q + 4 - shift) & 3)
            for row in range(3):
                held[pl.ds(8 * row + place, 1), :] = values[row : row + 1, :]
    for row in range(3):
        values = held[8 * row : 8 * row + 8, :]
        turned = {8 * k: pltpu.roll(values, 8 * k, 1) if k else values for k in range(16)}
        for x in range(X):
            picked = [
                jnp.where((lane // 8 & 3) == q, turned[(8 * q - 8 * x) % 128], 0.0) for q in range(4)
            ]
            for core in range(CORE):
                line = sum(picked[q][4 * core + q : 4 * core + q + 1, :] for q in range(4))
                out[x * CORE + core, row : row + 1, :] = line


def merged(parts):
    top = parts[0][0:1]
    for part in parts[1:]:
        top = jnp.maximum(top, part[0:1])
    total = sum(part[1:2] * jnp.exp(part[0:1] - top) for part in parts)
    hit = sum(part[2:3] for part in parts)
    return top, total, hit


def block_kernel(at, found, out):
    top, total, hit = merged([found[k] for k in range(X * CORE)])
    for k in range(Z * Y):
        out[k, 0:1, :], out[k, 1:2, :], out[k, 2:3, :] = top, total, hit


def finish_kernel(at, found, out):
    top, total, hit = merged([found[k] for k in range(Z * Y)])
    out[...] = hit - top - jnp.log(total)


def shards(
    tokens,
    log_decay,
    carried_state,
    q_weight,
    k_weight,
    v_weight,
    out_weight,
    final_gain,
    vocab_weight,
    targets,
):
    x, c, z, y = (lax.axis_index(a) for a in ALL)
    p, q = jnp.where(c == 0, y, z), jnp.where(c == 0, z, y)
    rows_here, width = tokens.shape
    heads_here = carried_state.shape[0]
    head_size = carried_state.shape[1]
    view = (rows_here, heads_here, head_size)
    vocab_local = vocab_weight.shape[1]
    offset = (((x * CORE + c) * Z + z) * Y + y) * vocab_local
    scalars = jnp.stack([x, c, z, y, p, q, offset, offset]).astype(jnp.int32)

    keys = jnp.dot(tokens, k_weight, preferred_element_type=F32).astype(BF16).reshape(view)
    values = jnp.dot(tokens, v_weight, preferred_element_type=F32).astype(BF16).reshape(view)
    lower = jnp.arange(rows_here)[:, None] >= jnp.arange(rows_here)[None, :]
    cumul = jnp.dot(lower.astype(F32), log_decay, precision=HIGHEST)
    last_cum = cumul[-1]
    ends = jnp.exp(last_cum[None, :] - cumul)
    state = jnp.einsum(
        "thd,the->hde",
        keys.astype(F32) * ends[:, :, None],
        values.astype(F32),
        precision=HIGHEST,
    )
    decay = jnp.broadcast_to(jnp.exp(last_cum)[:, None, None], (heads_here, 8, head_size))
    mine = jnp.concatenate([state, decay], axis=1)
    theirs = move(mine, other_core)
    chip = local(
        combine_kernel,
        on_chip((heads_here, head_size + 16, head_size), BF16),
        scalars,
        mine,
        theirs,
        name="combine",
    )
    tokens_then, chip = lax.optimization_barrier((tokens, chip))
    arrived = [(s, move(chip, along_x(s))) for s in (3, 2, 1)]

    queries = jnp.dot(tokens_then, q_weight, preferred_element_type=F32).astype(BF16).reshape(view)
    scores = jnp.einsum("thd,shd->hts", queries, keys, preferred_element_type=F32)
    diff = jnp.transpose(cumul[:, None, :] - cumul[None, :, :], (2, 0, 1))
    weight = (scores * jnp.exp(jnp.where(lower[None], diff, -1e30))).astype(BF16)
    intra = jnp.einsum("hts,shd->thd", weight, values, preferred_element_type=F32)

    state_in = local(
        state_kernel,
        on_chip(carried_state.shape, F32),
        scalars,
        carried_state,
        *[message for _, message in arrived],
        theirs,
        name="state",
    )
    inter = jnp.exp(cumul)[:, :, None] * jnp.einsum(
        "thd,hde->the", queries.astype(F32), state_in, precision=HIGHEST
    )
    attended = intra + inter
    normed_heads = attended * lax.rsqrt(
        jnp.mean(attended * attended, axis=-1, keepdims=True) + 1e-06
    )
    flat_heads = normed_heads.astype(BF16).reshape(rows_here, heads_here * head_size)

    inner = flat_heads.shape[1]
    wide = width // 3 if width % 384 == 0 else width
    share = pl.BlockSpec((32, wide), lambda n: (0, n))
    own, *sent = pl.pallas_call(
        project_kernel,
        out_shape=[in_hbm((32, width), F32)] + [in_hbm((32, width), BF16)] * 3,
        grid=(width // wide,),
        in_specs=[
            SCALARS,
            pl.BlockSpec((rows_here, inner), lambda n: (0, 0)),
            pl.BlockSpec((inner, wide), lambda n: (0, n)),
        ],
        out_specs=[share] * 4,
        scratch_shapes=[pltpu.VMEM((rows_here, inner), BF16)],
        compiler_params=pltpu.CompilerParams(vmem_limit_bytes=12 * 1024 * 1024),
        cost_estimate=pl.CostEstimate(
            flops=2 * rows_here * inner * width,
            bytes_accessed=2 * width * (inner + rows_here),
            transcendentals=0,
        ),
        name="project",
    )(scalars, flat_heads, leave(out_weight))
    came = [move(part, along_p(s)) for s, part in zip((1, 2, 3), sent)]
    own, *sent = local(
        partial_kernel,
        [on_chip((8, width), F32)] + [on_chip((8, width), BF16)] * 3,
        scalars,
        *came,
        loose=(own,),
        scratch=[pltpu.VMEM((32, width), F32)],
        bytes_=32 * width * 8,
        mib=8,
        name="partial",
    )
    came = [move(part, along_q(s)) for s, part in zip((1, 2, 3), sent)]
    own_tokens = lax.dynamic_slice_in_dim(tokens, 32 * p + 8 * q, 8, 0).astype(F32)
    final_rows = local(
        norm_kernel,
        on_chip((8, width), BF16),
        scalars,
        own,
        *came,
        own_tokens,
        final_gain.reshape(1, width),
        bytes_=8 * width * 16,
        name="norm",
    )

    on_x = gather(final_rows, along_x, scalars, "stack_x")
    on_x, source = lax.optimization_barrier((on_x, vocab_weight))
    vocab = pl.pallas_call(
        load_kernel,
        out_shape=on_chip(vocab_weight.shape, BF16),
        in_specs=[pl.BlockSpec(memory_space=pltpu.HBM)],
        out_specs=ANYWHERE,
        scratch_shapes=[pltpu.SemaphoreType.DMA],
        compiler_params=pltpu.CompilerParams(vmem_limit_bytes=1024 * 1024),
        cost_estimate=pl.CostEstimate(
            flops=0, bytes_accessed=4 * width * vocab_local, transcendentals=0
        ),
        name="load",
    )(leave(source))
    ours = gather(on_x, along_p, scalars, "stack_p")
    theirs = move(ours, other_core)
    ours, theirs = lax.optimization_barrier((ours, theirs))
    lines = jnp.transpose(targets.reshape(X, CORE, 4, 4, 8), (1, 3, 2, 0, 4)).reshape(8, 128)
    half = ours.shape[0] // 2
    low, high = ours[:half], ours[half:]
    early = (move(low, along_q(1)), move(high, along_q(3)))
    late = (move(low, along_q(3)), move(high, along_q(1)))
    far = (move(early[0], along_q(1)), move(early[1], along_q(3)))
    found = []
    for s, block in (((0, 0), ours), ((1, 3), early), ((3, 1), late), ((2, 2), far)):
        if s == (0, 0):
            swapped = theirs
        else:
            if s != (1, 3):
                block, found = lax.optimization_barrier((block, found))
            block = jnp.concatenate(block, axis=0)
            swapped = move(block, other_core)
        logits = [jnp.dot(b, vocab, preferred_element_type=F32) for b in (block, swapped)]
        found += local(
            functools.partial(score_kernel, *s),
            [on_chip((8, 128), F32)] * 2,
            scalars,
            lines,
            *logits,
            unread=(block, swapped),
            bytes_=8 * 128 * vocab_local,
            name="score",
        )
    sent = local(
        place_kernel,
        on_chip((X * CORE, 8, 128), F32),
        scalars,
        *found,
        scratch=[pltpu.VMEM((24, 128), F32)],
        name="place",
    )
    came = lax.all_to_all(sent, ("x", "core"), 0, 0)
    sent = local(block_kernel, on_chip((Z * Y, 8, 128), F32), scalars, came, name="block")
    came = lax.all_to_all(sent, ("z", "y"), 0, 0)
    loglik = local(
        finish_kernel, jax.ShapeDtypeStruct((1, 128), F32), scalars, came, name="finish"
    )
    return loglik.reshape(rows_here)


def solution(mesh):
    fine = Mesh(mesh.devices.reshape(X, CORE, Z, Y), ALL)
    seq, head = (("x", "core"), ("z", "y"))
    return jax.shard_map(
        shards,
        mesh=fine,
        in_specs=(
            P(seq, None),
            P(seq, head),
            P(head, None, None),
            P(None, head),
            P(None, head),
            P(None, head),
            P(head, None),
            P(),
            P(None, ALL),
            P(),
        ),
        out_specs=P(seq),
        check_vma=False,
    )
```

```python
import functools

import jax
import jax.numpy as jnp
from jax import lax
from jax.experimental import pallas as pl
from jax.experimental.pallas import tpu as pltpu
from jax.sharding import Mesh, PartitionSpec as P

X, CORE, Z, Y = 4, 2, 4, 4
ALL = ("x", "core", "z", "y")
F32 = jnp.float32
BF16 = jnp.bfloat16
HIGHEST = lax.Precision.HIGHEST


def move(array, target):
    pairs = []
    for i in range(X * CORE * Z * Y):
        at = (i // (CORE * Z * Y), i // (Z * Y) % CORE, i // Y % Z, i % Y)
        to = target(*at)
        pairs.append((i, ((to[0] * CORE + to[1]) * Z + to[2]) * Y + to[3]))
    return lax.ppermute(array, ALL, pairs)


def other_core(x, c, z, y):
    return (x, 1 - c, z, y)


def along_x(s):
    return lambda x, c, z, y: ((x + s) % X, c, z, y)


def along_p(s):
    return lambda x, c, z, y: (x, c, z, (y + s) % Y) if c == 0 else (x, c, (z + s) % Z, y)


def along_q(s):
    return lambda x, c, z, y: (x, c, (z + s) % Z, y) if c == 0 else (x, c, z, (y + s) % Y)


def on_chip(shape, dtype):
    return pltpu.VMEM(shape, dtype)


def in_hbm(shape, dtype):
    return pltpu.HBM(shape, dtype)


def leave(array):
    return pltpu.with_memory_space_constraint(array, pltpu.HBM)


def pin(array):
    return pltpu.with_memory_space_constraint(array, pltpu.VMEM)


ANYWHERE = pl.BlockSpec(memory_space=pl.ANY)
SCALARS = pl.BlockSpec(memory_space=pltpu.SMEM)
WHOLE = pl.BlockSpec(memory_space=pltpu.VMEM)


def local(kernel, outs, scalars, *arrays, loose=(), unread=(), scratch=(), flops=0, bytes_=0, mib=4, name=None):
    many = isinstance(outs, list)
    specs = [WHOLE] * len(outs) if many else WHOLE
    return pl.pallas_call(
        kernel,
        out_shape=outs,
        in_specs=[SCALARS] + [WHOLE] * len((*arrays, *loose)) + [ANYWHERE] * len(unread),
        out_specs=specs,
        scratch_shapes=list(scratch),
        compiler_params=pltpu.CompilerParams(vmem_limit_bytes=mib * 1024 * 1024),
        cost_estimate=pl.CostEstimate(flops=flops, bytes_accessed=bytes_, transcendentals=0),
        name=name,
    )(scalars, *[pin(a) for a in arrays], *[leave(a) for a in loose], *[pin(a) for a in unread])


def load_kernel(source, out, done):
    copy = pltpu.make_async_copy(source, out, done)
    copy.start()
    copy.wait()


def combine_kernel(at, mine, theirs, chip):
    size = mine.shape[2]
    low = at[1] == 0
    for h in range(mine.shape[0]):
        first = jnp.where(low, mine[h], theirs[h])
        second = jnp.where(low, theirs[h], mine[h])
        decay = jnp.broadcast_to((second[size:] * first[size:])[:1], (16, size))
        coarse = decay.astype(BF16).astype(F32)
        row = lax.broadcasted_iota(jnp.int32, (16, size), 0)
        chip[h, :size, :] = (second[size : size + 1] * first[:size] + second[:size]).astype(BF16)
        chip[h, size:, :] = jnp.where(row < 8, coarse, decay - coarse).astype(BF16)


def state_kernel(at, carried, three, two, one, theirs, out):
    size = carried.shape[2]
    for h in range(carried.shape[0]):
        state = carried[h]
        for s, message in ((3, three), (2, two), (1, one)):
            part = message[h].astype(F32)
            decay = part[size : size + 1] + part[size + 8 : size + 9]
            state = jnp.where(at[0] >= s, decay * state + part[:size], state)
        part = theirs[h]
        out[h] = jnp.where(at[1] == 1, part[size : size + 1] * state + part[:size], state)


def project_kernel(at, heads, weight, own, one, two, three, rolled):
    @pl.when(pl.program_id(0) == 0)
    def _():
        for s in range(4):
            start = pl.multiple_of((at[4] + s) % 4 * 32, 32)
            rolled[pl.ds(32 * s, 32), :] = heads[pl.ds(start, 32), :]

    out = jnp.dot(rolled[...], weight[...], preferred_element_type=F32)
    own[...] = out[:32]
    one[...] = out[32:64].astype(BF16)
    two[...] = out[64:96].astype(BF16)
    three[...] = out[96:].astype(BF16)


def partial_kernel(at, one, two, three, own, mine, first, second, third, total):
    q = at[5]
    total[...] = (
        own[...]
        + one[...].astype(F32)
        + two[...].astype(F32)
        + three[...].astype(F32)
    )
    for s, out in enumerate((mine, first, second, third)):
        start = pl.multiple_of((q + s) % 4 * 8, 8)
        out[...] = total[pl.ds(start, 8), :].astype(out.dtype)


def norm_kernel(at, own, one, two, three, tokens, gain, out):
    resid = (
        tokens[...]
        + own[...]
        + one[...].astype(F32)
        + two[...].astype(F32)
        + three[...].astype(F32)
    )
    scale = lax.rsqrt(jnp.mean(resid * resid, axis=1, keepdims=True) + 1e-06)
    out[...] = (resid * scale * gain[...].astype(F32)).astype(BF16)


def stack_kernel(at, a, b, c, d, out):
    rows = a.shape[0]
    out[0 : 2 * rows, :] = jnp.concatenate([a[...], b[...]], axis=0)
    out[2 * rows : 4 * rows, :] = jnp.concatenate([c[...], d[...]], axis=0)


def gather(block, target, scalars, name):
    parts = [move(block, target(s)) for s in (3, 2, 1)]
    rows, width = block.shape
    return local(
        stack_kernel,
        on_chip((4 * rows, width), block.dtype),
        scalars,
        block,
        *parts,
        bytes_=16 * rows * width,
        mib=8,
        name=name,
    )


def in_place(values, lane, p, x):
    values = pltpu.roll(values, 32 * p, 1)
    return jnp.where(
        (lane & 31) >= 8 * x,
        pltpu.roll(values, 8 * x, 1),
        pltpu.roll(values, (8 * x + 96) % 128, 1),
    )


def as_gathered(values, lane, p, x):
    values = pltpu.roll(values, (128 - 32 * p) % 128, 1)
    return jnp.where(
        (lane & 31) < 32 - 8 * x,
        pltpu.roll(values, (128 - 8 * x) % 128, 1),
        pltpu.roll(values, (160 - 8 * x) % 128, 1),
    )


def score_kernel(low, high, at, targets, mine, theirs, rows_mine, rows_theirs, out_mine, out_theirs):
    x = at[0]
    lane = lax.broadcasted_iota(jnp.int32, (8, 128), 1)
    i = lax.broadcasted_iota(jnp.int32, (128, 128), 0)
    j = lax.broadcasted_iota(jnp.int32, (128, 128), 1)
    for logits, out, p, q, core in (
        (mine, out_mine, at[4], at[5], at[1]),
        (theirs, out_theirs, at[5], at[4], 1 - at[1]),
    ):
        found = logits[...]
        lines = []
        for shift in (low, high):
            line = targets[pl.ds(core * 4 + ((q + 4 - shift) & 3), 1), :] - at[6]
            lines.append(as_gathered(jnp.broadcast_to(line, (8, 128)), lane, p, x))
        line = jnp.where(lane < 64, *lines)[:1]
        want = jnp.sum(jnp.where(i == j, line, 0), axis=1, keepdims=True)
        top = jnp.max(found, axis=1, keepdims=True)
        total = jnp.sum(jnp.exp(found - top), axis=1, keepdims=True)
        column = lax.broadcasted_iota(jnp.int32, found.shape, 1)
        hit = jnp.sum(jnp.where(column == want, found, 0.0), axis=1, keepdims=True)
        both = jnp.where(j == 0, top, jnp.where(j == 1, total, jnp.where(j == 2, hit, 0.0)))
        out[...] = in_place(jnp.transpose(both)[:8], lane, p, x)


def place_kernel(at, *refs):
    blocks, out, held = refs[:-2], refs[-2], refs[-1]
    lane = lax.broadcasted_iota(jnp.int32, (8, 128), 1)
    for k in range(2):
        p, q, core = (at[4], at[5], at[1]) if k == 0 else (at[5], at[4], 1 - at[1])
        here, early, late, far = (blocks[2 * g + k][...] for g in range(4))
        low = ((lane // 32 + 4 - p) & 3) < 2
        for shift, values in (
            (0, here),
            (1, jnp.where(low, early, late)),
            (2, far),
            (3, jnp.where(low, late, early)),
        ):
            place = core * 4 + ((q + 4 - shift) & 3)
            for row in range(3):
                held[pl.ds(8 * row + place, 1), :] = values[row : row + 1, :]
    for row in range(3):
        values = held[8 * row : 8 * row + 8, :]
        turned = {8 * k: pltpu.roll(values, 8 * k, 1) if k else values for k in range(16)}
        for x in range(X):
            picked = [
                jnp.where((lane // 8 & 3) == q, turned[(8 * q - 8 * x) % 128], 0.0) for q in range(4)
            ]
            for core in range(CORE):
                line = sum(picked[q][4 * core + q : 4 * core + q + 1, :] for q in range(4))
                out[x * CORE + core, row : row + 1, :] = line


def merged(parts):
    top = parts[0][0:1]
    for part in parts[1:]:
        top = jnp.maximum(top, part[0:1])
    total = sum(part[1:2] * jnp.exp(part[0:1] - top) for part in parts)
    hit = sum(part[2:3] for part in parts)
    return top, total, hit


def block_kernel(at, found, out):
    top, total, hit = merged([found[k] for k in range(X * CORE)])
    for k in range(Z * Y):
        out[k, 0:1, :], out[k, 1:2, :], out[k, 2:3, :] = top, total, hit


def finish_kernel(at, found, out):
    top, total, hit = merged([found[k] for k in range(Z * Y)])
    out[...] = hit - top - jnp.log(total)


def shards(
    tokens,
    log_decay,
    carried_state,
    q_weight,
    k_weight,
    v_weight,
    out_weight,
    final_gain,
    vocab_weight,
    targets,
):
    x, c, z, y = (lax.axis_index(a) for a in ALL)
    p, q = jnp.where(c == 0, y, z), jnp.where(c == 0, z, y)
    rows_here, width = tokens.shape
    heads_here = carried_state.shape[0]
    head_size = carried_state.shape[1]
    view = (rows_here, heads_here, head_size)
    vocab_local = vocab_weight.shape[1]
    offset = (((x * CORE + c) * Z + z) * Y + y) * vocab_local
    scalars = jnp.stack([x, c, z, y, p, q, offset, offset]).astype(jnp.int32)

    keys = jnp.dot(tokens, k_weight, preferred_element_type=F32).astype(BF16).reshape(view)
    values = jnp.dot(tokens, v_weight, preferred_element_type=F32).astype(BF16).reshape(view)
    lower = jnp.arange(rows_here)[:, None] >= jnp.arange(rows_here)[None, :]
    cumul = jnp.dot(lower.astype(F32), log_decay, precision=HIGHEST)
    last_cum = cumul[-1]
    ends = jnp.exp(last_cum[None, :] - cumul)
    state = jnp.einsum(
        "thd,the->hde",
        keys.astype(F32) * ends[:, :, None],
        values.astype(F32),
        precision=HIGHEST,
    )
    decay = jnp.broadcast_to(jnp.exp(last_cum)[:, None, None], (heads_here, 8, head_size))
    mine = jnp.concatenate([state, decay], axis=1)
    theirs = move(mine, other_core)
    chip = local(
        combine_kernel,
        on_chip((heads_here, head_size + 16, head_size), BF16),
        scalars,
        mine,
        theirs,
        name="combine",
    )
    tokens_then, chip = lax.optimization_barrier((tokens, chip))
    arrived = [(s, move(chip, along_x(s))) for s in (3, 2, 1)]

    queries = jnp.dot(tokens_then, q_weight, preferred_element_type=F32).astype(BF16).reshape(view)
    scores = jnp.einsum("thd,shd->hts", queries, keys, preferred_element_type=F32)
    diff = jnp.transpose(cumul[:, None, :] - cumul[None, :, :], (2, 0, 1))
    weight = (scores * jnp.exp(jnp.where(lower[None], diff, -1e30))).astype(BF16)
    intra = jnp.einsum("hts,shd->thd", weight, values, preferred_element_type=F32)

    state_in = local(
        state_kernel,
        on_chip(carried_state.shape, F32),
        scalars,
        carried_state,
        *[message for _, message in arrived],
        theirs,
        name="state",
    )
    inter = jnp.exp(cumul)[:, :, None] * jnp.einsum(
        "thd,hde->the", queries.astype(F32), state_in, precision=HIGHEST
    )
    attended = intra + inter
    normed_heads = attended * lax.rsqrt(
        jnp.mean(attended * attended, axis=-1, keepdims=True) + 1e-06
    )
    flat_heads = normed_heads.astype(BF16).reshape(rows_here, heads_here * head_size)

    inner = flat_heads.shape[1]
    wide = width // 3 if width % 384 == 0 else width
    share = pl.BlockSpec((32, wide), lambda n: (0, n))
    own, *sent = pl.pallas_call(
        project_kernel,
        out_shape=[in_hbm((32, width), F32)] + [in_hbm((32, width), BF16)] * 3,
        grid=(width // wide,),
        in_specs=[
            SCALARS,
            pl.BlockSpec((rows_here, inner), lambda n: (0, 0)),
            pl.BlockSpec((inner, wide), lambda n: (0, n)),
        ],
        out_specs=[share] * 4,
        scratch_shapes=[pltpu.VMEM((rows_here, inner), BF16)],
        compiler_params=pltpu.CompilerParams(vmem_limit_bytes=12 * 1024 * 1024),
        cost_estimate=pl.CostEstimate(
            flops=2 * rows_here * inner * width,
            bytes_accessed=2 * width * (inner + rows_here),
            transcendentals=0,
        ),
        name="project",
    )(scalars, flat_heads, leave(out_weight))
    came = [move(part, along_p(s)) for s, part in zip((1, 2, 3), sent)]
    own, *sent = local(
        partial_kernel,
        [on_chip((8, width), F32)] + [on_chip((8, width), BF16)] * 3,
        scalars,
        *came,
        loose=(own,),
        scratch=[pltpu.VMEM((32, width), F32)],
        bytes_=32 * width * 8,
        mib=8,
        name="partial",
    )
    came = [move(part, along_q(s)) for s, part in zip((1, 2, 3), sent)]
    own_tokens = lax.dynamic_slice_in_dim(tokens, 32 * p + 8 * q, 8, 0).astype(F32)
    final_rows = local(
        norm_kernel,
        on_chip((8, width), BF16),
        scalars,
        own,
        *came,
        own_tokens,
        final_gain.reshape(1, width),
        bytes_=8 * width * 16,
        name="norm",
    )

    on_x = gather(final_rows, along_x, scalars, "stack_x")
    on_x, source = lax.optimization_barrier((on_x, vocab_weight))
    vocab = pl.pallas_call(
        load_kernel,
        out_shape=on_chip(vocab_weight.shape, BF16),
        in_specs=[pl.BlockSpec(memory_space=pltpu.HBM)],
        out_specs=ANYWHERE,
        scratch_shapes=[pltpu.SemaphoreType.DMA],
        compiler_params=pltpu.CompilerParams(vmem_limit_bytes=1024 * 1024),
        cost_estimate=pl.CostEstimate(
            flops=0, bytes_accessed=4 * width * vocab_local, transcendentals=0
        ),
        name="load",
    )(leave(source))
    ours = gather(on_x, along_p, scalars, "stack_p")
    theirs = move(ours, other_core)
    ours, theirs = lax.optimization_barrier((ours, theirs))
    lines = jnp.transpose(targets.reshape(X, CORE, 4, 4, 8), (1, 3, 2, 0, 4)).reshape(8, 128)
    half = ours.shape[0] // 2
    low, high = ours[:half], ours[half:]
    early = (move(low, along_q(1)), move(high, along_q(3)))
    first = jnp.dot(ours, vocab, preferred_element_type=F32)
    low, high, first = lax.optimization_barrier((low, high, first))
    late = (move(low, along_q(3)), move(high, along_q(1)))
    far = (move(early[0], along_q(1)), move(early[1], along_q(3)))
    def dot(rows):
        return jnp.dot(rows, vocab, preferred_element_type=F32)

    def score(shifts, blocks, logits):
        return local(
            functools.partial(score_kernel, *shifts),
            [on_chip((8, 128), F32)] * 2,
            scalars,
            lines,
            *logits,
            unread=blocks,
            bytes_=8 * 128 * vocab_local,
            name="score",
        )

    def both(parts):
        joined = jnp.concatenate(parts, axis=0)
        return joined, move(joined, other_core)

    found = score((0, 0), (ours, theirs), (first, dot(theirs)))
    blocks = both(early)
    found += score((1, 3), blocks, [dot(b) for b in blocks])
    late, found = lax.optimization_barrier((late, found))
    blocks = both(late)
    first = dot(blocks[0])
    far, first = lax.optimization_barrier((far, first))
    found += score((3, 1), blocks, (first, dot(blocks[1])))
    blocks = both(far)
    found += score((2, 2), blocks, [dot(b) for b in blocks])
    sent = local(
        place_kernel,
        on_chip((X * CORE, 8, 128), F32),
        scalars,
        *found,
        scratch=[pltpu.VMEM((24, 128), F32)],
        name="place",
    )
    came = lax.all_to_all(sent, ("x", "core"), 0, 0)
    sent = local(block_kernel, on_chip((Z * Y, 8, 128), F32), scalars, came, name="block")
    came = lax.all_to_all(sent, ("z", "y"), 0, 0)
    loglik = local(
        finish_kernel, jax.ShapeDtypeStruct((1, 128), F32), scalars, came, name="finish"
    )
    return loglik.reshape(rows_here)


def solution(mesh):
    fine = Mesh(mesh.devices.reshape(X, CORE, Z, Y), ALL)
    seq, head = (("x", "core"), ("z", "y"))
    return jax.shard_map(
        shards,
        mesh=fine,
        in_specs=(
            P(seq, None),
            P(seq, head),
            P(head, None, None),
            P(None, head),
            P(None, head),
            P(None, head),
            P(head, None),
            P(),
            P(None, ALL),
            P(),
        ),
        out_specs=P(seq),
        check_vma=False,
    )
```

```python
import functools

import jax
import jax.numpy as jnp
from jax import lax
from jax.experimental import pallas as pl
from jax.experimental.pallas import tpu as pltpu
from jax.sharding import Mesh, PartitionSpec as P

X, CORE, Z, Y = 4, 2, 4, 4
ALL = ("x", "core", "z", "y")
F32 = jnp.float32
BF16 = jnp.bfloat16
HIGHEST = lax.Precision.HIGHEST


def move(array, target):
    pairs = []
    for i in range(X * CORE * Z * Y):
        at = (i // (CORE * Z * Y), i // (Z * Y) % CORE, i // Y % Z, i % Y)
        to = target(*at)
        pairs.append((i, ((to[0] * CORE + to[1]) * Z + to[2]) * Y + to[3]))
    return lax.ppermute(array, ALL, pairs)


def other_core(x, c, z, y):
    return (x, 1 - c, z, y)


def along_x(s):
    return lambda x, c, z, y: ((x + s) % X, c, z, y)


def along_p(s):
    return lambda x, c, z, y: (x, c, z, (y + s) % Y) if c == 0 else (x, c, (z + s) % Z, y)


def along_q(s):
    return lambda x, c, z, y: (x, c, (z + s) % Z, y) if c == 0 else (x, c, z, (y + s) % Y)


def on_chip(shape, dtype):
    return pltpu.VMEM(shape, dtype)


def in_hbm(shape, dtype):
    return pltpu.HBM(shape, dtype)


def leave(array):
    return pltpu.with_memory_space_constraint(array, pltpu.HBM)


def pin(array):
    return pltpu.with_memory_space_constraint(array, pltpu.VMEM)


ANYWHERE = pl.BlockSpec(memory_space=pl.ANY)
SCALARS = pl.BlockSpec(memory_space=pltpu.SMEM)
WHOLE = pl.BlockSpec(memory_space=pltpu.VMEM)


def local(kernel, outs, scalars, *arrays, loose=(), unread=(), scratch=(), flops=0, bytes_=0, mib=4, name=None):
    many = isinstance(outs, list)
    specs = [WHOLE] * len(outs) if many else WHOLE
    return pl.pallas_call(
        kernel,
        out_shape=outs,
        in_specs=[SCALARS] + [WHOLE] * len((*arrays, *loose)) + [ANYWHERE] * len(unread),
        out_specs=specs,
        scratch_shapes=list(scratch),
        compiler_params=pltpu.CompilerParams(vmem_limit_bytes=mib * 1024 * 1024),
        cost_estimate=pl.CostEstimate(flops=flops, bytes_accessed=bytes_, transcendentals=0),
        name=name,
    )(scalars, *[pin(a) for a in arrays], *[leave(a) for a in loose], *[pin(a) for a in unread])


def load_kernel(source, out, done):
    copy = pltpu.make_async_copy(source, out, done)
    copy.start()
    copy.wait()


def heads_kernel(count, tokens, *refs):
    weights, outs, totals = refs[:count], refs[count : 2 * count], refs[2 * count :]
    step = pl.program_id(0)
    for weight, out, total in zip(weights, outs, totals):
        part = jnp.dot(tokens[...], weight[...], preferred_element_type=F32)

        @pl.when(step == 0)
        def _():
            total[...] = part

        @pl.when(step > 0)
        def _():
            total[...] += part

        @pl.when(step == pl.num_programs(0) - 1)
        def _():
            out[...] = total[...].astype(BF16)


def heads(tokens, *weights):
    rows, width = tokens.shape
    columns = weights[0].shape[1]
    count = len(weights)
    deep = width // 6 if width % 768 == 0 else width
    return pl.pallas_call(
        functools.partial(heads_kernel, count),
        out_shape=[jax.ShapeDtypeStruct((rows, columns), BF16)] * count,
        grid=(width // deep,),
        in_specs=[pl.BlockSpec((rows, deep), lambda n: (0, n))]
        + [pl.BlockSpec((deep, columns), lambda n: (n, 0))] * count,
        out_specs=[pl.BlockSpec((rows, columns), lambda n: (0, 0))] * count,
        scratch_shapes=[pltpu.VMEM((rows, columns), F32)] * count,
        compiler_params=pltpu.CompilerParams(vmem_limit_bytes=8 * 1024 * 1024),
        cost_estimate=pl.CostEstimate(
            flops=2 * rows * width * columns * count,
            bytes_accessed=2 * width * (rows + columns * count),
            transcendentals=0,
        ),
        name="heads",
    )(leave(tokens), *[leave(w) for w in weights])


def combine_kernel(at, mine, theirs, chip):
    size = mine.shape[2]
    low = at[1] == 0
    for h in range(mine.shape[0]):
        first = jnp.where(low, mine[h], theirs[h])
        second = jnp.where(low, theirs[h], mine[h])
        decay = jnp.broadcast_to((second[size:] * first[size:])[:1], (16, size))
        coarse = decay.astype(BF16).astype(F32)
        row = lax.broadcasted_iota(jnp.int32, (16, size), 0)
        chip[h, :size, :] = (second[size : size + 1] * first[:size] + second[:size]).astype(BF16)
        chip[h, size:, :] = jnp.where(row < 8, coarse, decay - coarse).astype(BF16)


def state_kernel(at, carried, three, two, one, theirs, out):
    size = carried.shape[2]
    for h in range(carried.shape[0]):
        state = carried[h]
        for s, message in ((3, three), (2, two), (1, one)):
            part = message[h].astype(F32)
            decay = part[size : size + 1] + part[size + 8 : size + 9]
            state = jnp.where(at[0] >= s, decay * state + part[:size], state)
        part = theirs[h]
        out[h] = jnp.where(at[1] == 1, part[size : size + 1] * state + part[:size], state)


def project_kernel(at, heads, weight, own, one, two, three, rolled):
    @pl.when(pl.program_id(0) == 0)
    def _():
        for k, s in enumerate((0, 2, 1, 3)):
            start = pl.multiple_of((at[4] + s) % 4 * 32, 32)
            rolled[pl.ds(32 * k, 32), :] = heads[pl.ds(start, 32), :]

    out = jnp.dot(rolled[...], weight[...], preferred_element_type=F32)
    own[...] = out[:32]
    one[...] = out[32:64].astype(BF16)
    two[...] = out[64:96].astype(BF16)
    three[...] = out[96:].astype(BF16)


def partial_kernel(at, one, two, three, own, mine, first, second, third, total):
    q = at[5]
    total[...] = (
        own[...]
        + one[...].astype(F32)
        + two[...].astype(F32)
        + three[...].astype(F32)
    )
    for s, out in ((0, mine), (2, first), (1, second), (3, third)):
        start = pl.multiple_of((q + s) % 4 * 8, 8)
        out[...] = total[pl.ds(start, 8), :].astype(out.dtype)


def norm_kernel(at, own, one, two, three, tokens, gain, out):
    resid = (
        tokens[...]
        + own[...]
        + one[...].astype(F32)
        + two[...].astype(F32)
        + three[...].astype(F32)
    )
    scale = lax.rsqrt(jnp.mean(resid * resid, axis=1, keepdims=True) + 1e-06)
    out[...] = (resid * scale * gain[...].astype(F32)).astype(BF16)


def stack_kernel(at, *refs):
    *parts, out = refs
    if parts[0].shape[0] % 16:
        parts = [jnp.concatenate([a[...], b[...]], axis=0) for a, b in zip(parts[::2], parts[1::2])]
    row = 0
    for part in parts:
        out[row : row + part.shape[0], :] = part[...]
        row += part.shape[0]


def gather(block, target, scalars, name, forward=False):
    if forward:
        half = block.shape[0] // 2
        up, down = move(block, target(1)), move(block, target(3))
        parts = [down, move(up[:half], target(1)), move(down[half:], target(3)), up]
    else:
        far, after, before = (move(block, target(s)) for s in (2, 3, 1))
        parts = [after, far, before]
    rows, width = block.shape
    return local(
        stack_kernel,
        on_chip((4 * rows, width), block.dtype),
        scalars,
        block,
        *parts,
        bytes_=16 * rows * width,
        mib=8,
        name=name,
    )


def in_place(values, lane, p, x):
    values = pltpu.roll(values, 32 * p, 1)
    return jnp.where(
        (lane & 31) >= 8 * x,
        pltpu.roll(values, 8 * x, 1),
        pltpu.roll(values, (8 * x + 96) % 128, 1),
    )


def as_gathered(values, lane, p, x):
    values = pltpu.roll(values, (128 - 32 * p) % 128, 1)
    return jnp.where(
        (lane & 31) < 32 - 8 * x,
        pltpu.roll(values, (128 - 8 * x) % 128, 1),
        pltpu.roll(values, (160 - 8 * x) % 128, 1),
    )


def score_kernel(low, high, at, targets, mine, theirs, rows_mine, rows_theirs, out_mine, out_theirs):
    x = at[0]
    lane = lax.broadcasted_iota(jnp.int32, (8, 128), 1)
    i = lax.broadcasted_iota(jnp.int32, (128, 128), 0)
    j = lax.broadcasted_iota(jnp.int32, (128, 128), 1)
    for logits, out, p, q, core in (
        (mine, out_mine, at[4], at[5], at[1]),
        (theirs, out_theirs, at[5], at[4], 1 - at[1]),
    ):
        found = logits[...]
        lines = []
        for shift in (low, high):
            line = targets[pl.ds(core * 4 + ((q + 4 - shift) & 3), 1), :] - at[6]
            lines.append(as_gathered(jnp.broadcast_to(line, (8, 128)), lane, p, x))
        line = jnp.where(lane < 64, *lines)[:1]
        want = jnp.sum(jnp.where(i == j, line, 0), axis=1, keepdims=True)
        top = jnp.max(found, axis=1, keepdims=True)
        total = jnp.sum(jnp.exp(found - top), axis=1, keepdims=True)
        column = lax.broadcasted_iota(jnp.int32, found.shape, 1)
        hit = jnp.sum(jnp.where(column == want, found, 0.0), axis=1, keepdims=True)
        both = jnp.where(j == 0, top, jnp.where(j == 1, total, jnp.where(j == 2, hit, 0.0)))
        out[...] = in_place(jnp.transpose(both)[:8], lane, p, x)


def place_kernel(at, *refs):
    blocks, out, held = refs[:-2], refs[-2], refs[-1]
    lane = lax.broadcasted_iota(jnp.int32, (8, 128), 1)
    for k in range(2):
        p, q, core = (at[4], at[5], at[1]) if k == 0 else (at[5], at[4], 1 - at[1])
        here, early, late, far = (blocks[2 * g + k][...] for g in range(4))
        low = ((lane // 32 + 4 - p) & 3) < 2
        for shift, values in (
            (0, here),
            (1, jnp.where(low, early, late)),
            (2, far),
            (3, jnp.where(low, late, early)),
        ):
            place = core * 4 + ((q + 4 - shift) & 3)
            for row in range(3):
                held[pl.ds(8 * row + place, 1), :] = values[row : row + 1, :]
    for row in range(3):
        values = held[8 * row : 8 * row + 8, :]
        turned = {8 * k: pltpu.roll(values, 8 * k, 1) if k else values for k in range(16)}
        for x in range(X):
            picked = [
                jnp.where((lane // 8 & 3) == q, turned[(8 * q - 8 * x) % 128], 0.0) for q in range(4)
            ]
            for core in range(CORE):
                line = sum(picked[q][4 * core + q : 4 * core + q + 1, :] for q in range(4))
                out[x * CORE + core, row : row + 1, :] = line


def merged(parts):
    top = parts[0][0:1]
    for part in parts[1:]:
        top = jnp.maximum(top, part[0:1])
    total = sum(part[1:2] * jnp.exp(part[0:1] - top) for part in parts)
    hit = sum(part[2:3] for part in parts)
    return top, total, hit


def block_kernel(at, found, out):
    top, total, hit = merged([found[k] for k in range(X * CORE)])
    for k in range(Z * Y):
        out[k, 0:1, :], out[k, 1:2, :], out[k, 2:3, :] = top, total, hit


def finish_kernel(at, found, out):
    top, total, hit = merged([found[k] for k in range(Z * Y)])
    out[...] = hit - top - jnp.log(total)


def shards(
    tokens,
    log_decay,
    carried_state,
    q_weight,
    k_weight,
    v_weight,
    out_weight,
    final_gain,
    vocab_weight,
    targets,
):
    x, c, z, y = (lax.axis_index(a) for a in ALL)
    p, q = jnp.where(c == 0, y, z), jnp.where(c == 0, z, y)
    rows_here, width = tokens.shape
    heads_here = carried_state.shape[0]
    head_size = carried_state.shape[1]
    view = (rows_here, heads_here, head_size)
    vocab_local = vocab_weight.shape[1]
    offset = (((x * CORE + c) * Z + z) * Y + y) * vocab_local
    scalars = jnp.stack([x, c, z, y, p, q, offset, offset]).astype(jnp.int32)

    keys, values = (part.reshape(view) for part in heads(tokens, k_weight, v_weight))
    lower = jnp.arange(rows_here)[:, None] >= jnp.arange(rows_here)[None, :]
    cumul = jnp.dot(lower.astype(F32), log_decay, precision=HIGHEST)
    last_cum = cumul[-1]
    ends = jnp.exp(last_cum[None, :] - cumul)
    state = jnp.einsum(
        "thd,the->hde",
        keys.astype(F32) * ends[:, :, None],
        values.astype(F32),
        precision=HIGHEST,
    )
    decay = jnp.broadcast_to(jnp.exp(last_cum)[:, None, None], (heads_here, 8, head_size))
    mine = jnp.concatenate([state, decay], axis=1)
    theirs = move(mine, other_core)
    chip = local(
        combine_kernel,
        on_chip((heads_here, head_size + 16, head_size), BF16),
        scalars,
        mine,
        theirs,
        name="combine",
    )
    tokens_then, chip = lax.optimization_barrier((tokens, chip))
    arrived = [(s, move(chip, along_x(s))) for s in (3, 2, 1)]

    queries = heads(tokens_then, q_weight)[0].reshape(view)
    scores = jnp.einsum("thd,shd->hts", queries, keys, preferred_element_type=F32)
    diff = jnp.transpose(cumul[:, None, :] - cumul[None, :, :], (2, 0, 1))
    weight = (scores * jnp.exp(jnp.where(lower[None], diff, -1e30))).astype(BF16)
    intra = jnp.einsum("hts,shd->thd", weight, values, preferred_element_type=F32)

    state_in = local(
        state_kernel,
        on_chip(carried_state.shape, F32),
        scalars,
        carried_state,
        *[message for _, message in arrived],
        theirs,
        name="state",
    )
    inter = jnp.exp(cumul)[:, :, None] * jnp.einsum(
        "thd,hde->the", queries.astype(F32), state_in, precision=HIGHEST
    )
    attended = intra + inter
    normed_heads = attended * lax.rsqrt(
        jnp.mean(attended * attended, axis=-1, keepdims=True) + 1e-06
    )
    flat_heads = normed_heads.astype(BF16).reshape(rows_here, heads_here * head_size)

    inner = flat_heads.shape[1]
    wide = width // 3 if width % 384 == 0 else width
    share = pl.BlockSpec((32, wide), lambda n: (0, n))
    own, *sent = pl.pallas_call(
        project_kernel,
        out_shape=[in_hbm((32, width), F32)] + [in_hbm((32, width), BF16)] * 3,
        grid=(width // wide,),
        in_specs=[
            SCALARS,
            pl.BlockSpec((rows_here, inner), lambda n: (0, 0)),
            pl.BlockSpec((inner, wide), lambda n: (0, n)),
        ],
        out_specs=[share] * 4,
        scratch_shapes=[pltpu.VMEM((rows_here, inner), BF16)],
        compiler_params=pltpu.CompilerParams(vmem_limit_bytes=12 * 1024 * 1024),
        cost_estimate=pl.CostEstimate(
            flops=2 * rows_here * inner * width,
            bytes_accessed=2 * width * (inner + rows_here),
            transcendentals=0,
        ),
        name="project",
    )(scalars, flat_heads, leave(out_weight))
    came = [move(part, along_p(s)) for s, part in zip((2, 1, 3), sent)]
    own, *sent = local(
        partial_kernel,
        [on_chip((8, width), F32)] + [on_chip((8, width), BF16)] * 3,
        scalars,
        *came,
        loose=(own,),
        scratch=[pltpu.VMEM((32, width), F32)],
        bytes_=32 * width * 8,
        mib=8,
        name="partial",
    )
    came = [move(part, along_q(s)) for s, part in zip((2, 1, 3), sent)]
    own_tokens = lax.dynamic_slice_in_dim(tokens, 32 * p + 8 * q, 8, 0).astype(F32)
    final_rows = local(
        norm_kernel,
        on_chip((8, width), BF16),
        scalars,
        own,
        *came,
        own_tokens,
        final_gain.reshape(1, width),
        bytes_=8 * width * 16,
        name="norm",
    )

    on_x = gather(final_rows, along_x, scalars, "stack_x")
    on_x, source = lax.optimization_barrier((on_x, vocab_weight))
    vocab = pl.pallas_call(
        load_kernel,
        out_shape=on_chip(vocab_weight.shape, BF16),
        in_specs=[pl.BlockSpec(memory_space=pltpu.HBM)],
        out_specs=ANYWHERE,
        scratch_shapes=[pltpu.SemaphoreType.DMA],
        compiler_params=pltpu.CompilerParams(vmem_limit_bytes=1024 * 1024),
        cost_estimate=pl.CostEstimate(
            flops=0, bytes_accessed=4 * width * vocab_local, transcendentals=0
        ),
        name="load",
    )(leave(source))
    ours = gather(on_x, along_p, scalars, "stack_p", True)
    theirs = move(ours, other_core)
    ours, theirs = lax.optimization_barrier((ours, theirs))
    lines = jnp.transpose(targets.reshape(X, CORE, 4, 4, 8), (1, 3, 2, 0, 4)).reshape(8, 128)
    half = ours.shape[0] // 2
    low, high = ours[:half], ours[half:]
    early = (move(low, along_q(1)), move(high, along_q(3)))
    first = jnp.dot(ours, vocab, preferred_element_type=F32)
    low, high, first = lax.optimization_barrier((low, high, first))
    late = (move(low, along_q(3)), move(high, along_q(1)))
    far = (move(early[0], along_q(1)), move(early[1], along_q(3)))
    def dot(rows):
        return jnp.dot(rows, vocab, preferred_element_type=F32)

    def score(shifts, blocks, logits):
        return local(
            functools.partial(score_kernel, *shifts),
            [on_chip((8, 128), F32)] * 2,
            scalars,
            lines,
            *logits,
            unread=blocks,
            bytes_=8 * 128 * vocab_local,
            name="score",
        )

    def both(parts):
        joined = jnp.concatenate(parts, axis=0)
        return joined, move(joined, other_core)

    found = score((0, 0), (ours, theirs), (first, dot(theirs)))
    blocks = both(early)
    found += score((1, 3), blocks, [dot(b) for b in blocks])
    late, found = lax.optimization_barrier((late, found))
    blocks = both(late)
    first = dot(blocks[0])
    far, first = lax.optimization_barrier((far, first))
    found += score((3, 1), blocks, (first, dot(blocks[1])))
    blocks = both(far)
    found += score((2, 2), blocks, [dot(b) for b in blocks])
    sent = local(
        place_kernel,
        on_chip((X * CORE, 8, 128), F32),
        scalars,
        *found,
        scratch=[pltpu.VMEM((24, 128), F32)],
        name="place",
    )
    came = lax.all_to_all(sent, ("x", "core"), 0, 0)
    sent = local(block_kernel, on_chip((Z * Y, 8, 128), F32), scalars, came, name="block")
    came = lax.all_to_all(sent, ("z", "y"), 0, 0)
    loglik = local(
        finish_kernel, jax.ShapeDtypeStruct((1, 128), F32), scalars, came, name="finish"
    )
    return loglik.reshape(rows_here)


def solution(mesh):
    fine = Mesh(mesh.devices.reshape(X, CORE, Z, Y), ALL)
    seq, head = (("x", "core"), ("z", "y"))
    return jax.shard_map(
        shards,
        mesh=fine,
        in_specs=(
            P(seq, None),
            P(seq, head),
            P(head, None, None),
            P(None, head),
            P(None, head),
            P(None, head),
            P(head, None),
            P(),
            P(None, ALL),
            P(),
        ),
        out_specs=P(seq),
        check_vma=False,
    )
```

```python
import functools

import jax
import jax.numpy as jnp
from jax import lax
from jax.experimental import pallas as pl
from jax.experimental.pallas import tpu as pltpu
from jax.sharding import Mesh, PartitionSpec as P

X, CORE, Z, Y = 4, 2, 4, 4
ALL = ("x", "core", "z", "y")
F32 = jnp.float32
BF16 = jnp.bfloat16
HIGHEST = lax.Precision.HIGHEST


def move(array, target):
    pairs = []
    for i in range(X * CORE * Z * Y):
        at = (i // (CORE * Z * Y), i // (Z * Y) % CORE, i // Y % Z, i % Y)
        to = target(*at)
        pairs.append((i, ((to[0] * CORE + to[1]) * Z + to[2]) * Y + to[3]))
    return lax.ppermute(array, ALL, pairs)


def other_core(x, c, z, y):
    return (x, 1 - c, z, y)


def along_x(s):
    return lambda x, c, z, y: ((x + s) % X, c, z, y)


def along_p(s):
    return lambda x, c, z, y: (x, c, z, (y + s) % Y) if c == 0 else (x, c, (z + s) % Z, y)


def along_q(s):
    return lambda x, c, z, y: (x, c, (z + s) % Z, y) if c == 0 else (x, c, z, (y + s) % Y)


def on_chip(shape, dtype):
    return pltpu.VMEM(shape, dtype)


def in_hbm(shape, dtype):
    return pltpu.HBM(shape, dtype)


def leave(array):
    return pltpu.with_memory_space_constraint(array, pltpu.HBM)


def pin(array):
    return pltpu.with_memory_space_constraint(array, pltpu.VMEM)


ANYWHERE = pl.BlockSpec(memory_space=pl.ANY)
SCALARS = pl.BlockSpec(memory_space=pltpu.SMEM)
WHOLE = pl.BlockSpec(memory_space=pltpu.VMEM)


def local(kernel, outs, scalars, *arrays, loose=(), unread=(), scratch=(), flops=0, bytes_=0, mib=4, name=None):
    many = isinstance(outs, list)
    specs = [WHOLE] * len(outs) if many else WHOLE
    return pl.pallas_call(
        kernel,
        out_shape=outs,
        in_specs=[SCALARS] + [WHOLE] * len((*arrays, *loose)) + [ANYWHERE] * len(unread),
        out_specs=specs,
        scratch_shapes=list(scratch),
        compiler_params=pltpu.CompilerParams(vmem_limit_bytes=mib * 1024 * 1024),
        cost_estimate=pl.CostEstimate(flops=flops, bytes_accessed=bytes_, transcendentals=0),
        name=name,
    )(scalars, *[pin(a) for a in arrays], *[leave(a) for a in loose], *[pin(a) for a in unread])


def load_kernel(source, out, done):
    copy = pltpu.make_async_copy(source, out, done)
    copy.start()
    copy.wait()


def heads_kernel(count, tokens, *refs):
    weights, outs = refs[:count], refs[count : 2 * count]
    held, *held_weights, arrived = refs[2 * count :]
    chunks = arrived.shape[1]
    deep = tokens.shape[1] // chunks
    copies = []
    for n in range(chunks):
        part = pl.ds(n * deep, deep)
        copies.append(
            [pltpu.make_async_copy(tokens.at[:, part], held.at[:, part], arrived.at[count, n])]
            + [
                pltpu.make_async_copy(weight.at[part, :], here.at[part, :], arrived.at[k, n])
                for k, (weight, here) in enumerate(zip(weights, held_weights))
            ]
        )
        for copy in copies[-1]:
            copy.start()
    totals = [None] * count
    for n in range(chunks):
        part = pl.ds(n * deep, deep)
        for copy in copies[n]:
            copy.wait()
        for k, here in enumerate(held_weights):
            product = jnp.dot(held[:, part], here[part, :], preferred_element_type=F32)
            totals[k] = product if totals[k] is None else totals[k] + product
    for out, total in zip(outs, totals):
        out[...] = total.astype(BF16)


def heads(tokens, *weights):
    rows, width = tokens.shape
    columns = weights[0].shape[1]
    count = len(weights)
    chunks = 4 if width % 512 == 0 else 1
    return pl.pallas_call(
        functools.partial(heads_kernel, count),
        out_shape=[jax.ShapeDtypeStruct((rows, columns), BF16)] * count,
        in_specs=[pl.BlockSpec(memory_space=pltpu.HBM)] * (1 + count),
        out_specs=[WHOLE] * count,
        scratch_shapes=[pltpu.VMEM((rows, width), BF16)]
        + [pltpu.VMEM((width, columns), BF16)] * count
        + [pltpu.SemaphoreType.DMA((count + 1, chunks))],
        compiler_params=pltpu.CompilerParams(vmem_limit_bytes=16 * 1024 * 1024),
        cost_estimate=pl.CostEstimate(
            flops=2 * rows * width * columns * count,
            bytes_accessed=2 * width * (rows + columns * count),
            transcendentals=0,
        ),
        name="heads",
    )(leave(tokens), *[leave(w) for w in weights])


def combine_kernel(at, mine, theirs, chip):
    size = mine.shape[2]
    low = at[1] == 0
    for h in range(mine.shape[0]):
        first = jnp.where(low, mine[h], theirs[h])
        second = jnp.where(low, theirs[h], mine[h])
        decay = jnp.broadcast_to((second[size:] * first[size:])[:1], (16, size))
        coarse = decay.astype(BF16).astype(F32)
        row = lax.broadcasted_iota(jnp.int32, (16, size), 0)
        chip[h, :size, :] = (second[size : size + 1] * first[:size] + second[:size]).astype(BF16)
        chip[h, size:, :] = jnp.where(row < 8, coarse, decay - coarse).astype(BF16)


def state_kernel(at, carried, three, two, one, theirs, out):
    size = carried.shape[2]
    for h in range(carried.shape[0]):
        state = carried[h]
        for s, message in ((3, three), (2, two), (1, one)):
            part = message[h].astype(F32)
            decay = part[size : size + 1] + part[size + 8 : size + 9]
            state = jnp.where(at[0] >= s, decay * state + part[:size], state)
        part = theirs[h]
        out[h] = jnp.where(at[1] == 1, part[size : size + 1] * state + part[:size], state)


def project_kernel(at, heads, weight, own, one, two, three, rolled):
    @pl.when(pl.program_id(0) == 0)
    def _():
        for s in range(4):
            start = pl.multiple_of((at[4] + s) % 4 * 32, 32)
            rolled[pl.ds(32 * s, 32), :] = heads[pl.ds(start, 32), :]

    out = jnp.dot(rolled[...], weight[...], preferred_element_type=F32)
    own[...] = out[:32]
    one[...] = out[32:64].astype(BF16)
    two[...] = out[64:96].astype(BF16)
    three[...] = out[96:].astype(BF16)


def partial_kernel(at, one, two, three, own, mine, first, second, third, total):
    q = at[5]
    total[...] = (
        own[...]
        + one[...].astype(F32)
        + two[...].astype(F32)
        + three[...].astype(F32)
    )
    for s, out in enumerate((mine, first, second, third)):
        start = pl.multiple_of((q + s) % 4 * 8, 8)
        out[...] = total[pl.ds(start, 8), :].astype(out.dtype)


def norm_kernel(at, own, one, two, three, tokens, gain, out):
    resid = (
        tokens[...]
        + own[...]
        + one[...].astype(F32)
        + two[...].astype(F32)
        + three[...].astype(F32)
    )
    scale = lax.rsqrt(jnp.mean(resid * resid, axis=1, keepdims=True) + 1e-06)
    out[...] = (resid * scale * gain[...].astype(F32)).astype(BF16)


def stack_kernel(at, a, b, c, d, out):
    rows = a.shape[0]
    out[0 : 2 * rows, :] = jnp.concatenate([a[...], b[...]], axis=0)
    out[2 * rows : 4 * rows, :] = jnp.concatenate([c[...], d[...]], axis=0)


def gather(block, target, scalars, name):
    parts = [move(block, target(s)) for s in (3, 2, 1)]
    rows, width = block.shape
    return local(
        stack_kernel,
        on_chip((4 * rows, width), block.dtype),
        scalars,
        block,
        *parts,
        bytes_=16 * rows * width,
        mib=8,
        name=name,
    )


def in_place(values, lane, p, x):
    values = pltpu.roll(values, 32 * p, 1)
    return jnp.where(
        (lane & 31) >= 8 * x,
        pltpu.roll(values, 8 * x, 1),
        pltpu.roll(values, (8 * x + 96) % 128, 1),
    )


def as_gathered(values, lane, p, x):
    values = pltpu.roll(values, (128 - 32 * p) % 128, 1)
    return jnp.where(
        (lane & 31) < 32 - 8 * x,
        pltpu.roll(values, (128 - 8 * x) % 128, 1),
        pltpu.roll(values, (160 - 8 * x) % 128, 1),
    )


def score_kernel(low, high, at, targets, mine, theirs, rows_mine, rows_theirs, out_mine, out_theirs):
    x = at[0]
    lane = lax.broadcasted_iota(jnp.int32, (8, 128), 1)
    i = lax.broadcasted_iota(jnp.int32, (128, 128), 0)
    j = lax.broadcasted_iota(jnp.int32, (128, 128), 1)
    for logits, out, p, q, core in (
        (mine, out_mine, at[4], at[5], at[1]),
        (theirs, out_theirs, at[5], at[4], 1 - at[1]),
    ):
        found = logits[...]
        lines = []
        for shift in (low, high):
            line = targets[pl.ds(core * 4 + ((q + 4 - shift) & 3), 1), :] - at[6]
            lines.append(as_gathered(jnp.broadcast_to(line, (8, 128)), lane, p, x))
        line = jnp.where(lane < 64, *lines)[:1]
        want = jnp.sum(jnp.where(i == j, line, 0), axis=1, keepdims=True)
        top = jnp.max(found, axis=1, keepdims=True)
        total = jnp.sum(jnp.exp(found - top), axis=1, keepdims=True)
        column = lax.broadcasted_iota(jnp.int32, found.shape, 1)
        hit = jnp.sum(jnp.where(column == want, found, 0.0), axis=1, keepdims=True)
        both = jnp.where(j == 0, top, jnp.where(j == 1, total, jnp.where(j == 2, hit, 0.0)))
        out[...] = in_place(jnp.transpose(both)[:8], lane, p, x)


def place_kernel(at, *refs):
    blocks, out, held = refs[:-2], refs[-2], refs[-1]
    lane = lax.broadcasted_iota(jnp.int32, (8, 128), 1)
    for k in range(2):
        p, q, core = (at[4], at[5], at[1]) if k == 0 else (at[5], at[4], 1 - at[1])
        here, early, late, far = (blocks[2 * g + k][...] for g in range(4))
        low = ((lane // 32 + 4 - p) & 3) < 2
        for shift, values in (
            (0, here),
            (1, jnp.where(low, early, late)),
            (2, far),
            (3, jnp.where(low, late, early)),
        ):
            place = core * 4 + ((q + 4 - shift) & 3)
            for row in range(3):
                held[pl.ds(8 * row + place, 1), :] = values[row : row + 1, :]
    for row in range(3):
        values = held[8 * row : 8 * row + 8, :]
        turned = {8 * k: pltpu.roll(values, 8 * k, 1) if k else values for k in range(16)}
        for x in range(X):
            picked = [
                jnp.where((lane // 8 & 3) == q, turned[(8 * q - 8 * x) % 128], 0.0) for q in range(4)
            ]
            for core in range(CORE):
                line = sum(picked[q][4 * core + q : 4 * core + q + 1, :] for q in range(4))
                out[x * CORE + core, row : row + 1, :] = line


def merged(parts):
    top = parts[0][0:1]
    for part in parts[1:]:
        top = jnp.maximum(top, part[0:1])
    total = sum(part[1:2] * jnp.exp(part[0:1] - top) for part in parts)
    hit = sum(part[2:3] for part in parts)
    return top, total, hit


def block_kernel(at, found, out):
    top, total, hit = merged([found[k] for k in range(X * CORE)])
    for k in range(Z * Y):
        out[k, 0:1, :], out[k, 1:2, :], out[k, 2:3, :] = top, total, hit


def finish_kernel(at, found, out):
    top, total, hit = merged([found[k] for k in range(Z * Y)])
    out[...] = hit - top - jnp.log(total)


def shards(
    tokens,
    log_decay,
    carried_state,
    q_weight,
    k_weight,
    v_weight,
    out_weight,
    final_gain,
    vocab_weight,
    targets,
):
    x, c, z, y = (lax.axis_index(a) for a in ALL)
    p, q = jnp.where(c == 0, y, z), jnp.where(c == 0, z, y)
    rows_here, width = tokens.shape
    heads_here = carried_state.shape[0]
    head_size = carried_state.shape[1]
    view = (rows_here, heads_here, head_size)
    vocab_local = vocab_weight.shape[1]
    offset = (((x * CORE + c) * Z + z) * Y + y) * vocab_local
    scalars = jnp.stack([x, c, z, y, p, q, offset, offset]).astype(jnp.int32)

    keys, values = (part.reshape(view) for part in heads(tokens, k_weight, v_weight))
    lower = jnp.arange(rows_here)[:, None] >= jnp.arange(rows_here)[None, :]
    cumul = jnp.dot(lower.astype(F32), log_decay, precision=HIGHEST)
    last_cum = cumul[-1]
    ends = jnp.exp(last_cum[None, :] - cumul)
    state = jnp.einsum(
        "thd,the->hde",
        keys.astype(F32) * ends[:, :, None],
        values.astype(F32),
        precision=HIGHEST,
    )
    decay = jnp.broadcast_to(jnp.exp(last_cum)[:, None, None], (heads_here, 8, head_size))
    mine = jnp.concatenate([state, decay], axis=1)
    theirs = move(mine, other_core)
    chip = local(
        combine_kernel,
        on_chip((heads_here, head_size + 16, head_size), BF16),
        scalars,
        mine,
        theirs,
        name="combine",
    )
    tokens_then, chip = lax.optimization_barrier((tokens, chip))
    arrived = [(s, move(chip, along_x(s))) for s in (3, 2, 1)]

    queries = heads(tokens_then, q_weight)[0].reshape(view)
    scores = jnp.einsum("thd,shd->hts", queries, keys, preferred_element_type=F32)
    diff = jnp.transpose(cumul[:, None, :] - cumul[None, :, :], (2, 0, 1))
    weight = (scores * jnp.exp(jnp.where(lower[None], diff, -1e30))).astype(BF16)
    intra = jnp.einsum("hts,shd->thd", weight, values, preferred_element_type=F32)

    state_in = local(
        state_kernel,
        on_chip(carried_state.shape, F32),
        scalars,
        carried_state,
        *[message for _, message in arrived],
        theirs,
        name="state",
    )
    inter = jnp.exp(cumul)[:, :, None] * jnp.einsum(
        "thd,hde->the", queries.astype(F32), state_in, precision=HIGHEST
    )
    attended = intra + inter
    normed_heads = attended * lax.rsqrt(
        jnp.mean(attended * attended, axis=-1, keepdims=True) + 1e-06
    )
    flat_heads = normed_heads.astype(BF16).reshape(rows_here, heads_here * head_size)

    inner = flat_heads.shape[1]
    wide = width // 3 if width % 384 == 0 else width
    share = pl.BlockSpec((32, wide), lambda n: (0, n))
    own, *sent = pl.pallas_call(
        project_kernel,
        out_shape=[in_hbm((32, width), F32)] + [in_hbm((32, width), BF16)] * 3,
        grid=(width // wide,),
        in_specs=[
            SCALARS,
            pl.BlockSpec((rows_here, inner), lambda n: (0, 0)),
            pl.BlockSpec((inner, wide), lambda n: (0, n)),
        ],
        out_specs=[share] * 4,
        scratch_shapes=[pltpu.VMEM((rows_here, inner), BF16)],
        compiler_params=pltpu.CompilerParams(vmem_limit_bytes=12 * 1024 * 1024),
        cost_estimate=pl.CostEstimate(
            flops=2 * rows_here * inner * width,
            bytes_accessed=2 * width * (inner + rows_here),
            transcendentals=0,
        ),
        name="project",
    )(scalars, flat_heads, leave(out_weight))
    came = [move(part, along_p(s)) for s, part in zip((1, 2, 3), sent)]
    own, *sent = local(
        partial_kernel,
        [on_chip((8, width), F32)] + [on_chip((8, width), BF16)] * 3,
        scalars,
        *came,
        loose=(own,),
        scratch=[pltpu.VMEM((32, width), F32)],
        bytes_=32 * width * 8,
        mib=8,
        name="partial",
    )
    came = [move(part, along_q(s)) for s, part in zip((1, 2, 3), sent)]
    own_tokens = lax.dynamic_slice_in_dim(tokens, 32 * p + 8 * q, 8, 0).astype(F32)
    final_rows = local(
        norm_kernel,
        on_chip((8, width), BF16),
        scalars,
        own,
        *came,
        own_tokens,
        final_gain.reshape(1, width),
        bytes_=8 * width * 16,
        name="norm",
    )

    on_x = gather(final_rows, along_x, scalars, "stack_x")
    on_x, source = lax.optimization_barrier((on_x, vocab_weight))
    vocab = pl.pallas_call(
        load_kernel,
        out_shape=on_chip(vocab_weight.shape, BF16),
        in_specs=[pl.BlockSpec(memory_space=pltpu.HBM)],
        out_specs=ANYWHERE,
        scratch_shapes=[pltpu.SemaphoreType.DMA],
        compiler_params=pltpu.CompilerParams(vmem_limit_bytes=1024 * 1024),
        cost_estimate=pl.CostEstimate(
            flops=0, bytes_accessed=4 * width * vocab_local, transcendentals=0
        ),
        name="load",
    )(leave(source))
    ours = gather(on_x, along_p, scalars, "stack_p")
    theirs = move(ours, other_core)
    ours, theirs = lax.optimization_barrier((ours, theirs))
    lines = jnp.transpose(targets.reshape(X, CORE, 4, 4, 8), (1, 3, 2, 0, 4)).reshape(8, 128)
    half = ours.shape[0] // 2
    low, high = ours[:half], ours[half:]
    early = (move(low, along_q(1)), move(high, along_q(3)))
    first = jnp.dot(ours, vocab, preferred_element_type=F32)
    low, high, first = lax.optimization_barrier((low, high, first))
    late = (move(low, along_q(3)), move(high, along_q(1)))
    far = (move(early[0], along_q(1)), move(early[1], along_q(3)))
    def dot(rows):
        return jnp.dot(rows, vocab, preferred_element_type=F32)

    def score(shifts, blocks, logits):
        return local(
            functools.partial(score_kernel, *shifts),
            [on_chip((8, 128), F32)] * 2,
            scalars,
            lines,
            *logits,
            unread=blocks,
            bytes_=8 * 128 * vocab_local,
            name="score",
        )

    def both(parts):
        joined = jnp.concatenate(parts, axis=0)
        return joined, move(joined, other_core)

    found = score((0, 0), (ours, theirs), (first, dot(theirs)))
    blocks = both(early)
    found += score((1, 3), blocks, [dot(b) for b in blocks])
    late, found = lax.optimization_barrier((late, found))
    blocks = both(late)
    first = dot(blocks[0])
    far, first = lax.optimization_barrier((far, first))
    found += score((3, 1), blocks, (first, dot(blocks[1])))
    blocks = both(far)
    found += score((2, 2), blocks, [dot(b) for b in blocks])
    sent = local(
        place_kernel,
        on_chip((X * CORE, 8, 128), F32),
        scalars,
        *found,
        scratch=[pltpu.VMEM((24, 128), F32)],
        name="place",
    )
    came = lax.all_to_all(sent, ("x", "core"), 0, 0)
    sent = local(block_kernel, on_chip((Z * Y, 8, 128), F32), scalars, came, name="block")
    came = lax.all_to_all(sent, ("z", "y"), 0, 0)
    loglik = local(
        finish_kernel, jax.ShapeDtypeStruct((1, 128), F32), scalars, came, name="finish"
    )
    return loglik.reshape(rows_here)


def solution(mesh):
    fine = Mesh(mesh.devices.reshape(X, CORE, Z, Y), ALL)
    seq, head = (("x", "core"), ("z", "y"))
    return jax.shard_map(
        shards,
        mesh=fine,
        in_specs=(
            P(seq, None),
            P(seq, head),
            P(head, None, None),
            P(None, head),
            P(None, head),
            P(None, head),
            P(head, None),
            P(),
            P(None, ALL),
            P(),
        ),
        out_specs=P(seq),
        check_vma=False,
    )
```

```python
import functools

import jax
import jax.numpy as jnp
from jax import lax
from jax.experimental import pallas as pl
from jax.experimental.pallas import tpu as pltpu
from jax.sharding import Mesh, PartitionSpec as P

X, CORE, Z, Y = 4, 2, 4, 4
ALL = ("x", "core", "z", "y")
F32 = jnp.float32
BF16 = jnp.bfloat16
HIGHEST = lax.Precision.HIGHEST


def move(array, target):
    pairs = []
    for i in range(X * CORE * Z * Y):
        at = (i // (CORE * Z * Y), i // (Z * Y) % CORE, i // Y % Z, i % Y)
        to = target(*at)
        pairs.append((i, ((to[0] * CORE + to[1]) * Z + to[2]) * Y + to[3]))
    return lax.ppermute(array, ALL, pairs)


def other_core(x, c, z, y):
    return (x, 1 - c, z, y)


def along_x(s):
    return lambda x, c, z, y: ((x + s) % X, c, z, y)


def along_p(s):
    return lambda x, c, z, y: (x, c, z, (y + s) % Y) if c == 0 else (x, c, (z + s) % Z, y)


def along_q(s):
    return lambda x, c, z, y: (x, c, (z + s) % Z, y) if c == 0 else (x, c, z, (y + s) % Y)


def on_chip(shape, dtype):
    return pltpu.VMEM(shape, dtype)


def in_hbm(shape, dtype):
    return pltpu.HBM(shape, dtype)


def leave(array):
    return pltpu.with_memory_space_constraint(array, pltpu.HBM)


def pin(array):
    return pltpu.with_memory_space_constraint(array, pltpu.VMEM)


ANYWHERE = pl.BlockSpec(memory_space=pl.ANY)
SCALARS = pl.BlockSpec(memory_space=pltpu.SMEM)
WHOLE = pl.BlockSpec(memory_space=pltpu.VMEM)


def local(kernel, outs, scalars, *arrays, loose=(), unread=(), scratch=(), flops=0, bytes_=0, mib=4, name=None):
    many = isinstance(outs, list)
    specs = [WHOLE] * len(outs) if many else WHOLE
    return pl.pallas_call(
        kernel,
        out_shape=outs,
        in_specs=[SCALARS] + [WHOLE] * len((*arrays, *loose)) + [ANYWHERE] * len(unread),
        out_specs=specs,
        scratch_shapes=list(scratch),
        compiler_params=pltpu.CompilerParams(vmem_limit_bytes=mib * 1024 * 1024),
        cost_estimate=pl.CostEstimate(flops=flops, bytes_accessed=bytes_, transcendentals=0),
        name=name,
    )(scalars, *[pin(a) for a in arrays], *[leave(a) for a in loose], *[pin(a) for a in unread])


def load_kernel(source, out, done):
    copy = pltpu.make_async_copy(source, out, done)
    copy.start()
    copy.wait()


def heads_kernel(count, tokens, *refs):
    weights, outs = refs[:count], refs[count : 2 * count]
    held, *held_weights, arrived = refs[2 * count :]
    chunks = arrived.shape[1]
    deep = tokens.shape[1] // chunks
    copies = []
    for n in range(chunks):
        part = pl.ds(n * deep, deep)
        copies.append(
            [pltpu.make_async_copy(tokens.at[:, part], held.at[:, part], arrived.at[count, n])]
            + [
                pltpu.make_async_copy(weight.at[part, :], here.at[part, :], arrived.at[k, n])
                for k, (weight, here) in enumerate(zip(weights, held_weights))
            ]
        )
        for copy in copies[-1]:
            copy.start()
    totals = [None] * count
    for n in range(chunks):
        part = pl.ds(n * deep, deep)
        for copy in copies[n]:
            copy.wait()
        for k, here in enumerate(held_weights):
            product = jnp.dot(held[:, part], here[part, :], preferred_element_type=F32)
            totals[k] = product if totals[k] is None else totals[k] + product
    for out, total in zip(outs, totals):
        out[...] = total.astype(BF16)


def heads(tokens, *weights):
    rows, width = tokens.shape
    columns = weights[0].shape[1]
    count = len(weights)
    chunks = 4 if width % 512 == 0 else 1
    return pl.pallas_call(
        functools.partial(heads_kernel, count),
        out_shape=[jax.ShapeDtypeStruct((rows, columns), BF16)] * count,
        in_specs=[pl.BlockSpec(memory_space=pltpu.HBM)] * (1 + count),
        out_specs=[WHOLE] * count,
        scratch_shapes=[pltpu.VMEM((rows, width), BF16)]
        + [pltpu.VMEM((width, columns), BF16)] * count
        + [pltpu.SemaphoreType.DMA((count + 1, chunks))],
        compiler_params=pltpu.CompilerParams(vmem_limit_bytes=16 * 1024 * 1024),
        cost_estimate=pl.CostEstimate(
            flops=2 * rows * width * columns * count,
            bytes_accessed=2 * width * (rows + columns * count),
            transcendentals=0,
        ),
        name="heads",
    )(leave(tokens), *[leave(w) for w in weights])


def combine_kernel(at, mine, theirs, chip):
    size = mine.shape[2]
    low = at[1] == 0
    for h in range(mine.shape[0]):
        first = jnp.where(low, mine[h], theirs[h])
        second = jnp.where(low, theirs[h], mine[h])
        decay = jnp.broadcast_to((second[size:] * first[size:])[:1], (16, size))
        coarse = decay.astype(BF16).astype(F32)
        row = lax.broadcasted_iota(jnp.int32, (16, size), 0)
        chip[h, :size, :] = (second[size : size + 1] * first[:size] + second[:size]).astype(BF16)
        chip[h, size:, :] = jnp.where(row < 8, coarse, decay - coarse).astype(BF16)


def state_kernel(at, carried, three, two, one, theirs, out):
    size = carried.shape[2]
    for h in range(carried.shape[0]):
        state = carried[h]
        for s, message in ((3, three), (2, two), (1, one)):
            part = message[h].astype(F32)
            decay = part[size : size + 1] + part[size + 8 : size + 9]
            state = jnp.where(at[0] >= s, decay * state + part[:size], state)
        part = theirs[h]
        out[h] = jnp.where(at[1] == 1, part[size : size + 1] * state + part[:size], state)


def project_kernel(at, heads, weight, own, one, two, three, held, rolled, arrived):
    chunks = arrived.shape[0]
    wide = weight.shape[1] // chunks
    copies = []
    for n in range(chunks):
        part = pl.ds(n * wide, wide)
        copies.append(pltpu.make_async_copy(weight.at[:, part], held.at[:, part], arrived.at[n]))
        copies[-1].start()
    for s in range(4):
        start = pl.multiple_of((at[4] + s) % 4 * 32, 32)
        rolled[pl.ds(32 * s, 32), :] = heads[pl.ds(start, 32), :]
    for n in range(chunks):
        part = pl.ds(n * wide, wide)
        copies[n].wait()
        out = jnp.dot(rolled[...], held[:, part], preferred_element_type=F32)
        own[:, part] = out[:32]
        one[:, part] = out[32:64].astype(BF16)
        two[:, part] = out[64:96].astype(BF16)
        three[:, part] = out[96:].astype(BF16)


def partial_kernel(at, one, two, three, own, mine, first, second, third, total):
    q = at[5]
    total[...] = (
        own[...]
        + one[...].astype(F32)
        + two[...].astype(F32)
        + three[...].astype(F32)
    )
    for s, out in enumerate((mine, first, second, third)):
        start = pl.multiple_of((q + s) % 4 * 8, 8)
        out[...] = total[pl.ds(start, 8), :].astype(out.dtype)


def norm_kernel(at, own, one, two, three, tokens, gain, out):
    resid = (
        tokens[...]
        + own[...]
        + one[...].astype(F32)
        + two[...].astype(F32)
        + three[...].astype(F32)
    )
    scale = lax.rsqrt(jnp.mean(resid * resid, axis=1, keepdims=True) + 1e-06)
    out[...] = (resid * scale * gain[...].astype(F32)).astype(BF16)


def stack_kernel(at, a, b, c, d, out):
    rows = a.shape[0]
    out[0 : 2 * rows, :] = jnp.concatenate([a[...], b[...]], axis=0)
    out[2 * rows : 4 * rows, :] = jnp.concatenate([c[...], d[...]], axis=0)


def gather(block, target, scalars, name):
    parts = [move(block, target(s)) for s in (3, 2, 1)]
    rows, width = block.shape
    return local(
        stack_kernel,
        on_chip((4 * rows, width), block.dtype),
        scalars,
        block,
        *parts,
        bytes_=16 * rows * width,
        mib=8,
        name=name,
    )


def in_place(values, lane, p, x):
    values = pltpu.roll(values, 32 * p, 1)
    return jnp.where(
        (lane & 31) >= 8 * x,
        pltpu.roll(values, 8 * x, 1),
        pltpu.roll(values, (8 * x + 96) % 128, 1),
    )


def as_gathered(values, lane, p, x):
    values = pltpu.roll(values, (128 - 32 * p) % 128, 1)
    return jnp.where(
        (lane & 31) < 32 - 8 * x,
        pltpu.roll(values, (128 - 8 * x) % 128, 1),
        pltpu.roll(values, (160 - 8 * x) % 128, 1),
    )


def score_kernel(low, high, at, targets, mine, theirs, rows_mine, rows_theirs, out_mine, out_theirs):
    x = at[0]
    lane = lax.broadcasted_iota(jnp.int32, (8, 128), 1)
    i = lax.broadcasted_iota(jnp.int32, (128, 128), 0)
    j = lax.broadcasted_iota(jnp.int32, (128, 128), 1)
    for logits, out, p, q, core in (
        (mine, out_mine, at[4], at[5], at[1]),
        (theirs, out_theirs, at[5], at[4], 1 - at[1]),
    ):
        found = logits[...]
        lines = []
        for shift in (low, high):
            line = targets[pl.ds(core * 4 + ((q + 4 - shift) & 3), 1), :] - at[6]
            lines.append(as_gathered(jnp.broadcast_to(line, (8, 128)), lane, p, x))
        line = jnp.where(lane < 64, *lines)[:1]
        want = jnp.sum(jnp.where(i == j, line, 0), axis=1, keepdims=True)
        top = jnp.max(found, axis=1, keepdims=True)
        total = jnp.sum(jnp.exp(found - top), axis=1, keepdims=True)
        column = lax.broadcasted_iota(jnp.int32, found.shape, 1)
        hit = jnp.sum(jnp.where(column == want, found, 0.0), axis=1, keepdims=True)
        both = jnp.where(j == 0, top, jnp.where(j == 1, total, jnp.where(j == 2, hit, 0.0)))
        out[...] = in_place(jnp.transpose(both)[:8], lane, p, x)


def place_kernel(at, *refs):
    blocks, out, held = refs[:-2], refs[-2], refs[-1]
    lane = lax.broadcasted_iota(jnp.int32, (8, 128), 1)
    for k in range(2):
        p, q, core = (at[4], at[5], at[1]) if k == 0 else (at[5], at[4], 1 - at[1])
        here, early, late, far = (blocks[2 * g + k][...] for g in range(4))
        low = ((lane // 32 + 4 - p) & 3) < 2
        for shift, values in (
            (0, here),
            (1, jnp.where(low, early, late)),
            (2, far),
            (3, jnp.where(low, late, early)),
        ):
            place = core * 4 + ((q + 4 - shift) & 3)
            for row in range(3):
                held[pl.ds(8 * row + place, 1), :] = values[row : row + 1, :]
    for row in range(3):
        values = held[8 * row : 8 * row + 8, :]
        turned = {8 * k: pltpu.roll(values, 8 * k, 1) if k else values for k in range(16)}
        for x in range(X):
            picked = [
                jnp.where((lane // 8 & 3) == q, turned[(8 * q - 8 * x) % 128], 0.0) for q in range(4)
            ]
            for core in range(CORE):
                line = sum(picked[q][4 * core + q : 4 * core + q + 1, :] for q in range(4))
                out[x * CORE + core, row : row + 1, :] = line


def merged(parts):
    top = parts[0][0:1]
    for part in parts[1:]:
        top = jnp.maximum(top, part[0:1])
    total = sum(part[1:2] * jnp.exp(part[0:1] - top) for part in parts)
    hit = sum(part[2:3] for part in parts)
    return top, total, hit


def block_kernel(at, found, out):
    top, total, hit = merged([found[k] for k in range(X * CORE)])
    for k in range(Z * Y):
        out[k, 0:1, :], out[k, 1:2, :], out[k, 2:3, :] = top, total, hit


def finish_kernel(at, found, out):
    top, total, hit = merged([found[k] for k in range(Z * Y)])
    out[...] = hit - top - jnp.log(total)


def shards(
    tokens,
    log_decay,
    carried_state,
    q_weight,
    k_weight,
    v_weight,
    out_weight,
    final_gain,
    vocab_weight,
    targets,
):
    x, c, z, y = (lax.axis_index(a) for a in ALL)
    p, q = jnp.where(c == 0, y, z), jnp.where(c == 0, z, y)
    rows_here, width = tokens.shape
    heads_here = carried_state.shape[0]
    head_size = carried_state.shape[1]
    view = (rows_here, heads_here, head_size)
    vocab_local = vocab_weight.shape[1]
    offset = (((x * CORE + c) * Z + z) * Y + y) * vocab_local
    scalars = jnp.stack([x, c, z, y, p, q, offset, offset]).astype(jnp.int32)

    keys, values = (part.reshape(view) for part in heads(tokens, k_weight, v_weight))
    lower = jnp.arange(rows_here)[:, None] >= jnp.arange(rows_here)[None, :]
    cumul = jnp.dot(lower.astype(F32), log_decay, precision=HIGHEST)
    last_cum = cumul[-1]
    ends = jnp.exp(last_cum[None, :] - cumul)
    state = jnp.einsum(
        "thd,the->hde",
        keys.astype(F32) * ends[:, :, None],
        values.astype(F32),
        precision=HIGHEST,
    )
    decay = jnp.broadcast_to(jnp.exp(last_cum)[:, None, None], (heads_here, 8, head_size))
    mine = jnp.concatenate([state, decay], axis=1)
    theirs = move(mine, other_core)
    chip = local(
        combine_kernel,
        on_chip((heads_here, head_size + 16, head_size), BF16),
        scalars,
        mine,
        theirs,
        name="combine",
    )
    tokens_then, chip = lax.optimization_barrier((tokens, chip))
    arrived = [(s, move(chip, along_x(s))) for s in (3, 2, 1)]

    queries = heads(tokens_then, q_weight)[0].reshape(view)
    scores = jnp.einsum("thd,shd->hts", queries, keys, preferred_element_type=F32)
    diff = jnp.transpose(cumul[:, None, :] - cumul[None, :, :], (2, 0, 1))
    weight = (scores * jnp.exp(jnp.where(lower[None], diff, -1e30))).astype(BF16)
    intra = jnp.einsum("hts,shd->thd", weight, values, preferred_element_type=F32)

    state_in = local(
        state_kernel,
        on_chip(carried_state.shape, F32),
        scalars,
        carried_state,
        *[message for _, message in arrived],
        theirs,
        name="state",
    )
    inter = jnp.exp(cumul)[:, :, None] * jnp.einsum(
        "thd,hde->the", queries.astype(F32), state_in, precision=HIGHEST
    )
    attended = intra + inter
    normed_heads = attended * lax.rsqrt(
        jnp.mean(attended * attended, axis=-1, keepdims=True) + 1e-06
    )
    flat_heads = normed_heads.astype(BF16).reshape(rows_here, heads_here * head_size)

    inner = flat_heads.shape[1]
    chunks = 4 if width % 512 == 0 else 1
    own, *sent = pl.pallas_call(
        project_kernel,
        out_shape=[in_hbm((32, width), F32)] + [on_chip((32, width), BF16)] * 3,
        in_specs=[SCALARS, WHOLE, pl.BlockSpec(memory_space=pltpu.HBM)],
        out_specs=[WHOLE] * 4,
        scratch_shapes=[
            pltpu.VMEM(out_weight.shape, BF16),
            pltpu.VMEM(flat_heads.shape, BF16),
            pltpu.SemaphoreType.DMA((chunks,)),
        ],
        compiler_params=pltpu.CompilerParams(vmem_limit_bytes=12 * 1024 * 1024),
        cost_estimate=pl.CostEstimate(
            flops=2 * rows_here * inner * width,
            bytes_accessed=2 * width * (inner + rows_here),
            transcendentals=0,
        ),
        name="project",
    )(scalars, flat_heads, leave(out_weight))
    came = [move(part, along_p(s)) for s, part in zip((1, 2, 3), sent)]
    own, *sent = local(
        partial_kernel,
        [on_chip((8, width), F32)] + [on_chip((8, width), BF16)] * 3,
        scalars,
        *came,
        loose=(own,),
        scratch=[pltpu.VMEM((32, width), F32)],
        bytes_=32 * width * 8,
        mib=8,
        name="partial",
    )
    came = [move(part, along_q(s)) for s, part in zip((1, 2, 3), sent)]
    own_tokens = lax.dynamic_slice_in_dim(tokens, 32 * p + 8 * q, 8, 0).astype(F32)
    final_rows = local(
        norm_kernel,
        on_chip((8, width), BF16),
        scalars,
        own,
        *came,
        own_tokens,
        final_gain.reshape(1, width),
        bytes_=8 * width * 16,
        name="norm",
    )

    on_x = gather(final_rows, along_x, scalars, "stack_x")
    on_x, source = lax.optimization_barrier((on_x, vocab_weight))
    vocab = pl.pallas_call(
        load_kernel,
        out_shape=on_chip(vocab_weight.shape, BF16),
        in_specs=[pl.BlockSpec(memory_space=pltpu.HBM)],
        out_specs=ANYWHERE,
        scratch_shapes=[pltpu.SemaphoreType.DMA],
        compiler_params=pltpu.CompilerParams(vmem_limit_bytes=1024 * 1024),
        cost_estimate=pl.CostEstimate(
            flops=0, bytes_accessed=4 * width * vocab_local, transcendentals=0
        ),
        name="load",
    )(leave(source))
    ours = gather(on_x, along_p, scalars, "stack_p")
    theirs = move(ours, other_core)
    ours, theirs = lax.optimization_barrier((ours, theirs))
    lines = jnp.transpose(targets.reshape(X, CORE, 4, 4, 8), (1, 3, 2, 0, 4)).reshape(8, 128)
    half = ours.shape[0] // 2
    low, high = ours[:half], ours[half:]
    early = (move(low, along_q(1)), move(high, along_q(3)))
    first = jnp.dot(ours, vocab, preferred_element_type=F32)
    low, high, first = lax.optimization_barrier((low, high, first))
    late = (move(low, along_q(3)), move(high, along_q(1)))
    far = (move(early[0], along_q(1)), move(early[1], along_q(3)))
    def dot(rows):
        return jnp.dot(rows, vocab, preferred_element_type=F32)

    def score(shifts, blocks, logits):
        return local(
            functools.partial(score_kernel, *shifts),
            [on_chip((8, 128), F32)] * 2,
            scalars,
            lines,
            *logits,
            unread=blocks,
            bytes_=8 * 128 * vocab_local,
            name="score",
        )

    def both(parts):
        joined = jnp.concatenate(parts, axis=0)
        return joined, move(joined, other_core)

    found = score((0, 0), (ours, theirs), (first, dot(theirs)))
    blocks = both(early)
    found += score((1, 3), blocks, [dot(b) for b in blocks])
    late, found = lax.optimization_barrier((late, found))
    blocks = both(late)
    first = dot(blocks[0])
    far, first = lax.optimization_barrier((far, first))
    found += score((3, 1), blocks, (first, dot(blocks[1])))
    blocks = both(far)
    found += score((2, 2), blocks, [dot(b) for b in blocks])
    sent = local(
        place_kernel,
        on_chip((X * CORE, 8, 128), F32),
        scalars,
        *found,
        scratch=[pltpu.VMEM((24, 128), F32)],
        name="place",
    )
    came = lax.all_to_all(sent, ("x", "core"), 0, 0)
    sent = local(block_kernel, on_chip((Z * Y, 8, 128), F32), scalars, came, name="block")
    came = lax.all_to_all(sent, ("z", "y"), 0, 0)
    loglik = local(
        finish_kernel, jax.ShapeDtypeStruct((1, 128), F32), scalars, came, name="finish"
    )
    return loglik.reshape(rows_here)


def solution(mesh):
    fine = Mesh(mesh.devices.reshape(X, CORE, Z, Y), ALL)
    seq, head = (("x", "core"), ("z", "y"))
    return jax.shard_map(
        shards,
        mesh=fine,
        in_specs=(
            P(seq, None),
            P(seq, head),
            P(head, None, None),
            P(None, head),
            P(None, head),
            P(None, head),
            P(head, None),
            P(),
            P(None, ALL),
            P(),
        ),
        out_specs=P(seq),
        check_vma=False,
    )
```

```python
import functools

import jax
import jax.numpy as jnp
from jax import lax
from jax.experimental import pallas as pl
from jax.experimental.pallas import tpu as pltpu
from jax.sharding import Mesh, PartitionSpec as P

X, CORE, Z, Y = 4, 2, 4, 4
ALL = ("x", "core", "z", "y")
F32 = jnp.float32
BF16 = jnp.bfloat16
HIGHEST = lax.Precision.HIGHEST


def move(array, target):
    pairs = []
    for i in range(X * CORE * Z * Y):
        at = (i // (CORE * Z * Y), i // (Z * Y) % CORE, i // Y % Z, i % Y)
        to = target(*at)
        pairs.append((i, ((to[0] * CORE + to[1]) * Z + to[2]) * Y + to[3]))
    return lax.ppermute(array, ALL, pairs)


def other_core(x, c, z, y):
    return (x, 1 - c, z, y)


def along_x(s):
    return lambda x, c, z, y: ((x + s) % X, c, z, y)


def along_p(s):
    return lambda x, c, z, y: (x, c, z, (y + s) % Y) if c == 0 else (x, c, (z + s) % Z, y)


def along_q(s):
    return lambda x, c, z, y: (x, c, (z + s) % Z, y) if c == 0 else (x, c, z, (y + s) % Y)


def on_chip(shape, dtype):
    return pltpu.VMEM(shape, dtype)


def in_hbm(shape, dtype):
    return pltpu.HBM(shape, dtype)


def leave(array):
    return pltpu.with_memory_space_constraint(array, pltpu.HBM)


def pin(array):
    return pltpu.with_memory_space_constraint(array, pltpu.VMEM)


ANYWHERE = pl.BlockSpec(memory_space=pl.ANY)
SCALARS = pl.BlockSpec(memory_space=pltpu.SMEM)
WHOLE = pl.BlockSpec(memory_space=pltpu.VMEM)


def local(kernel, outs, scalars, *arrays, loose=(), unread=(), scratch=(), flops=0, bytes_=0, mib=4, name=None):
    many = isinstance(outs, list)
    specs = [WHOLE] * len(outs) if many else WHOLE
    return pl.pallas_call(
        kernel,
        out_shape=outs,
        in_specs=[SCALARS] + [WHOLE] * len((*arrays, *loose)) + [ANYWHERE] * len(unread),
        out_specs=specs,
        scratch_shapes=list(scratch),
        compiler_params=pltpu.CompilerParams(vmem_limit_bytes=mib * 1024 * 1024),
        cost_estimate=pl.CostEstimate(flops=flops, bytes_accessed=bytes_, transcendentals=0),
        name=name,
    )(scalars, *[pin(a) for a in arrays], *[leave(a) for a in loose], *[pin(a) for a in unread])


def load_kernel(source, out, done):
    copy = pltpu.make_async_copy(source, out, done)
    copy.start()
    copy.wait()


def heads_kernel(count, tokens, *refs):
    weights, outs = refs[:count], refs[count : 2 * count]
    held, *held_weights, arrived = refs[2 * count :]
    chunks = arrived.shape[1]
    deep = tokens.shape[1] // chunks
    copies = []
    for n in range(chunks):
        part = pl.ds(n * deep, deep)
        copies.append(
            [pltpu.make_async_copy(tokens.at[:, part], held.at[:, part], arrived.at[count, n])]
            + [
                pltpu.make_async_copy(weight.at[part, :], here.at[part, :], arrived.at[k, n])
                for k, (weight, here) in enumerate(zip(weights, held_weights))
            ]
        )
        for copy in copies[-1]:
            copy.start()
    totals = [None] * count
    for n in range(chunks):
        part = pl.ds(n * deep, deep)
        for copy in copies[n]:
            copy.wait()
        for k, here in enumerate(held_weights):
            product = jnp.dot(held[:, part], here[part, :], preferred_element_type=F32)
            totals[k] = product if totals[k] is None else totals[k] + product
    for out, total in zip(outs, totals):
        out[...] = total.astype(BF16)


def heads(tokens, *weights):
    rows, width = tokens.shape
    columns = weights[0].shape[1]
    count = len(weights)
    chunks = 4 if width % 512 == 0 else 1
    return pl.pallas_call(
        functools.partial(heads_kernel, count),
        out_shape=[jax.ShapeDtypeStruct((rows, columns), BF16)] * count,
        in_specs=[pl.BlockSpec(memory_space=pltpu.HBM)] * (1 + count),
        out_specs=[WHOLE] * count,
        scratch_shapes=[pltpu.VMEM((rows, width), BF16)]
        + [pltpu.VMEM((width, columns), BF16)] * count
        + [pltpu.SemaphoreType.DMA((count + 1, chunks))],
        compiler_params=pltpu.CompilerParams(vmem_limit_bytes=16 * 1024 * 1024),
        cost_estimate=pl.CostEstimate(
            flops=2 * rows * width * columns * count,
            bytes_accessed=2 * width * (rows + columns * count),
            transcendentals=0,
        ),
        name="heads",
    )(leave(tokens), *[leave(w) for w in weights])


def combine_kernel(at, mine, theirs, chip):
    size = mine.shape[2]
    low = at[1] == 0
    for h in range(mine.shape[0]):
        first = jnp.where(low, mine[h], theirs[h])
        second = jnp.where(low, theirs[h], mine[h])
        decay = jnp.broadcast_to((second[size:] * first[size:])[:1], (16, size))
        coarse = decay.astype(BF16).astype(F32)
        row = lax.broadcasted_iota(jnp.int32, (16, size), 0)
        chip[h, :size, :] = (second[size : size + 1] * first[:size] + second[:size]).astype(BF16)
        chip[h, size:, :] = jnp.where(row < 8, coarse, decay - coarse).astype(BF16)


def state_kernel(at, carried, three, two, one, theirs, out):
    size = carried.shape[2]
    for h in range(carried.shape[0]):
        state = carried[h]
        for s, message in ((3, three), (2, two), (1, one)):
            part = message[h].astype(F32)
            decay = part[size : size + 1] + part[size + 8 : size + 9]
            state = jnp.where(at[0] >= s, decay * state + part[:size], state)
        part = theirs[h]
        out[h] = jnp.where(at[1] == 1, part[size : size + 1] * state + part[:size], state)


def project_kernel(at, heads, weight, own, one, two, three, held, rolled, arrived):
    chunks = arrived.shape[0]
    wide = weight.shape[1] // chunks
    copies = []
    for n in range(chunks):
        part = pl.ds(n * wide, wide)
        copies.append(pltpu.make_async_copy(weight.at[:, part], held.at[:, part], arrived.at[n]))
        copies[-1].start()
    for s in range(4):
        start = pl.multiple_of((at[4] + s) % 4 * 32, 32)
        rolled[pl.ds(32 * s, 32), :] = heads[pl.ds(start, 32), :]
    for n in range(chunks):
        part = pl.ds(n * wide, wide)
        copies[n].wait()
        out = jnp.dot(rolled[...], held[:, part], preferred_element_type=F32)
        own[:, part] = out[:32]
        one[:, part] = out[32:64].astype(BF16)
        two[:, part] = out[64:96].astype(BF16)
        three[:, part] = out[96:].astype(BF16)


def partial_kernel(at, one, two, three, own, mine, first, second, third, total):
    q = at[5]
    total[...] = (
        own[...]
        + one[...].astype(F32)
        + two[...].astype(F32)
        + three[...].astype(F32)
    )
    for s, out in enumerate((mine, first, second, third)):
        start = pl.multiple_of((q + s) % 4 * 8, 8)
        out[...] = total[pl.ds(start, 8), :].astype(out.dtype)


def norm_kernel(at, own, one, two, three, tokens, gain, out):
    resid = (
        tokens[...]
        + own[...]
        + one[...].astype(F32)
        + two[...].astype(F32)
        + three[...].astype(F32)
    )
    scale = lax.rsqrt(jnp.mean(resid * resid, axis=1, keepdims=True) + 1e-06)
    out[...] = (resid * scale * gain[...].astype(F32)).astype(BF16)


def stack_kernel(at, a, b, c, d, out):
    rows = a.shape[0]
    out[0 : 2 * rows, :] = jnp.concatenate([a[...], b[...]], axis=0)
    out[2 * rows : 4 * rows, :] = jnp.concatenate([c[...], d[...]], axis=0)


def gather(block, target, scalars, name):
    parts = [move(block, target(s)) for s in (3, 2, 1)]
    rows, width = block.shape
    return local(
        stack_kernel,
        on_chip((4 * rows, width), block.dtype),
        scalars,
        block,
        *parts,
        bytes_=16 * rows * width,
        mib=8,
        name=name,
    )


def in_place(values, lane, p, x):
    values = pltpu.roll(values, 32 * p, 1)
    return jnp.where(
        (lane & 31) >= 8 * x,
        pltpu.roll(values, 8 * x, 1),
        pltpu.roll(values, (8 * x + 96) % 128, 1),
    )


def as_gathered(values, lane, p, x):
    values = pltpu.roll(values, (128 - 32 * p) % 128, 1)
    return jnp.where(
        (lane & 31) < 32 - 8 * x,
        pltpu.roll(values, (128 - 8 * x) % 128, 1),
        pltpu.roll(values, (160 - 8 * x) % 128, 1),
    )


def score_kernel(low, high, at, targets, mine, theirs, rows_mine, rows_theirs, out_mine, out_theirs):
    x = at[0]
    lane = lax.broadcasted_iota(jnp.int32, (8, 128), 1)
    i = lax.broadcasted_iota(jnp.int32, (128, 128), 0)
    j = lax.broadcasted_iota(jnp.int32, (128, 128), 1)
    for logits, out, p, q, core in (
        (mine, out_mine, at[4], at[5], at[1]),
        (theirs, out_theirs, at[5], at[4], 1 - at[1]),
    ):
        found = logits[...]
        lines = []
        for shift in (low, high):
            line = targets[pl.ds(core * 4 + ((q + 4 - shift) & 3), 1), :] - at[6]
            lines.append(as_gathered(jnp.broadcast_to(line, (8, 128)), lane, p, x))
        line = jnp.where(lane < 64, *lines)[:1]
        want = jnp.sum(jnp.where(i == j, line, 0), axis=1, keepdims=True)
        top = jnp.max(found, axis=1, keepdims=True)
        total = jnp.sum(jnp.exp(found - top), axis=1, keepdims=True)
        column = lax.broadcasted_iota(jnp.int32, found.shape, 1)
        hit = jnp.sum(jnp.where(column == want, found, 0.0), axis=1, keepdims=True)
        both = jnp.where(j == 0, top, jnp.where(j == 1, total, jnp.where(j == 2, hit, 0.0)))
        out[...] = in_place(jnp.transpose(both)[:8], lane, p, x)


def place_kernel(at, *refs):
    blocks, out, held = refs[:-2], refs[-2], refs[-1]
    lane = lax.broadcasted_iota(jnp.int32, (8, 128), 1)
    for k in range(2):
        p, q, core = (at[4], at[5], at[1]) if k == 0 else (at[5], at[4], 1 - at[1])
        here, early, late, far = (blocks[2 * g + k][...] for g in range(4))
        low = ((lane // 32 + 4 - p) & 3) < 2
        for shift, values in (
            (0, here),
            (1, jnp.where(low, early, late)),
            (2, far),
            (3, jnp.where(low, late, early)),
        ):
            place = core * 4 + ((q + 4 - shift) & 3)
            for row in range(3):
                held[pl.ds(8 * row + place, 1), :] = values[row : row + 1, :]
    for row in range(3):
        values = held[8 * row : 8 * row + 8, :]
        turned = {8 * k: pltpu.roll(values, 8 * k, 1) if k else values for k in range(16)}
        for x in range(X):
            picked = [
                jnp.where((lane // 8 & 3) == q, turned[(8 * q - 8 * x) % 128], 0.0) for q in range(4)
            ]
            for core in range(CORE):
                line = sum(picked[q][4 * core + q : 4 * core + q + 1, :] for q in range(4))
                out[x * CORE + core, row : row + 1, :] = line


def merged(parts):
    top = parts[0][0:1]
    for part in parts[1:]:
        top = jnp.maximum(top, part[0:1])
    total = sum(part[1:2] * jnp.exp(part[0:1] - top) for part in parts)
    hit = sum(part[2:3] for part in parts)
    return top, total, hit


def block_kernel(at, found, out):
    top, total, hit = merged([found[k] for k in range(X * CORE)])
    for k in range(Z * Y):
        out[k, 0:1, :], out[k, 1:2, :], out[k, 2:3, :] = top, total, hit


def finish_kernel(at, found, out):
    top, total, hit = merged([found[k] for k in range(Z * Y)])
    out[...] = hit - top - jnp.log(total)


def shards(
    tokens,
    log_decay,
    carried_state,
    q_weight,
    k_weight,
    v_weight,
    out_weight,
    final_gain,
    vocab_weight,
    targets,
):
    x, c, z, y = (lax.axis_index(a) for a in ALL)
    p, q = jnp.where(c == 0, y, z), jnp.where(c == 0, z, y)
    rows_here, width = tokens.shape
    heads_here = carried_state.shape[0]
    head_size = carried_state.shape[1]
    view = (rows_here, heads_here, head_size)
    vocab_local = vocab_weight.shape[1]
    offset = (((x * CORE + c) * Z + z) * Y + y) * vocab_local
    scalars = jnp.stack([x, c, z, y, p, q, offset, offset]).astype(jnp.int32)

    keys, values = (part.reshape(view) for part in heads(tokens, k_weight, v_weight))
    lower = jnp.arange(rows_here)[:, None] >= jnp.arange(rows_here)[None, :]
    cumul = jnp.dot(lower.astype(F32), log_decay, precision=HIGHEST)
    last_cum = cumul[-1]
    ends = jnp.exp(last_cum[None, :] - cumul)
    state = jnp.einsum(
        "thd,the->hde",
        keys.astype(F32) * ends[:, :, None],
        values.astype(F32),
        precision=HIGHEST,
    )
    decay = jnp.broadcast_to(jnp.exp(last_cum)[:, None, None], (heads_here, 8, head_size))
    mine = jnp.concatenate([state, decay], axis=1)
    theirs = move(mine, other_core)
    chip = local(
        combine_kernel,
        on_chip((heads_here, head_size + 16, head_size), BF16),
        scalars,
        mine,
        theirs,
        name="combine",
    )
    tokens_then, chip = lax.optimization_barrier((tokens, chip))
    arrived = [(s, move(chip, along_x(s))) for s in (3, 2, 1)]

    queries = heads(tokens_then, q_weight)[0].reshape(view)
    scores = jnp.einsum("thd,shd->hts", queries, keys, preferred_element_type=F32)
    diff = jnp.transpose(cumul[:, None, :] - cumul[None, :, :], (2, 0, 1))
    weight = (scores * jnp.exp(jnp.where(lower[None], diff, -1e30))).astype(BF16)
    intra = jnp.einsum("hts,shd->thd", weight, values, preferred_element_type=F32)

    state_in = local(
        state_kernel,
        on_chip(carried_state.shape, F32),
        scalars,
        carried_state,
        *[message for _, message in arrived],
        theirs,
        name="state",
    )
    inter = jnp.exp(cumul)[:, :, None] * jnp.einsum(
        "thd,hde->the", queries.astype(F32), state_in, precision=HIGHEST
    )
    attended = intra + inter
    normed_heads = attended * lax.rsqrt(
        jnp.mean(attended * attended, axis=-1, keepdims=True) + 1e-06
    )
    flat_heads = normed_heads.astype(BF16).reshape(rows_here, heads_here * head_size)

    inner = flat_heads.shape[1]
    chunks = 4 if width % 512 == 0 else 1
    own, *sent = pl.pallas_call(
        project_kernel,
        out_shape=[in_hbm((32, width), F32)] + [on_chip((32, width), BF16)] * 3,
        in_specs=[SCALARS, WHOLE, pl.BlockSpec(memory_space=pltpu.HBM)],
        out_specs=[WHOLE] * 4,
        scratch_shapes=[
            pltpu.VMEM(out_weight.shape, BF16),
            pltpu.VMEM(flat_heads.shape, BF16),
            pltpu.SemaphoreType.DMA((chunks,)),
        ],
        compiler_params=pltpu.CompilerParams(vmem_limit_bytes=12 * 1024 * 1024),
        cost_estimate=pl.CostEstimate(
            flops=2 * rows_here * inner * width,
            bytes_accessed=2 * width * (inner + rows_here),
            transcendentals=0,
        ),
        name="project",
    )(scalars, flat_heads, leave(out_weight))
    came = [move(part, along_p(s)) for s, part in zip((1, 2, 3), sent)]
    own, *sent = local(
        partial_kernel,
        [on_chip((8, width), F32)] + [on_chip((8, width), BF16)] * 3,
        scalars,
        *came,
        loose=(own,),
        scratch=[pltpu.VMEM((32, width), F32)],
        bytes_=32 * width * 8,
        mib=8,
        name="partial",
    )
    came = [move(part, along_q(s)) for s, part in zip((1, 2, 3), sent)]
    own_tokens = lax.dynamic_slice_in_dim(tokens, 32 * p + 8 * q, 8, 0).astype(F32)
    final_rows = local(
        norm_kernel,
        on_chip((8, width), BF16),
        scalars,
        own,
        *came,
        own_tokens,
        final_gain.reshape(1, width),
        bytes_=8 * width * 16,
        name="norm",
    )

    on_x = gather(final_rows, along_x, scalars, "stack_x")
    on_x, source = lax.optimization_barrier((on_x, vocab_weight))
    vocab = pl.pallas_call(
        load_kernel,
        out_shape=on_chip(vocab_weight.shape, BF16),
        in_specs=[pl.BlockSpec(memory_space=pltpu.HBM)],
        out_specs=ANYWHERE,
        scratch_shapes=[pltpu.SemaphoreType.DMA],
        compiler_params=pltpu.CompilerParams(vmem_limit_bytes=1024 * 1024),
        cost_estimate=pl.CostEstimate(
            flops=0, bytes_accessed=4 * width * vocab_local, transcendentals=0
        ),
        name="load",
    )(leave(source))
    ours = gather(on_x, along_p, scalars, "stack_p")
    theirs = move(ours, other_core)
    lines = jnp.transpose(targets.reshape(X, CORE, 4, 4, 8), (1, 3, 2, 0, 4)).reshape(8, 128)
    half = ours.shape[0] // 2
    low, high = ours[:half], ours[half:]
    early = (move(low, along_q(1)), move(high, along_q(3)))
    first = jnp.dot(ours, vocab, preferred_element_type=F32)
    low, high, first = lax.optimization_barrier((low, high, first))
    late = (move(low, along_q(3)), move(high, along_q(1)))
    far = (move(early[0], along_q(1)), move(early[1], along_q(3)))
    def dot(rows):
        return jnp.dot(rows, vocab, preferred_element_type=F32)

    def score(shifts, blocks, logits):
        return local(
            functools.partial(score_kernel, *shifts),
            [on_chip((8, 128), F32)] * 2,
            scalars,
            lines,
            *logits,
            unread=blocks,
            bytes_=8 * 128 * vocab_local,
            name="score",
        )

    def both(parts):
        joined = jnp.concatenate(parts, axis=0)
        return joined, move(joined, other_core)

    found = score((0, 0), (ours, theirs), (first, dot(theirs)))
    blocks = both(early)
    found += score((1, 3), blocks, [dot(b) for b in blocks])
    late, found = lax.optimization_barrier((late, found))
    blocks = both(late)
    first = dot(blocks[0])
    far, first = lax.optimization_barrier((far, first))
    found += score((3, 1), blocks, (first, dot(blocks[1])))
    blocks = both(far)
    found += score((2, 2), blocks, [dot(b) for b in blocks])
    sent = local(
        place_kernel,
        on_chip((X * CORE, 8, 128), F32),
        scalars,
        *found,
        scratch=[pltpu.VMEM((24, 128), F32)],
        name="place",
    )
    came = lax.all_to_all(sent, ("x", "core"), 0, 0)
    sent = local(block_kernel, on_chip((Z * Y, 8, 128), F32), scalars, came, name="block")
    came = lax.all_to_all(sent, ("z", "y"), 0, 0)
    loglik = local(
        finish_kernel, jax.ShapeDtypeStruct((1, 128), F32), scalars, came, name="finish"
    )
    return loglik.reshape(rows_here)


def solution(mesh):
    fine = Mesh(mesh.devices.reshape(X, CORE, Z, Y), ALL)
    seq, head = (("x", "core"), ("z", "y"))
    return jax.shard_map(
        shards,
        mesh=fine,
        in_specs=(
            P(seq, None),
            P(seq, head),
            P(head, None, None),
            P(None, head),
            P(None, head),
            P(None, head),
            P(head, None),
            P(),
            P(None, ALL),
            P(),
        ),
        out_specs=P(seq),
        check_vma=False,
    )
```
